128 devices in a mesh: row: 8 (over y, core), col: 16 (over x, z).
Axes of the slice: x: 4, y: 4, z: 4, core: 2. Of those that a mesh axis runs over, the one named last changes fastest.
Arguments:
- amplitudes: bfloat16 [8192, 32768], P('row', 'col'), may hold values from -6 to 6
- t2_mask: int32 [128, 512], P('row', 'col'), may hold values 0 or 1
- eri_tiles: bfloat16 [40960, 4096], P(('row', 'col')), may hold values from -0.046875 to 0.046875
- eri_slot: int32 [32768], replicated, may hold values from -1 to 40959, as said below
Outputs:
- cycle_term: float32 [4096, 8192], P('col', 'row')
The draws below stay inside these ranges and needn't reach their ends.
Inputs may be any that keep to these rules, and one draw needn't show every extreme that they name: `eri_slot`: different tiles have different slots. For each col index g, of the tiles whose virtual tile c lies in [g * 2, (g + 1) * 2), at most 20 have slots on one device (slots s with s // 320 equal), and exactly 20 on some device.
All inputs are finite; a program needn't handle non-finite values. No bound on the sum of `t2_mask` on one device may be relied on, other than what follows from the above.
Results may differ from the reference program's by a relative error of at most 0.0003.
Values may be sent and summed in bfloat16 or wider, within the bound.
No kernel may reach another device: no remote copies, remote signals or barrier semaphores. Data moves between devices by JAX's collectives and lax.ppermute only.
A program may use at most 192 MiB of HBM per device.

```python
import jax
import jax.numpy as jnp

TILE = 64
VTILES = 32
KOCC = 16
JOCC = 2
NROWS = 8192
OCC_I = 128
NEED = 2048
CAP = 20
W_DEV = 320
SLOTS = 40960
NW = 32768
DEVICES = 128


def draw_eri_slot(key, part):
    key = jax.random.fold_in(key, 7)
    k_perm, k_live, k_hot, k_tok, k_pos = jax.random.split(key, 5)
    groups = NW // NEED
    order = jax.vmap(lambda k: jax.random.permutation(k, NEED))(jax.random.split(k_perm, groups))
    seq = jnp.arange(NEED)
    live = jnp.logical_or(seq[None, :] < CAP, jax.random.randint(k_live, (groups, NEED), 0, 10) < 6)
    token_pos = jnp.maximum(jnp.cumsum(live.astype(jnp.int32), axis=1) - 1, 0)
    hottest = jax.random.randint(k_hot, (groups,), 0, DEVICES)
    others = (jnp.arange((DEVICES - 1) * CAP)[None, :] // CAP + hottest[:, None] + 1) % DEVICES
    others = jax.vmap(lambda k, r: jax.random.permutation(k, r))(jax.random.split(k_tok, groups), others)
    tokens = jnp.concatenate([jnp.broadcast_to(hottest[:, None], (groups, CAP)), others], axis=1)
    owner_seq = jnp.where(live, jnp.take_along_axis(tokens, token_pos, axis=1), -1)
    owner = jnp.zeros((groups, NEED), jnp.int32).at[jnp.arange(groups)[:, None], order].set(owner_seq.astype(jnp.int32))
    owner = owner.reshape(NW)
    onehot = (owner[:, None] == jnp.arange(DEVICES)[None, :]).astype(jnp.int32)
    rank_in = jnp.sum((jnp.cumsum(onehot, axis=0) - 1) * onehot, axis=1)
    positions = jax.vmap(lambda k: jax.random.permutation(k, W_DEV))(jax.random.split(k_pos, DEVICES))
    safe_owner = jnp.maximum(owner, 0)
    slot_of = safe_owner * W_DEV + positions[safe_owner, jnp.clip(rank_in, 0, W_DEV - 1)]
    return jnp.where(owner >= 0, slot_of, -1).astype(jnp.int32)


def touch_ends(array, rng, smallest, largest):
    longest = array.shape.index(max(array.shape))
    spots = []
    for shift in (0, 1):
        where = [jax.random.randint(jax.random.fold_in(rng, axis), (), 0, length) for axis, length in enumerate(array.shape)]
        where[longest] = (where[longest] + shift) % array.shape[longest]
        spots.append(tuple(where))
    return array.at[spots[0]].set(smallest).at[spots[1]].set(largest)


def level_of(key, dims, cuts, low, top_value):
    gain, own = 1.0, jax.random.fold_in(key, 6)
    for position, parts in cuts:
        steps = jnp.exp(jax.random.uniform(jax.random.fold_in(own, position), (parts,), jnp.float32, low / len(cuts), top_value / len(cuts)))
        gain = gain * jnp.repeat(steps, dims[position] // parts).reshape([-1 if axis == position else 1 for axis in range(len(dims))])
    return gain


def scatter_about(own_key, shape, width, reach, cuts=(), held_as=jnp.bfloat16):
    array = jax.random.normal(own_key, shape, jnp.float32) * width
    if len(cuts) > 0:
        array = level_of(own_key, shape, cuts, -0.22, 0.18) * array
    return jnp.clip(array, min=-reach, max=reach).astype(held_as)


def setup_inputs(seed: int = 0) -> dict:
    arg_keys = jax.random.split(jax.random.key(seed), 5)
    amplitudes = scatter_about(arg_keys[0], (NROWS, VTILES * KOCC * TILE), 1.0, 6.0, ((0, 8), (1, 16)))
    t2_mask = touch_ends((jax.random.randint(arg_keys[1], (OCC_I, VTILES * KOCC), 0, 10) < 7).astype(jnp.int32), jax.random.fold_in(arg_keys[1], 1), 0, 1)
    eri_tiles = scatter_about(arg_keys[2], (SLOTS, TILE * TILE), (VTILES * KOCC * TILE // 2) ** -0.5, 0.046875, ((0, 128),))
    eri_slot = draw_eri_slot(jax.random.fold_in(arg_keys[4], 71), 0)
    return dict(amplitudes=amplitudes, t2_mask=t2_mask, eri_tiles=eri_tiles, eri_slot=eri_slot)


def reference(amplitudes, t2_mask, eri_tiles, eri_slot):
    block_mask = jnp.repeat(jnp.repeat(t2_mask, TILE, axis=0), TILE, axis=1).astype(jnp.bfloat16)
    masked = amplitudes * block_mask
    padded = jnp.concatenate([eri_tiles, jnp.zeros((1, TILE * TILE), eri_tiles.dtype)], axis=0)
    index = jnp.where(eri_slot < 0, eri_tiles.shape[0], eri_slot).astype(jnp.int32)
    weight = padded[index].reshape(VTILES, KOCC, VTILES, JOCC, TILE, TILE)
    weight = weight.transpose(0, 1, 4, 2, 3, 5).reshape(VTILES * KOCC * TILE, VTILES * JOCC * TILE)
    return jnp.dot(weight.T, masked.T, preferred_element_type=jnp.float32)
```

```python
import functools

import jax
import jax.numpy as jnp
from jax import lax
from jax.experimental import pallas as pl
from jax.experimental.pallas import tpu as pltpu
from jax.sharding import Mesh
from jax.sharding import PartitionSpec as P

TILE = 64
VTILES = 32
KOCC = 16
JOCC = 2
CAP = 20
COLS = 16
ROWS = 8
DEVS = 128
GROUP = VTILES * KOCC * VTILES * JOCC // COLS
KB = GROUP // (VTILES * JOCC)
NB = VTILES * JOCC
SUB = TILE * TILE // 128
BATCH = CAP // 2
EXTRA = 48
CORE = 4 * COLS * BATCH + 4 * EXTRA
THIRD = ROWS * (COLS * BATCH - EXTRA)
POOL = 2 * CORE + THIRD
FAR, NEAR = (2,), (1, 3)
PARTS = 12
HALF = 512
PACKED = HALF + HALF // 16
VMEM_GRANT = 16 * 1024 * 1024


def route_kernel(slots_dev, me_ref, slot_ref, out_ref):
    base = me_ref[0] * slots_dev
    slot = slot_ref[...]
    rows = slot.shape[0]
    per = rows // COLS
    local = slot - base
    mine = jnp.logical_and(local >= 0, local < slots_dev)
    ones = jnp.where(mine, 1.0, 0.0).astype(jnp.bfloat16)
    r = lax.broadcasted_iota(jnp.int32, (128, 128), 0)
    c = lax.broadcasted_iota(jnp.int32, (128, 128), 1)
    before = jnp.where(r < c, 1.0, 0.0).astype(jnp.bfloat16)
    within = jnp.dot(ones, before, preferred_element_type=jnp.float32)
    r = lax.broadcasted_iota(jnp.int32, (rows, rows), 0)
    c = lax.broadcasted_iota(jnp.int32, (rows, rows), 1)
    above = jnp.where(jnp.logical_and(r // per == c // per, c < r), 1.0, 0.0).astype(jnp.bfloat16)
    upto = jnp.dot(above, ones, preferred_element_type=jnp.float32)
    rank = within + jnp.sum(upto, axis=1, keepdims=True)
    rank = jnp.where(mine, rank, -1.0).reshape(COLS, per, 128)
    parity = lax.broadcasted_iota(jnp.int32, (rows, 128), 1) % 2
    local = jnp.where(mine, 2 * local + parity, 0).astype(jnp.float32).reshape(COLS, per, 128)
    lane = lax.broadcasted_iota(jnp.int32, (COLS, 128), 1)
    out = jnp.zeros((COLS, 128), jnp.float32)
    for j in range(CAP):
        picked = jnp.sum(jnp.where(rank == float(j), local, 0.0), axis=1)
        out = jnp.where(lane == j, jnp.sum(picked, axis=1, keepdims=True), out)
    out_ref[...] = out.astype(jnp.int32)


def fill_kernel(index_ref, tiles_ref, first_ref, second_ref):
    def group(g, carry):
        codes = [index_ref[g, j] for j in range(CAP)]
        tiles = [tiles_ref[code // 2] for code in codes]
        for j in range(CAP):
            turned = jnp.concatenate([tiles[j][:, TILE:], tiles[j][:, :TILE]], axis=1)
            tiles[j] = jnp.where(codes[j] % 2 == 1, turned, tiles[j])
        for j in range(CAP):
            out_ref = first_ref if j < BATCH else second_ref
            out_ref[g * BATCH + j % BATCH] = tiles[j]
        return carry

    lax.fori_loop(0, COLS, group, 0)


def compact_kernel(index_ref, tiles_ref, first_ref, second_ref):
    def place(out_ref, base):
        def body(i, carry):
            tiles = [tiles_ref[index_ref[base + i * 16 + k]] for k in range(16)]
            for k in range(16):
                out_ref[i * 16 + k] = tiles[k]
            return carry

        lax.fori_loop(0, out_ref.shape[0] // 16, body, 0)

    place(first_ref, 0)
    place(second_ref, EXTRA)


def prep_kernel(mask_ref, amp_ref, even_ref, odd_ref):
    blk = pl.program_id(0)
    rows = amp_ref.shape[0]
    r = lax.broadcasted_iota(jnp.int32, (256, 256), 0)
    c = lax.broadcasted_iota(jnp.int32, (256, 256), 1)
    source = (c % 128 // SUB) * TILE + 2 * (c % SUB) + c // 128
    shuffle = jnp.where(r == source, 1.0, 0.0).astype(jnp.bfloat16)
    moved = jnp.dot(amp_ref[...], shuffle, preferred_element_type=jnp.float32)
    mask = mask_ref[...].astype(jnp.bfloat16)
    r = lax.broadcasted_iota(jnp.int32, (mask.shape[1], 128), 0)
    c = lax.broadcasted_iota(jnp.int32, (mask.shape[1], 128), 1)
    spread = jnp.where(r == 4 * blk + c // SUB, 1.0, 0.0).astype(jnp.bfloat16)
    wide = jnp.dot(mask, spread, preferred_element_type=jnp.float32).astype(jnp.bfloat16)
    r = lax.broadcasted_iota(jnp.int32, (rows, mask.shape[0]), 0)
    c = lax.broadcasted_iota(jnp.int32, (rows, mask.shape[0]), 1)
    tall = jnp.where(r // TILE == c, 1.0, 0.0).astype(jnp.bfloat16)
    full = jnp.dot(tall, wide, preferred_element_type=jnp.float32)
    even_ref[...] = (moved[:, :128] * full).astype(jnp.bfloat16)
    odd_ref[...] = (moved[:, 128:] * full).astype(jnp.bfloat16)


def pack(out_ref, value):
    value = value.reshape(HALF // 16, 16, 128)
    top = jnp.maximum(jnp.max(jnp.abs(value), axis=1), 1e-30)
    exponent = jnp.ceil(jnp.log2(top * 1.0001))
    scaled = jnp.round(value * jnp.exp2(15.0 - exponent)[:, None, :]).reshape(HALF, 128)
    out_ref[pl.ds(0, HALF)] = scaled.astype(jnp.int32).astype(jnp.int16)
    out_ref[pl.ds(HALF, HALF // 16)] = exponent.astype(jnp.int32).astype(jnp.int16)


def unpack(ref):
    mantissa = ref[pl.ds(0, HALF)].astype(jnp.int32).astype(jnp.float32)
    exponent = ref[pl.ds(HALF, HALF // 16)].astype(jnp.int32).astype(jnp.float32)
    value = mantissa.reshape(HALF // 16, 16, 128) * jnp.exp2(exponent - 15.0)[:, None, :]
    return value.reshape(HALF, 128)


def collect_kernel(misc_ref, *refs):
    parts, third_ref, tiles, sems = refs[:PARTS], refs[PARTS], refs[PARTS + 1], refs[PARTS + 2]
    copies, base = [], 0
    for k, part in enumerate(parts):
        size = part.shape[0]
        copies.append(pltpu.make_async_copy(part, tiles.at[pl.ds(base, size)], sems.at[k]))
        base += size
    for copy in copies:
        copy.start()
    tiles[pl.ds(POOL, 1)] = jnp.zeros((1, SUB, 128), jnp.bfloat16)

    @pl.when(misc_ref[2] > 0)
    def _():
        copy = pltpu.make_async_copy(third_ref, tiles.at[pl.ds(base, THIRD)], sems.at[PARTS])
        copy.start()
        copy.wait()

    for copy in copies:
        copy.wait()


def collect_call(misc, parts, third):
    return pl.pallas_call(
        collect_kernel,
        in_specs=[pl.BlockSpec(memory_space=pltpu.SMEM)] + [pl.BlockSpec(memory_space=pl.ANY)] * (PARTS + 1),
        out_specs=pl.BlockSpec(memory_space=pltpu.VMEM),
        out_shape=jax.ShapeDtypeStruct((POOL + 1, SUB, 128), jnp.bfloat16),
        scratch_shapes=[pltpu.SemaphoreType.DMA((PARTS + 1,))],
        compiler_params=pltpu.CompilerParams(vmem_limit_bytes=VMEM_GRANT),
        cost_estimate=pl.CostEstimate(flops=0, bytes_accessed=POOL * 8192, transcendentals=0),
        name="collect",
    )(misc, *parts, third)


def build(hop, unit, index_ref, misc_ref, tiles, weight):
    at = [((misc_ref[0] + hop) % 4 * 4 + unit) * 4, (unit * 4 + (misc_ref[1] + hop) % 4) * 4 + 2]
    left = lax.broadcasted_iota(jnp.int32, (SUB, 128), 1) < TILE
    for kb in range(KB):
        picked = [tiles[index_ref[kb * NB + at[pair] + k]] for pair in range(2) for k in range(2)]
        rows = slice(kb * SUB, (kb + 1) * SUB)
        for pair in range(2):
            one, two = picked[2 * pair : 2 * pair + 2]
            columns = slice(128 * pair, 128 * pair + 128)
            weight[0][rows, columns] = jnp.where(left, one, two)
            weight[1][rows, columns] = jnp.where(left, two, one)


def product_kernel(hops, index_ref, misc_ref, even_ref, odd_ref, tiles, *refs):
    outs, weights = refs[:-4], (refs[-4:-2], refs[-2:])
    build(hops[0], 0, index_ref, misc_ref, tiles, weights[0])

    def emit(at, unit, weight):
        straight = jnp.dot(even_ref[...], weight[0][...], preferred_element_type=jnp.float32)
        crossed = jnp.dot(odd_ref[...], weight[1][...], preferred_element_type=jnp.float32)
        for way in range(2):
            columns = slice(way * 128, way * 128 + 128)
            value = straight[:, columns] + pltpu.roll(crossed[:, columns], TILE, 1)
            if hops == (0,):
                outs[way][unit] = value
                continue
            for half in range(2):
                out_ref = outs[2 * way + half] if hops == FAR else outs[2 * way + at].at[half]
                pack(out_ref.at[unit], value[half * HALF : (half + 1) * HALF])

    for at, hop in enumerate(hops):
        after = hops[min(at + 1, len(hops) - 1)]

        def two_units(i, carry, at=at, hop=hop, after=after):
            build(hop, 2 * i + 1, index_ref, misc_ref, tiles, weights[1])
            emit(at, 2 * i, weights[0])
            build(jnp.where(i == 0, hop, after), 2 - 2 * i, index_ref, misc_ref, tiles, weights[0])
            emit(at, 2 * i + 1, weights[1])
            return carry

        lax.fori_loop(0, 2, two_units, 0)


def product_call(name, hops, scalars, even, odd, tiles):
    rows_dev, depth_half = even.shape
    vmem = pl.BlockSpec(memory_space=pltpu.VMEM)
    if hops == FAR:
        outs = [jax.ShapeDtypeStruct((4, PACKED, 128), jnp.int16)] * 4
    elif hops == NEAR:
        outs = [jax.ShapeDtypeStruct((2, 4, PACKED, 128), jnp.int16)] * 4
    else:
        outs = [jax.ShapeDtypeStruct((4, rows_dev, 128), jnp.float32)] * 2
    return pl.pallas_call(
        functools.partial(product_kernel, hops),
        grid_spec=pltpu.PrefetchScalarGridSpec(
            num_scalar_prefetch=2,
            grid=(),
            in_specs=[vmem] * 3,
            out_specs=[vmem] * len(outs),
            scratch_shapes=[pltpu.VMEM((depth_half, 256), jnp.bfloat16)] * 4,
        ),
        out_shape=outs,
        compiler_params=pltpu.CompilerParams(vmem_limit_bytes=VMEM_GRANT),
        cost_estimate=pl.CostEstimate(
            flops=8 * len(hops) * rows_dev * depth_half * 512, bytes_accessed=POOL * 8192, transcendentals=0
        ),
        name=name,
    )(*scalars, even, odd, tiles)


def ahead(axis, value):
    return lax.ppermute(value, axis, [(i, (i + 1) % 4) for i in range(4)])


def behind(axis, value):
    return lax.ppermute(value, axis, [(i, (i + 3) % 4) for i in range(4)])


def reach(tiles):
    return ahead("y", tiles), behind("y", tiles)


def swap(parts):
    return [lax.ppermute(part, "core", [(0, 1), (1, 0)]) for part in parts]


def add_first_kernel(*refs):
    def body(i, carry):
        for way in range(2):
            ahead_in, behind_in, came_a, came_b = refs[4 * way : 4 * way + 4]
            ahead_out, behind_out = refs[8 + 2 * way : 10 + 2 * way]
            pack(ahead_out.at[0, i], unpack(ahead_in.at[0, i]) + unpack(came_a.at[i]))
            ahead_out[1, i] = ahead_in[1, i]
            behind_out[0, i] = behind_in[0, i]
            pack(behind_out.at[1, i], unpack(behind_in.at[1, i]) + unpack(came_b.at[i]))
        return carry

    lax.fori_loop(0, 4, body, 0)


def add_second_kernel(*refs):
    for way in range(2):
        ahead_in, behind_in, came_a, came_b = refs[4 * way : 4 * way + 4]
        ahead_out, behind_out = refs[8 + 2 * way : 10 + 2 * way]
        pack(ahead_out.at[0], unpack(ahead_in.at[0]) + unpack(came_a.at[0]))
        ahead_out[1] = ahead_in[1]
        behind_out[0] = behind_in[0]
        pack(behind_out.at[1], unpack(behind_in.at[1]) + unpack(came_b.at[0]))


def whole_call(body, name, outs, *arrays, scalars=()):
    vmem = pl.BlockSpec(memory_space=pltpu.VMEM)
    size = sum(a.size * a.dtype.itemsize for a in [*arrays, *outs])
    return pl.pallas_call(
        body,
        in_specs=[pl.BlockSpec(memory_space=pltpu.SMEM)] * len(scalars) + [vmem] * len(arrays),
        out_specs=[vmem] * len(outs),
        out_shape=outs,
        compiler_params=pltpu.CompilerParams(vmem_limit_bytes=VMEM_GRANT),
        cost_estimate=pl.CostEstimate(flops=10 * size, bytes_accessed=size, transcendentals=0),
        name=name,
    )(*scalars, *arrays)


def middle_kernel(misc_ref, one_ref, two_ref, *refs):
    came, outs, own_ref = refs[:4], refs[4:12], refs[12]
    for way, own in enumerate((one_ref, two_ref)):
        right, left = came[2 * way : 2 * way + 2]
        far_a, far_b, ahead_ref, behind_ref = outs[4 * way : 4 * way + 4]
        for hop, ahead_by in enumerate((2, 1, 3, 0)):
            at = (misc_ref[1 - way] + ahead_by) % 4
            total = [
                own[at, pl.ds(half * HALF, HALF)] + unpack(right.at[half, at]) + unpack(left.at[half, at])
                for half in range(2)
            ]
            for half in range(2):
                if hop == 0:
                    pack((far_a, far_b)[half].at[0], total[half])
                elif hop < 3:
                    pack((ahead_ref, behind_ref)[hop - 1].at[half], total[half])
                else:
                    own_ref[pl.ds(half * HALF, HALF), pl.ds(way * 128, 128)] = total[half]


def last_kernel(own_ref, *refs):
    came, out_ref = refs[:4], refs[4]
    for way in range(2):
        right, left = came[2 * way : 2 * way + 2]
        columns = pl.ds(way * 128, 128)
        for half in range(2):
            rows = pl.ds(half * HALF, HALF)
            total = own_ref[rows, columns] + unpack(right.at[half]) + unpack(left.at[half])
            out_ref[columns, rows] = total.T


def shards(amplitudes, t2_mask, eri_tiles, eri_slot):
    y, core, x, z = (lax.axis_index(name) for name in ("y", "core", "x", "z"))
    group = x * 4 + z
    myself = (y * 2 + core) * COLS + group
    rows_dev, depth_dev = amplitudes.shape
    slots_dev = eri_tiles.shape[0]

    send_index = pl.pallas_call(
        lambda *refs: route_kernel(slots_dev, *refs),
        out_shape=jax.ShapeDtypeStruct((COLS, 128), jnp.int32),
        in_specs=[
            pl.BlockSpec(memory_space=pltpu.SMEM),
            pl.BlockSpec(memory_space=pltpu.VMEM),
        ],
        out_specs=pl.BlockSpec(memory_space=pltpu.VMEM),
        compiler_params=pltpu.CompilerParams(vmem_limit_bytes=VMEM_GRANT),
        name="route",
    )(myself.reshape(1).astype(jnp.int32), eri_slot.reshape(-1, 128))
    vmem = pl.BlockSpec(memory_space=pltpu.VMEM)
    batch = jax.ShapeDtypeStruct((COLS * BATCH, SUB, 128), jnp.bfloat16)
    outgoing = pl.pallas_call(
        fill_kernel,
        grid_spec=pltpu.PrefetchScalarGridSpec(
            num_scalar_prefetch=1, grid=(), in_specs=[vmem], out_specs=[vmem] * 2
        ),
        out_shape=[batch] * 2,
        compiler_params=pltpu.CompilerParams(vmem_limit_bytes=VMEM_GRANT),
        name="fill",
    )(send_index, eri_tiles.reshape(slots_dev, SUB, 128))
    def send(part):
        part = part.reshape(COLS, BATCH, SUB, 128)
        part = lax.all_to_all(part, ("x", "z"), split_axis=0, concat_axis=0, tiled=True)
        return part.reshape(COLS * BATCH, SUB, 128)

    first = send(outgoing[0])
    first, second, eri_slot = lax.optimization_barrier((first, outgoing[1], eri_slot))
    up, down = reach(first)
    second = send(second)

    devices = jnp.arange(DEVS, dtype=jnp.int32)
    owner_all = jnp.where(eri_slot >= 0, eri_slot // slots_dev, -1).reshape(COLS, 1, GROUP)
    held = jnp.sum((owner_all == devices[None, :, None]).astype(jnp.int32), axis=2)
    tail = jnp.maximum(held - BATCH, 0).reshape(COLS, ROWS, COLS)
    spill = jnp.any(jnp.sum(tail, axis=2) > EXTRA)
    tail = lax.dynamic_index_in_dim(tail, group, 0, keepdims=False)
    upto = jnp.sum(jnp.where(jnp.arange(COLS)[:, None] >= jnp.arange(COLS)[None, :], tail[:, None, :], 0), axis=2)
    start = upto - tail
    mine_upto = lax.dynamic_index_in_dim(upto, y * 2 + core, 0, keepdims=False)
    mine_start = lax.dynamic_index_in_dim(start, y * 2 + core, 0, keepdims=False)
    spot = jnp.arange(COLS * BATCH, dtype=jnp.int32)
    inside = jnp.logical_and(spot[:, None] >= mine_start[None, :], spot[:, None] < mine_upto[None, :])
    source = jnp.arange(COLS, dtype=jnp.int32)[None, :] * BATCH + spot[:, None] - mine_start[None, :]
    source = jnp.sum(jnp.where(inside, source, 0), axis=1).astype(jnp.int32)
    some, rest = pl.pallas_call(
        compact_kernel,
        grid_spec=pltpu.PrefetchScalarGridSpec(
            num_scalar_prefetch=1, grid=(), in_specs=[vmem], out_specs=[vmem] * 2
        ),
        out_shape=[
            jax.ShapeDtypeStruct((EXTRA, SUB, 128), jnp.bfloat16),
            jax.ShapeDtypeStruct((COLS * BATCH - EXTRA, SUB, 128), jnp.bfloat16),
        ],
        compiler_params=pltpu.CompilerParams(vmem_limit_bytes=VMEM_GRANT),
        name="compact",
    )(source, second)
    wanted = lax.dynamic_slice_in_dim(eri_slot, group * GROUP, GROUP)
    up, down, amplitudes, wanted = lax.optimization_barrier((up, down, amplitudes, wanted))
    half = COLS * BATCH // 2
    from_up = ahead("y", jnp.concatenate([up[:half], some]))
    from_down = behind("y", jnp.concatenate([down[half:], some]))
    parted = jax.ShapeDtypeStruct((rows_dev, depth_dev // 2), jnp.bfloat16)
    even, odd = pl.pallas_call(
        prep_kernel,
        grid=(depth_dev // 256,),
        out_shape=[parted] * 2,
        in_specs=[
            pl.BlockSpec(t2_mask.shape, lambda i: (0, 0)),
            pl.BlockSpec((rows_dev, 256), lambda i: (0, i)),
        ],
        out_specs=[pl.BlockSpec((rows_dev, 128), lambda i: (0, i))] * 2,
        compiler_params=pltpu.CompilerParams(vmem_limit_bytes=VMEM_GRANT),
        name="prep",
    )(t2_mask, amplitudes)

    owner = jnp.where(wanted >= 0, wanted // slots_dev, -1)
    mine = owner[:, None] == devices[None, :]
    spot = jnp.arange(GROUP, dtype=jnp.int32)
    before = (spot[:, None] > spot[None, :]).astype(jnp.bfloat16)
    counts = jnp.dot(before, mine.astype(jnp.bfloat16), preferred_element_type=jnp.float32)
    rank = jnp.sum(jnp.where(mine, counts, 0.0), axis=1).astype(jnp.int32)
    begin = jnp.sum(jnp.where(mine, start.reshape(1, DEVS), 0), axis=1)
    behind_first = begin + rank - BATCH
    owner_row = owner // COLS
    turn = (owner_row // 2 - y) % 4
    turn = jnp.where(turn == 1, 2, jnp.where(turn == 2, 3, jnp.where(turn == 3, 1, 0)))
    size = COLS * BATCH
    slot = owner % COLS * BATCH + rank
    early = turn * size + slot + jnp.where(jnp.logical_and(turn == 3, slot >= half), EXTRA, 0)
    begins = (4 * size + 2 * EXTRA, 3 * size + half, 4 * size + EXTRA, 4 * size + 3 * EXTRA)
    late = behind_first + sum(jnp.where(turn == k, begin_late, 0) for k, begin_late in enumerate(begins))
    tile_index = jnp.where(rank < BATCH, early, late) + CORE * (owner_row % 2 != core)
    spilled = 2 * CORE + owner_row * (size - EXTRA) + behind_first - EXTRA
    tile_index = jnp.where(jnp.logical_or(rank < BATCH, behind_first < EXTRA), tile_index, spilled)
    tile_index = jnp.where(wanted < 0, POOL, tile_index)
    misc = jnp.stack([x, z, spill.astype(jnp.int32)]).astype(jnp.int32)
    third = lax.cond(
        misc[2] > 0,
        lambda value: lax.all_gather(value, ("y", "core"), axis=0, tiled=True),
        lambda value: jnp.zeros((THIRD, SUB, 128), jnp.bfloat16),
        rest,
    )
    from_up, from_down, even, odd, tile_index, misc, third = lax.optimization_barrier(
        (from_up, from_down, even, odd, tile_index, misc, third)
    )
    tail = jnp.concatenate(
        [
            some,
            ahead("y", from_up[half : half + EXTRA // 2]),
            behind("y", from_down[half + EXTRA // 2 :]),
        ]
    )
    same = [first, up, down, from_up, from_down, tail]
    tiles = collect_call(misc, same + swap(same), third)

    scalars, arrays = (tile_index, misc), (even, odd, tiles)
    far = product_call("far", FAR, scalars, *arrays)
    near = product_call("near", NEAR, scalars, *arrays)
    axes = ("x", "z")
    inputs = []
    for way, axis in enumerate(axes):
        inputs += [*near[2 * way : 2 * way + 2], ahead(axis, far[2 * way]), behind(axis, far[2 * way + 1])]
    packed = jax.ShapeDtypeStruct((2, 4, PACKED, 128), jnp.int16)
    added = whole_call(add_first_kernel, "add_first", [packed] * 4, *inputs)
    came = []
    for way, axis in enumerate(axes):
        came += [ahead(axis, added[2 * way]), behind(axis, added[2 * way + 1])]
    one, two = product_call("own", (0,), scalars, *arrays)
    single = jax.ShapeDtypeStruct((1, PACKED, 128), jnp.int16)
    double = jax.ShapeDtypeStruct((2, PACKED, 128), jnp.int16)
    *outs, own = whole_call(
        middle_kernel,
        "middle",
        [single, single, double, double] * 2 + [jax.ShapeDtypeStruct((rows_dev, 256), jnp.float32)],
        one,
        two,
        *came,
        scalars=(misc,),
    )
    axes = ("z", "x")
    inputs = []
    for way, axis in enumerate(axes):
        far_a, far_b, next_ab, prev_ab = outs[4 * way : 4 * way + 4]
        inputs += [next_ab, prev_ab, ahead(axis, far_a), behind(axis, far_b)]
    added = whole_call(add_second_kernel, "add_second", [double] * 4, *inputs)
    came = []
    for way, axis in enumerate(axes):
        came += [ahead(axis, added[2 * way]), behind(axis, added[2 * way + 1])]
    return whole_call(
        last_kernel, "last", [jax.ShapeDtypeStruct((256, rows_dev), jnp.float32)], own, *came
    )[0]


def solution(mesh):
    axes = ("y", "core", "x", "z")
    fine = Mesh(mesh.devices.reshape(4, 2, 4, 4), axes)
    row, col = ("y", "core"), ("x", "z")
    in_specs = (P(row, col), P(row, col), P(axes, None), P())
    out_specs = P(col, row)
    return jax.shard_map(shards, mesh=fine, in_specs=in_specs, out_specs=out_specs, check_vma=False)
```

```python
import functools

import jax
import jax.numpy as jnp
from jax import lax
from jax.experimental import pallas as pl
from jax.experimental.pallas import tpu as pltpu
from jax.sharding import Mesh
from jax.sharding import PartitionSpec as P

TILE = 64
VTILES = 32
KOCC = 16
JOCC = 2
CAP = 20
COLS = 16
ROWS = 8
DEVS = 128
GROUP = VTILES * KOCC * VTILES * JOCC // COLS
KB = GROUP // (VTILES * JOCC)
NB = VTILES * JOCC
SUB = TILE * TILE // 128
BATCH = CAP // 2
EXTRA = 48
CORE = 4 * COLS * BATCH + 4 * EXTRA
THIRD = ROWS * (COLS * BATCH - EXTRA)
POOL = 2 * CORE + THIRD
PARTS = 12
HALF = 512
PACKED = HALF + HALF // 16
VMEM_GRANT = 10 * 1024 * 1024


def route_kernel(slots_dev, me_ref, slot_ref, out_ref):
    base = me_ref[0] * slots_dev
    slot = slot_ref[...]
    rows = slot.shape[0]
    per = rows // COLS
    local = slot - base
    mine = jnp.logical_and(local >= 0, local < slots_dev)
    ones = jnp.where(mine, 1.0, 0.0).astype(jnp.bfloat16)
    r = lax.broadcasted_iota(jnp.int32, (128, 128), 0)
    c = lax.broadcasted_iota(jnp.int32, (128, 128), 1)
    before = jnp.where(r < c, 1.0, 0.0).astype(jnp.bfloat16)
    within = jnp.dot(ones, before, preferred_element_type=jnp.float32)
    r = lax.broadcasted_iota(jnp.int32, (rows, rows), 0)
    c = lax.broadcasted_iota(jnp.int32, (rows, rows), 1)
    above = jnp.where(jnp.logical_and(r // per == c // per, c < r), 1.0, 0.0).astype(jnp.bfloat16)
    upto = jnp.dot(above, ones, preferred_element_type=jnp.float32)
    rank = within + jnp.sum(upto, axis=1, keepdims=True)
    rank = jnp.where(mine, rank, -1.0).reshape(COLS, per, 128)
    parity = lax.broadcasted_iota(jnp.int32, (rows, 128), 1) % 2
    local = jnp.where(mine, 2 * local + parity, 0).astype(jnp.float32).reshape(COLS, per, 128)
    lane = lax.broadcasted_iota(jnp.int32, (COLS, 128), 1)
    out = jnp.zeros((COLS, 128), jnp.float32)
    for j in range(CAP):
        picked = jnp.sum(jnp.where(rank == float(j), local, 0.0), axis=1)
        out = jnp.where(lane == j, jnp.sum(picked, axis=1, keepdims=True), out)
    out_ref[...] = out.astype(jnp.int32)


def fill_kernel(index_ref, tiles_ref, first_ref, second_ref, filled, sems):
    copies = []
    for k, out_ref in enumerate((first_ref, second_ref)):

        def group(g, carry, k=k):
            codes = [index_ref[g, k * BATCH + j] for j in range(BATCH)]
            tiles = [tiles_ref[code // 2] for code in codes]
            for j in range(BATCH):
                turned = jnp.concatenate([tiles[j][:, TILE:], tiles[j][:, :TILE]], axis=1)
                filled[k, g * BATCH + j] = jnp.where(codes[j] % 2 == 1, turned, tiles[j])
            return carry

        lax.fori_loop(0, COLS, group, 0)
        copies.append(pltpu.make_async_copy(filled.at[k], out_ref, sems.at[k]))
        copies[k].start()
    for copy in copies:
        copy.wait()


def mix_kernel(index_ref, second_ref, up_ref, down_ref, up_out, down_out, some_out, rest_out, sems):
    half = COLS * BATCH // 2
    copies = [
        pltpu.make_async_copy(up_ref.at[pl.ds(0, half)], up_out.at[pl.ds(0, half)], sems.at[0]),
        pltpu.make_async_copy(down_ref.at[pl.ds(half, half)], down_out.at[pl.ds(0, half)], sems.at[1]),
    ]
    for copy in copies:
        copy.start()

    def body(i, carry):
        tiles = [second_ref[index_ref[i * 16 + k]] for k in range(16)]
        for k in range(16):
            some_out[i * 16 + k] = tiles[k]
        return carry

    lax.fori_loop(0, EXTRA // 16, body, 0)
    copies += [
        pltpu.make_async_copy(some_out, up_out.at[pl.ds(half, EXTRA)], sems.at[2]),
        pltpu.make_async_copy(some_out, down_out.at[pl.ds(half, EXTRA)], sems.at[3]),
    ]
    for copy in copies[2:]:
        copy.start()

    def body_rest(i, carry):
        tiles = [second_ref[index_ref[EXTRA + i * 16 + k]] for k in range(16)]
        for k in range(16):
            rest_out[i * 16 + k] = tiles[k]
        return carry

    lax.fori_loop(0, (COLS * BATCH - EXTRA) // 16, body_rest, 0)
    for copy in copies:
        copy.wait()


def prep_kernel(mask_ref, amp_ref, even_ref, odd_ref):
    blk = pl.program_id(0)
    rows = amp_ref.shape[0]
    r = lax.broadcasted_iota(jnp.int32, (256, 256), 0)
    c = lax.broadcasted_iota(jnp.int32, (256, 256), 1)
    source = (c % 128 // SUB) * TILE + 2 * (c % SUB) + c // 128
    shuffle = jnp.where(r == source, 1.0, 0.0).astype(jnp.bfloat16)
    moved = jnp.dot(amp_ref[...], shuffle, preferred_element_type=jnp.float32)
    mask = mask_ref[...].astype(jnp.bfloat16)
    r = lax.broadcasted_iota(jnp.int32, (mask.shape[1], 128), 0)
    c = lax.broadcasted_iota(jnp.int32, (mask.shape[1], 128), 1)
    spread = jnp.where(r == 4 * blk + c // SUB, 1.0, 0.0).astype(jnp.bfloat16)
    wide = jnp.dot(mask, spread, preferred_element_type=jnp.float32).astype(jnp.bfloat16)
    r = lax.broadcasted_iota(jnp.int32, (rows, mask.shape[0]), 0)
    c = lax.broadcasted_iota(jnp.int32, (rows, mask.shape[0]), 1)
    tall = jnp.where(r // TILE == c, 1.0, 0.0).astype(jnp.bfloat16)
    full = jnp.dot(tall, wide, preferred_element_type=jnp.float32)
    even_ref[...] = (moved[:, :128] * full).astype(jnp.bfloat16)
    odd_ref[...] = (moved[:, 128:] * full).astype(jnp.bfloat16)


def pack(out_ref, value):
    value = value.reshape(HALF // 16, 16, 128)
    top = jnp.maximum(jnp.max(jnp.abs(value), axis=1), 1e-30)
    exponent = jnp.ceil(jnp.log2(top * 1.0001))
    scaled = jnp.round(value * jnp.exp2(15.0 - exponent)[:, None, :]).reshape(HALF, 128)
    out_ref[pl.ds(0, HALF)] = scaled.astype(jnp.int32).astype(jnp.int16)
    out_ref[pl.ds(HALF, HALF // 16)] = exponent.astype(jnp.int32).astype(jnp.int16)


def unpack(ref):
    mantissa = ref[pl.ds(0, HALF)].astype(jnp.int32).astype(jnp.float32)
    exponent = ref[pl.ds(HALF, HALF // 16)].astype(jnp.int32).astype(jnp.float32)
    value = mantissa.reshape(HALF // 16, 16, 128) * jnp.exp2(exponent - 15.0)[:, None, :]
    return value.reshape(HALF, 128)


def collect_kernel(misc_ref, *refs):
    parts, third_ref, tiles, sems = refs[:PARTS], refs[PARTS], refs[PARTS + 1], refs[PARTS + 2]
    copies, base = [], 0
    for k, part in enumerate(parts):
        size = part.shape[0]
        copies.append(pltpu.make_async_copy(part, tiles.at[pl.ds(base, size)], sems.at[k]))
        base += size
    for copy in copies:
        copy.start()
    tiles[pl.ds(POOL, 1)] = jnp.zeros((1, SUB, 128), jnp.bfloat16)

    @pl.when(misc_ref[2] > 0)
    def _():
        copy = pltpu.make_async_copy(third_ref, tiles.at[pl.ds(base, THIRD)], sems.at[PARTS])
        copy.start()
        copy.wait()

    for copy in copies:
        copy.wait()


def collect_call(misc, parts, third):
    return pl.pallas_call(
        collect_kernel,
        in_specs=[pl.BlockSpec(memory_space=pltpu.SMEM)] + [pl.BlockSpec(memory_space=pl.ANY)] * (PARTS + 1),
        out_specs=pl.BlockSpec(memory_space=pltpu.VMEM),
        out_shape=jax.ShapeDtypeStruct((POOL + 1, SUB, 128), jnp.bfloat16),
        scratch_shapes=[pltpu.SemaphoreType.DMA((PARTS + 1,))],
        compiler_params=pltpu.CompilerParams(vmem_limit_bytes=VMEM_GRANT),
        cost_estimate=pl.CostEstimate(flops=0, bytes_accessed=POOL * 8192, transcendentals=0),
        name="collect",
    )(misc, *parts, third)


def build(hop, unit, index_ref, misc_ref, tiles, weight):
    at = [((misc_ref[0] + hop) % 4 * 4 + unit) * 4, (unit * 4 + (misc_ref[1] + hop) % 4) * 4 + 2]
    left = lax.broadcasted_iota(jnp.int32, (SUB, 128), 1) < TILE
    for kb in range(KB):
        picked = [tiles[index_ref[kb * NB + at[pair] + k]] for pair in range(2) for k in range(2)]
        rows = slice(kb * SUB, (kb + 1) * SUB)
        for pair in range(2):
            one, two = picked[2 * pair : 2 * pair + 2]
            columns = slice(128 * pair, 128 * pair + 128)
            weight[0][rows, columns] = jnp.where(left, one, two)
            weight[1][rows, columns] = jnp.where(left, two, one)


def product_kernel(hops, index_ref, misc_ref, even_ref, odd_ref, tiles, *refs):
    outs, weights = refs[:-4], (refs[-4:-2], refs[-2:])
    build(hops[0], 0, index_ref, misc_ref, tiles, weights[0])

    def emit(at, unit, weight):
        straight = jnp.dot(even_ref[...], weight[0][...], preferred_element_type=jnp.float32)
        crossed = jnp.dot(odd_ref[...], weight[1][...], preferred_element_type=jnp.float32)
        for way in range(2):
            columns = slice(way * 128, way * 128 + 128)
            value = straight[:, columns] + pltpu.roll(crossed[:, columns], TILE, 1)
            if hops == (0,):
                outs[way][unit] = value
                continue
            for half in range(2):
                out_ref = outs[2 * way + half] if len(hops) == 1 else outs[2 * way + at].at[half]
                pack(out_ref.at[unit], value[half * HALF : (half + 1) * HALF])

    for at, hop in enumerate(hops):
        after = hops[min(at + 1, len(hops) - 1)]

        def two_units(i, carry, at=at, hop=hop, after=after):
            build(hop, 2 * i + 1, index_ref, misc_ref, tiles, weights[1])
            emit(at, 2 * i, weights[0])
            build(jnp.where(i == 0, hop, after), 2 - 2 * i, index_ref, misc_ref, tiles, weights[0])
            emit(at, 2 * i + 1, weights[1])
            return carry

        lax.fori_loop(0, 2, two_units, 0)


def product_call(name, hops, scalars, arrays):
    rows_dev, depth_half = arrays[0].shape
    vmem = pl.BlockSpec(memory_space=pltpu.VMEM)
    if hops == (0,):
        outs = [jax.ShapeDtypeStruct((4, rows_dev, 128), jnp.float32)] * 2
    elif len(hops) == 1:
        outs = [jax.ShapeDtypeStruct((4, PACKED, 128), jnp.int16)] * 4
    else:
        outs = [jax.ShapeDtypeStruct((2, 4, PACKED, 128), jnp.int16)] * 4
    handed = [] if hops == (0,) else [jax.ShapeDtypeStruct(a.shape, a.dtype) for a in arrays]
    result = pl.pallas_call(
        functools.partial(product_kernel, hops),
        grid_spec=pltpu.PrefetchScalarGridSpec(
            num_scalar_prefetch=2,
            grid=(),
            in_specs=[vmem] * 3,
            out_specs=[vmem] * (len(outs) + len(handed)),
            scratch_shapes=[pltpu.VMEM((depth_half, 256), jnp.bfloat16)] * 4,
        ),
        out_shape=outs + handed,
        input_output_aliases={2 + k: len(outs) + k for k in range(len(handed))},
        compiler_params=pltpu.CompilerParams(vmem_limit_bytes=VMEM_GRANT),
        cost_estimate=pl.CostEstimate(
            flops=8 * len(hops) * rows_dev * depth_half * 512, bytes_accessed=POOL * 8192, transcendentals=0
        ),
        name=name,
    )(*scalars, *arrays)
    return result[: len(outs)], result[len(outs) :]


def ahead(axis, value):
    return lax.ppermute(value, axis, [(i, (i + 1) % 4) for i in range(4)])


def behind(axis, value):
    return lax.ppermute(value, axis, [(i, (i + 3) % 4) for i in range(4)])


def reach(tiles):
    return ahead("y", tiles), behind("y", tiles)


def swap(parts):
    return [lax.ppermute(part, "core", [(0, 1), (1, 0)]) for part in parts]


def add_first_kernel(*refs):
    def body(i, carry):
        for way in range(2):
            ahead_in, behind_in, came_a, came_b = refs[4 * way : 4 * way + 4]
            ahead_out, behind_out = refs[8 + 2 * way : 10 + 2 * way]
            pack(ahead_out.at[0, i], unpack(ahead_in.at[0, i]) + unpack(came_a.at[i]))
            ahead_out[1, i] = ahead_in[1, i]
            behind_out[0, i] = behind_in[0, i]
            pack(behind_out.at[1, i], unpack(behind_in.at[1, i]) + unpack(came_b.at[i]))
        return carry

    lax.fori_loop(0, 4, body, 0)


def add_second_kernel(*refs):
    for way in range(2):
        ahead_in, behind_in, came_a, came_b = refs[4 * way : 4 * way + 4]
        ahead_out, behind_out = refs[8 + 2 * way : 10 + 2 * way]
        pack(ahead_out.at[0], unpack(ahead_in.at[0]) + unpack(came_a.at[0]))
        ahead_out[1] = ahead_in[1]
        behind_out[0] = behind_in[0]
        pack(behind_out.at[1], unpack(behind_in.at[1]) + unpack(came_b.at[0]))


def whole_call(body, name, outs, *arrays, scalars=()):
    vmem = pl.BlockSpec(memory_space=pltpu.VMEM)
    size = sum(a.size * a.dtype.itemsize for a in [*arrays, *outs])
    return pl.pallas_call(
        body,
        in_specs=[pl.BlockSpec(memory_space=pltpu.SMEM)] * len(scalars) + [vmem] * len(arrays),
        out_specs=[vmem] * len(outs),
        out_shape=outs,
        compiler_params=pltpu.CompilerParams(vmem_limit_bytes=VMEM_GRANT),
        cost_estimate=pl.CostEstimate(flops=10 * size, bytes_accessed=size, transcendentals=0),
        name=name,
    )(*scalars, *arrays)


def middle_kernel(misc_ref, one_ref, two_ref, *refs):
    came, outs, own_ref = refs[:4], refs[4:12], refs[12]
    for way, own in enumerate((one_ref, two_ref)):
        right, left = came[2 * way : 2 * way + 2]
        far_a, far_b, ahead_ref, behind_ref = outs[4 * way : 4 * way + 4]
        for hop, ahead_by in enumerate((2, 1, 3, 0)):
            at = (misc_ref[1 - way] + ahead_by) % 4
            total = [
                own[at, pl.ds(half * HALF, HALF)] + unpack(right.at[half, at]) + unpack(left.at[half, at])
                for half in range(2)
            ]
            for half in range(2):
                if hop == 0:
                    pack((far_a, far_b)[half].at[0], total[half])
                elif hop < 3:
                    pack((ahead_ref, behind_ref)[hop - 1].at[half], total[half])
                else:
                    own_ref[pl.ds(half * HALF, HALF), pl.ds(way * 128, 128)] = total[half]


def last_kernel(own_ref, *refs):
    came, out_ref = refs[:4], refs[4]
    for way in range(2):
        right, left = came[2 * way : 2 * way + 2]
        columns = pl.ds(way * 128, 128)
        for half in range(2):
            rows = pl.ds(half * HALF, HALF)
            total = own_ref[rows, columns] + unpack(right.at[half]) + unpack(left.at[half])
            out_ref[columns, rows] = total.T


def shards(amplitudes, t2_mask, eri_tiles, eri_slot):
    y, core, x, z = (lax.axis_index(name) for name in ("y", "core", "x", "z"))
    group = x * 4 + z
    myself = (y * 2 + core) * COLS + group
    rows_dev, depth_dev = amplitudes.shape
    slots_dev = eri_tiles.shape[0]

    send_index = pl.pallas_call(
        lambda *refs: route_kernel(slots_dev, *refs),
        out_shape=jax.ShapeDtypeStruct((COLS, 128), jnp.int32),
        in_specs=[
            pl.BlockSpec(memory_space=pltpu.SMEM),
            pl.BlockSpec(memory_space=pltpu.VMEM),
        ],
        out_specs=pl.BlockSpec(memory_space=pltpu.VMEM),
        compiler_params=pltpu.CompilerParams(vmem_limit_bytes=VMEM_GRANT),
        name="route",
    )(myself.reshape(1).astype(jnp.int32), eri_slot.reshape(-1, 128))
    vmem = pl.BlockSpec(memory_space=pltpu.VMEM)
    batch = jax.ShapeDtypeStruct((COLS * BATCH, SUB, 128), jnp.bfloat16)
    outgoing = pl.pallas_call(
        fill_kernel,
        grid_spec=pltpu.PrefetchScalarGridSpec(
            num_scalar_prefetch=1,
            grid=(),
            in_specs=[vmem],
            out_specs=[pl.BlockSpec(memory_space=pl.ANY)] * 2,
            scratch_shapes=[
                pltpu.VMEM((2, COLS * BATCH, SUB, 128), jnp.bfloat16),
                pltpu.SemaphoreType.DMA((2,)),
            ],
        ),
        out_shape=[batch] * 2,
        compiler_params=pltpu.CompilerParams(vmem_limit_bytes=VMEM_GRANT),
        name="fill",
    )(send_index, eri_tiles.reshape(slots_dev, SUB, 128))

    def send(part):
        part = part.reshape(COLS, BATCH, SUB, 128)
        part = lax.all_to_all(part, ("x", "z"), split_axis=0, concat_axis=0, tiled=True)
        return part.reshape(COLS * BATCH, SUB, 128)

    first = send(outgoing[0])
    first, second, eri_slot = lax.optimization_barrier((first, outgoing[1], eri_slot))
    up, down = reach(first)
    second = send(second)
    devices = jnp.arange(DEVS, dtype=jnp.int32)
    owner_all = jnp.where(eri_slot >= 0, eri_slot // slots_dev, -1).reshape(COLS, 1, GROUP)
    held = jnp.sum((owner_all == devices[None, :, None]).astype(jnp.int32), axis=2)
    tail = jnp.maximum(held - BATCH, 0).reshape(COLS, ROWS, COLS)
    spill = jnp.any(jnp.sum(tail, axis=2) > EXTRA)
    tail = lax.dynamic_index_in_dim(tail, group, 0, keepdims=False)
    upto = jnp.sum(jnp.where(jnp.arange(COLS)[:, None] >= jnp.arange(COLS)[None, :], tail[:, None, :], 0), axis=2)
    start = upto - tail
    mine_upto = lax.dynamic_index_in_dim(upto, y * 2 + core, 0, keepdims=False)
    mine_start = lax.dynamic_index_in_dim(start, y * 2 + core, 0, keepdims=False)
    spot = jnp.arange(COLS * BATCH, dtype=jnp.int32)
    inside = jnp.logical_and(spot[:, None] >= mine_start[None, :], spot[:, None] < mine_upto[None, :])
    source = jnp.arange(COLS, dtype=jnp.int32)[None, :] * BATCH + spot[:, None] - mine_start[None, :]
    source = jnp.sum(jnp.where(inside, source, 0), axis=1).astype(jnp.int32)
    second, up, down, source, spill = lax.optimization_barrier((second, up, down, source, spill))
    half = COLS * BATCH // 2
    mixed = jax.ShapeDtypeStruct((half + EXTRA, SUB, 128), jnp.bfloat16)
    from_up, from_down, some, rest = pl.pallas_call(
        mix_kernel,
        grid_spec=pltpu.PrefetchScalarGridSpec(
            num_scalar_prefetch=1,
            grid=(),
            in_specs=[vmem] * 3,
            out_specs=[vmem] * 4,
            scratch_shapes=[pltpu.SemaphoreType.DMA((4,))],
        ),
        out_shape=[mixed] * 2
        + [
            jax.ShapeDtypeStruct((EXTRA, SUB, 128), jnp.bfloat16),
            jax.ShapeDtypeStruct((COLS * BATCH - EXTRA, SUB, 128), jnp.bfloat16),
        ],
        compiler_params=pltpu.CompilerParams(vmem_limit_bytes=VMEM_GRANT),
        name="mix",
    )(source, second, up, down)
    from_up, from_down = ahead("y", from_up), behind("y", from_down)
    wanted = lax.dynamic_slice_in_dim(eri_slot, group * GROUP, GROUP)
    some, up, down, amplitudes, wanted = lax.optimization_barrier((some, up, down, amplitudes, wanted))
    swapped = swap([first, up, down])

    parted = jax.ShapeDtypeStruct((rows_dev, depth_dev // 2), jnp.bfloat16)
    even, odd = pl.pallas_call(
        prep_kernel,
        grid=(depth_dev // 256,),
        out_shape=[parted] * 2,
        in_specs=[
            pl.BlockSpec(t2_mask.shape, lambda i: (0, 0)),
            pl.BlockSpec((rows_dev, 256), lambda i: (0, i)),
        ],
        out_specs=[pl.BlockSpec((rows_dev, 128), lambda i: (0, i))] * 2,
        compiler_params=pltpu.CompilerParams(vmem_limit_bytes=VMEM_GRANT),
        name="prep",
    )(t2_mask, amplitudes)

    owner = jnp.where(wanted >= 0, wanted // slots_dev, -1)
    mine = owner[:, None] == devices[None, :]
    spot = jnp.arange(GROUP, dtype=jnp.int32)
    before = (spot[:, None] > spot[None, :]).astype(jnp.bfloat16)
    counts = jnp.dot(before, mine.astype(jnp.bfloat16), preferred_element_type=jnp.float32)
    rank = jnp.sum(jnp.where(mine, counts, 0.0), axis=1).astype(jnp.int32)
    begin = jnp.sum(jnp.where(mine, start.reshape(1, DEVS), 0), axis=1)
    behind_first = begin + rank - BATCH
    owner_row = owner // COLS
    turn = (owner_row // 2 - y) % 4
    turn = jnp.where(turn == 1, 2, jnp.where(turn == 2, 3, jnp.where(turn == 3, 1, 0)))
    size = COLS * BATCH
    slot = owner % COLS * BATCH + rank
    early = turn * size + slot + jnp.where(jnp.logical_and(turn == 3, slot >= half), EXTRA, 0)
    begins = (4 * size + 2 * EXTRA, 3 * size + half, 4 * size + EXTRA, 4 * size + 3 * EXTRA)
    late = behind_first + sum(jnp.where(turn == k, begin_late, 0) for k, begin_late in enumerate(begins))
    tile_index = jnp.where(rank < BATCH, early, late) + CORE * (owner_row % 2 != core)
    spilled = 2 * CORE + owner_row * (size - EXTRA) + behind_first - EXTRA
    tile_index = jnp.where(jnp.logical_or(rank < BATCH, behind_first < EXTRA), tile_index, spilled)
    tile_index = jnp.where(wanted < 0, POOL, tile_index)
    misc = jnp.stack([x, z, spill.astype(jnp.int32)]).astype(jnp.int32)
    third = lax.cond(
        misc[2] > 0,
        lambda value: lax.all_gather(value, ("y", "core"), axis=0, tiled=True),
        lambda value: jnp.zeros((THIRD, SUB, 128), jnp.bfloat16),
        rest,
    )
    from_up, from_down, even, odd, tile_index, misc, third = lax.optimization_barrier(
        (from_up, from_down, even, odd, tile_index, misc, third)
    )
    tail = jnp.concatenate(
        [
            some,
            ahead("y", from_up[half : half + EXTRA // 2]),
            behind("y", from_down[half + EXTRA // 2 :]),
        ]
    )
    late_parts = [from_up, from_down, tail]
    tiles = collect_call(misc, [first, up, down, *late_parts, *swapped, *swap(late_parts)], third)

    scalars = (tile_index, misc)
    far, arrays = product_call("far", (2,), scalars, (even, odd, tiles))
    axes = ("x", "z")
    near, arrays = product_call("near", (1, 3), scalars, arrays)
    inputs = []
    for way, axis in enumerate(axes):
        inputs += [*near[2 * way : 2 * way + 2], ahead(axis, far[2 * way]), behind(axis, far[2 * way + 1])]
    packed = jax.ShapeDtypeStruct((2, 4, PACKED, 128), jnp.int16)
    added = whole_call(add_first_kernel, "add_first", [packed] * 4, *inputs)
    came = []
    for way, axis in enumerate(axes):
        came += [ahead(axis, added[2 * way]), behind(axis, added[2 * way + 1])]
    (one, two), _ = product_call("own", (0,), scalars, arrays)
    single = jax.ShapeDtypeStruct((1, PACKED, 128), jnp.int16)
    double = jax.ShapeDtypeStruct((2, PACKED, 128), jnp.int16)
    *outs, own = whole_call(
        middle_kernel,
        "middle",
        [single, single, double, double] * 2 + [jax.ShapeDtypeStruct((rows_dev, 256), jnp.float32)],
        one,
        two,
        *came,
        scalars=(misc,),
    )
    axes = ("z", "x")
    inputs = []
    for way, axis in enumerate(axes):
        far_a, far_b, next_ab, prev_ab = outs[4 * way : 4 * way + 4]
        inputs += [next_ab, prev_ab, ahead(axis, far_a), behind(axis, far_b)]
    added = whole_call(add_second_kernel, "add_second", [double] * 4, *inputs)
    came = []
    for way, axis in enumerate(axes):
        came += [ahead(axis, added[2 * way]), behind(axis, added[2 * way + 1])]
    return whole_call(
        last_kernel, "last", [jax.ShapeDtypeStruct((256, rows_dev), jnp.float32)], own, *came
    )[0]


def solution(mesh):
    axes = ("y", "core", "x", "z")
    fine = Mesh(mesh.devices.reshape(4, 2, 4, 4), axes)
    row, col = ("y", "core"), ("x", "z")
    in_specs = (P(row, col), P(row, col), P(axes, None), P())
    out_specs = P(col, row)
    return jax.shard_map(shards, mesh=fine, in_specs=in_specs, out_specs=out_specs, check_vma=False)
```

```python
import functools

import jax
import jax.numpy as jnp
from jax import lax
from jax.experimental import pallas as pl
from jax.experimental.pallas import tpu as pltpu
from jax.sharding import Mesh
from jax.sharding import PartitionSpec as P

TILE = 64
VTILES = 32
KOCC = 16
JOCC = 2
CAP = 20
COLS = 16
ROWS = 8
DEVS = 128
GROUP = VTILES * KOCC * VTILES * JOCC // COLS
KB = GROUP // (VTILES * JOCC)
NB = VTILES * JOCC
SUB = TILE * TILE // 128
BATCH = 8
FIRST = COLS * BATCH
SECOND = COLS * (CAP - BATCH)
EXTRA = 80
CORE = 4 * FIRST + 4 * EXTRA
THIRD = ROWS * (SECOND - EXTRA)
POOL = 2 * CORE + THIRD
PARTS = 12
HALF = 512
PACKED = HALF + HALF // 16
VMEM_GRANT = 10 * 1024 * 1024


def route_kernel(slots_dev, me_ref, slot_ref, out_ref):
    base = me_ref[0] * slots_dev
    slot = slot_ref[...]
    rows = slot.shape[0]
    per = rows // COLS
    local = slot - base
    mine = jnp.logical_and(local >= 0, local < slots_dev)
    ones = jnp.where(mine, 1.0, 0.0).astype(jnp.bfloat16)
    r = lax.broadcasted_iota(jnp.int32, (128, 128), 0)
    c = lax.broadcasted_iota(jnp.int32, (128, 128), 1)
    before = jnp.where(r < c, 1.0, 0.0).astype(jnp.bfloat16)
    within = jnp.dot(ones, before, preferred_element_type=jnp.float32)
    r = lax.broadcasted_iota(jnp.int32, (rows, rows), 0)
    c = lax.broadcasted_iota(jnp.int32, (rows, rows), 1)
    above = jnp.where(jnp.logical_and(r // per == c // per, c < r), 1.0, 0.0).astype(jnp.bfloat16)
    upto = jnp.dot(above, ones, preferred_element_type=jnp.float32)
    rank = within + jnp.sum(upto, axis=1, keepdims=True)
    rank = jnp.where(mine, rank, -1.0).reshape(COLS, per, 128)
    parity = lax.broadcasted_iota(jnp.int32, (rows, 128), 1) % 2
    local = jnp.where(mine, 2 * local + parity, 0).astype(jnp.float32).reshape(COLS, per, 128)
    lane = lax.broadcasted_iota(jnp.int32, (COLS, 128), 1)
    out = jnp.zeros((COLS, 128), jnp.float32)
    for j in range(CAP):
        picked = jnp.sum(jnp.where(rank == float(j), local, 0.0), axis=1)
        out = jnp.where(lane == j, jnp.sum(picked, axis=1, keepdims=True), out)
    out_ref[...] = out.astype(jnp.int32)


def fill_kernel(index_ref, tiles_ref, first_ref, second_ref, first_filled, second_filled, sems):
    copies = []
    for k, (filled, out_ref, base) in enumerate(((first_filled, first_ref, 0), (second_filled, second_ref, BATCH))):
        size = filled.shape[0] // COLS

        def group(g, carry, filled=filled, size=size, base=base):
            codes = [index_ref[g, base + j] for j in range(size)]
            tiles = [tiles_ref[code // 2] for code in codes]
            for j in range(size):
                turned = jnp.concatenate([tiles[j][:, TILE:], tiles[j][:, :TILE]], axis=1)
                filled[g * size + j] = jnp.where(codes[j] % 2 == 1, turned, tiles[j])
            return carry

        lax.fori_loop(0, COLS, group, 0)
        copies.append(pltpu.make_async_copy(filled, out_ref, sems.at[k]))
        copies[k].start()
    for copy in copies:
        copy.wait()


def compact_kernel(index_ref, spill_ref, second_ref, some_ref, rest_ref):
    def move(out_ref, base):
        def body(i, carry):
            tiles = [second_ref[index_ref[base + i * 16 + k]] for k in range(16)]
            for k in range(16):
                out_ref[i * 16 + k] = tiles[k]
            return carry

        lax.fori_loop(0, out_ref.shape[0] // 16, body, 0)

    move(some_ref, 0)

    @pl.when(spill_ref[0] > 0)
    def _():
        move(rest_ref, EXTRA)


def join_kernel(up_ref, down_ref, some_ref, up_out, down_out, sems):
    half = FIRST // 2
    copies = [
        pltpu.make_async_copy(up_ref.at[pl.ds(0, half)], up_out.at[pl.ds(0, half)], sems.at[0]),
        pltpu.make_async_copy(down_ref.at[pl.ds(half, half)], down_out.at[pl.ds(0, half)], sems.at[1]),
        pltpu.make_async_copy(some_ref, up_out.at[pl.ds(half, EXTRA)], sems.at[2]),
        pltpu.make_async_copy(some_ref, down_out.at[pl.ds(half, EXTRA)], sems.at[3]),
    ]
    for copy in copies:
        copy.start()
    for copy in copies:
        copy.wait()


def no_spill_kernel(tiles_ref, out_ref, sem):
    copy = pltpu.make_async_copy(tiles_ref.at[pl.ds(0, 1)], out_ref.at[pl.ds(0, 1)], sem)
    copy.start()
    copy.wait()


def no_spill_call(tiles):
    return pl.pallas_call(
        no_spill_kernel,
        in_specs=[pl.BlockSpec(memory_space=pl.ANY)],
        out_specs=pl.BlockSpec(memory_space=pl.ANY),
        out_shape=jax.ShapeDtypeStruct((THIRD, SUB, 128), jnp.bfloat16),
        scratch_shapes=[pltpu.SemaphoreType.DMA],
        compiler_params=pltpu.CompilerParams(vmem_limit_bytes=VMEM_GRANT),
        name="no_spill",
    )(tiles)


def prep_kernel(mask_ref, amp_ref, even_ref, odd_ref):
    blk = pl.program_id(0)
    rows = amp_ref.shape[0]
    r = lax.broadcasted_iota(jnp.int32, (256, 256), 0)
    c = lax.broadcasted_iota(jnp.int32, (256, 256), 1)
    source = (c % 128 // SUB) * TILE + 2 * (c % SUB) + c // 128
    shuffle = jnp.where(r == source, 1.0, 0.0).astype(jnp.bfloat16)
    moved = jnp.dot(amp_ref[...], shuffle, preferred_element_type=jnp.float32)
    mask = mask_ref[...].astype(jnp.bfloat16)
    r = lax.broadcasted_iota(jnp.int32, (mask.shape[1], 128), 0)
    c = lax.broadcasted_iota(jnp.int32, (mask.shape[1], 128), 1)
    spread = jnp.where(r == 4 * blk + c // SUB, 1.0, 0.0).astype(jnp.bfloat16)
    wide = jnp.dot(mask, spread, preferred_element_type=jnp.float32).astype(jnp.bfloat16)
    r = lax.broadcasted_iota(jnp.int32, (rows, mask.shape[0]), 0)
    c = lax.broadcasted_iota(jnp.int32, (rows, mask.shape[0]), 1)
    tall = jnp.where(r // TILE == c, 1.0, 0.0).astype(jnp.bfloat16)
    full = jnp.dot(tall, wide, preferred_element_type=jnp.float32)
    even_ref[...] = (moved[:, :128] * full).astype(jnp.bfloat16)
    odd_ref[...] = (moved[:, 128:] * full).astype(jnp.bfloat16)


def pack(out_ref, value):
    value = value.reshape(HALF // 16, 16, 128)
    top = jnp.maximum(jnp.max(jnp.abs(value), axis=1), 1e-30)
    exponent = jnp.ceil(jnp.log2(top * 1.0001))
    scaled = jnp.round(value * jnp.exp2(15.0 - exponent)[:, None, :]).reshape(HALF, 128)
    out_ref[pl.ds(0, HALF)] = scaled.astype(jnp.int32).astype(jnp.int16)
    out_ref[pl.ds(HALF, HALF // 16)] = exponent.astype(jnp.int32).astype(jnp.int16)


def unpack(ref):
    mantissa = ref[pl.ds(0, HALF)].astype(jnp.int32).astype(jnp.float32)
    exponent = ref[pl.ds(HALF, HALF // 16)].astype(jnp.int32).astype(jnp.float32)
    value = mantissa.reshape(HALF // 16, 16, 128) * jnp.exp2(exponent - 15.0)[:, None, :]
    return value.reshape(HALF, 128)


def collect_kernel(misc_ref, *refs):
    parts, third_ref, tiles, sems = refs[:PARTS], refs[PARTS], refs[PARTS + 1], refs[PARTS + 2]
    copies, base = [], 0
    for k, part in enumerate(parts):
        size = part.shape[0]
        copies.append(pltpu.make_async_copy(part, tiles.at[pl.ds(base, size)], sems.at[k]))
        base += size
    for copy in copies:
        copy.start()
    tiles[pl.ds(POOL, 1)] = jnp.zeros((1, SUB, 128), jnp.bfloat16)

    @pl.when(misc_ref[2] > 0)
    def _():
        copy = pltpu.make_async_copy(third_ref, tiles.at[pl.ds(base, THIRD)], sems.at[PARTS])
        copy.start()
        copy.wait()

    for copy in copies:
        copy.wait()


def collect_call(misc, parts, third):
    return pl.pallas_call(
        collect_kernel,
        in_specs=[pl.BlockSpec(memory_space=pltpu.SMEM)] + [pl.BlockSpec(memory_space=pl.ANY)] * (PARTS + 1),
        out_specs=pl.BlockSpec(memory_space=pltpu.VMEM),
        out_shape=jax.ShapeDtypeStruct((POOL + 1, SUB, 128), jnp.bfloat16),
        scratch_shapes=[pltpu.SemaphoreType.DMA((PARTS + 1,))],
        compiler_params=pltpu.CompilerParams(vmem_limit_bytes=VMEM_GRANT),
        cost_estimate=pl.CostEstimate(flops=0, bytes_accessed=POOL * 8192, transcendentals=0),
        name="collect",
    )(misc, *parts, third)


def build(hop, unit, index_ref, misc_ref, tiles, weight):
    at = [((misc_ref[0] + hop) % 4 * 4 + unit) * 4, (unit * 4 + (misc_ref[1] + hop) % 4) * 4 + 2]
    left = lax.broadcasted_iota(jnp.int32, (SUB, 128), 1) < TILE
    for kb in range(KB):
        picked = [tiles[index_ref[kb * NB + at[pair] + k]] for pair in range(2) for k in range(2)]
        rows = slice(kb * SUB, (kb + 1) * SUB)
        for pair in range(2):
            one, two = picked[2 * pair : 2 * pair + 2]
            columns = slice(128 * pair, 128 * pair + 128)
            weight[0][rows, columns] = jnp.where(left, one, two)
            weight[1][rows, columns] = jnp.where(left, two, one)


def product_kernel(hops, index_ref, misc_ref, even_ref, odd_ref, tiles, *refs):
    outs, weights = refs[:-4], (refs[-4:-2], refs[-2:])
    build(hops[0], 0, index_ref, misc_ref, tiles, weights[0])

    def emit(at, unit, weight):
        straight = jnp.dot(even_ref[...], weight[0][...], preferred_element_type=jnp.float32)
        crossed = jnp.dot(odd_ref[...], weight[1][...], preferred_element_type=jnp.float32)
        for way in range(2):
            columns = slice(way * 128, way * 128 + 128)
            value = straight[:, columns] + pltpu.roll(crossed[:, columns], TILE, 1)
            if hops == (0,):
                outs[way][unit] = value
                continue
            for half in range(2):
                out_ref = outs[2 * way + half] if len(hops) == 1 else outs[2 * way + at].at[half]
                pack(out_ref.at[unit], value[half * HALF : (half + 1) * HALF])

    for at, hop in enumerate(hops):
        after = hops[min(at + 1, len(hops) - 1)]

        def two_units(i, carry, at=at, hop=hop, after=after):
            build(hop, 2 * i + 1, index_ref, misc_ref, tiles, weights[1])
            emit(at, 2 * i, weights[0])
            build(jnp.where(i == 0, hop, after), 2 - 2 * i, index_ref, misc_ref, tiles, weights[0])
            emit(at, 2 * i + 1, weights[1])
            return carry

        lax.fori_loop(0, 2, two_units, 0)


def product_call(name, hops, scalars, arrays):
    rows_dev, depth_half = arrays[0].shape
    vmem = pl.BlockSpec(memory_space=pltpu.VMEM)
    if hops == (0,):
        outs = [jax.ShapeDtypeStruct((4, rows_dev, 128), jnp.float32)] * 2
    elif len(hops) == 1:
        outs = [jax.ShapeDtypeStruct((4, PACKED, 128), jnp.int16)] * 4
    else:
        outs = [jax.ShapeDtypeStruct((2, 4, PACKED, 128), jnp.int16)] * 4
    handed = [] if hops == (0,) else [jax.ShapeDtypeStruct(a.shape, a.dtype) for a in arrays]
    result = pl.pallas_call(
        functools.partial(product_kernel, hops),
        grid_spec=pltpu.PrefetchScalarGridSpec(
            num_scalar_prefetch=2,
            grid=(),
            in_specs=[vmem] * 3,
            out_specs=[vmem] * (len(outs) + len(handed)),
            scratch_shapes=[pltpu.VMEM((depth_half, 256), jnp.bfloat16)] * 4,
        ),
        out_shape=outs + handed,
        input_output_aliases={2 + k: len(outs) + k for k in range(len(handed))},
        compiler_params=pltpu.CompilerParams(vmem_limit_bytes=VMEM_GRANT),
        cost_estimate=pl.CostEstimate(
            flops=8 * len(hops) * rows_dev * depth_half * 512, bytes_accessed=POOL * 8192, transcendentals=0
        ),
        name=name,
    )(*scalars, *arrays)
    return result[: len(outs)], result[len(outs) :]


def ahead(axis, value):
    return lax.ppermute(value, axis, [(i, (i + 1) % 4) for i in range(4)])


def behind(axis, value):
    return lax.ppermute(value, axis, [(i, (i + 3) % 4) for i in range(4)])


def reach(tiles):
    return ahead("y", tiles), behind("y", tiles)


def swap(parts):
    return [lax.ppermute(part, "core", [(0, 1), (1, 0)]) for part in parts]


def add_first_kernel(*refs):
    def body(i, carry):
        for way in range(2):
            ahead_in, behind_in, came_a, came_b = refs[4 * way : 4 * way + 4]
            ahead_out, behind_out = refs[8 + 2 * way : 10 + 2 * way]
            pack(ahead_out.at[0, i], unpack(ahead_in.at[0, i]) + unpack(came_a.at[i]))
            ahead_out[1, i] = ahead_in[1, i]
            behind_out[0, i] = behind_in[0, i]
            pack(behind_out.at[1, i], unpack(behind_in.at[1, i]) + unpack(came_b.at[i]))
        return carry

    lax.fori_loop(0, 4, body, 0)


def add_second_kernel(*refs):
    for way in range(2):
        ahead_in, behind_in, came_a, came_b = refs[4 * way : 4 * way + 4]
        ahead_out, behind_out = refs[8 + 2 * way : 10 + 2 * way]
        pack(ahead_out.at[0], unpack(ahead_in.at[0]) + unpack(came_a.at[0]))
        ahead_out[1] = ahead_in[1]
        behind_out[0] = behind_in[0]
        pack(behind_out.at[1], unpack(behind_in.at[1]) + unpack(came_b.at[0]))


def whole_call(body, name, outs, *arrays, scalars=()):
    vmem = pl.BlockSpec(memory_space=pltpu.VMEM)
    size = sum(a.size * a.dtype.itemsize for a in [*arrays, *outs])
    return pl.pallas_call(
        body,
        in_specs=[pl.BlockSpec(memory_space=pltpu.SMEM)] * len(scalars) + [vmem] * len(arrays),
        out_specs=[vmem] * len(outs),
        out_shape=outs,
        compiler_params=pltpu.CompilerParams(vmem_limit_bytes=VMEM_GRANT),
        cost_estimate=pl.CostEstimate(flops=10 * size, bytes_accessed=size, transcendentals=0),
        name=name,
    )(*scalars, *arrays)


def middle_kernel(misc_ref, one_ref, two_ref, *refs):
    came, outs, own_ref = refs[:4], refs[4:12], refs[12]
    for way, own in enumerate((one_ref, two_ref)):
        right, left = came[2 * way : 2 * way + 2]
        far_a, far_b, ahead_ref, behind_ref = outs[4 * way : 4 * way + 4]
        for hop, ahead_by in enumerate((2, 1, 3, 0)):
            at = (misc_ref[1 - way] + ahead_by) % 4
            total = [
                own[at, pl.ds(half * HALF, HALF)] + unpack(right.at[half, at]) + unpack(left.at[half, at])
                for half in range(2)
            ]
            for half in range(2):
                if hop == 0:
                    pack((far_a, far_b)[half].at[0], total[half])
                elif hop < 3:
                    pack((ahead_ref, behind_ref)[hop - 1].at[half], total[half])
                else:
                    own_ref[pl.ds(half * HALF, HALF), pl.ds(way * 128, 128)] = total[half]


def last_kernel(own_ref, *refs):
    came, out_ref = refs[:4], refs[4]
    for way in range(2):
        right, left = came[2 * way : 2 * way + 2]
        columns = pl.ds(way * 128, 128)
        for half in range(2):
            rows = pl.ds(half * HALF, HALF)
            total = own_ref[rows, columns] + unpack(right.at[half]) + unpack(left.at[half])
            out_ref[columns, rows] = total.T


def shards(amplitudes, t2_mask, eri_tiles, eri_slot):
    y, core, x, z = (lax.axis_index(name) for name in ("y", "core", "x", "z"))
    group = x * 4 + z
    myself = (y * 2 + core) * COLS + group
    rows_dev, depth_dev = amplitudes.shape
    slots_dev = eri_tiles.shape[0]

    send_index = pl.pallas_call(
        lambda *refs: route_kernel(slots_dev, *refs),
        out_shape=jax.ShapeDtypeStruct((COLS, 128), jnp.int32),
        in_specs=[
            pl.BlockSpec(memory_space=pltpu.SMEM),
            pl.BlockSpec(memory_space=pltpu.VMEM),
        ],
        out_specs=pl.BlockSpec(memory_space=pltpu.VMEM),
        compiler_params=pltpu.CompilerParams(vmem_limit_bytes=VMEM_GRANT),
        name="route",
    )(myself.reshape(1).astype(jnp.int32), eri_slot.reshape(-1, 128))
    vmem = pl.BlockSpec(memory_space=pltpu.VMEM)
    outgoing = pl.pallas_call(
        fill_kernel,
        grid_spec=pltpu.PrefetchScalarGridSpec(
            num_scalar_prefetch=1,
            grid=(),
            in_specs=[vmem],
            out_specs=[pl.BlockSpec(memory_space=pltpu.HBM)] * 2,
            scratch_shapes=[
                pltpu.VMEM((FIRST, SUB, 128), jnp.bfloat16),
                pltpu.VMEM((SECOND, SUB, 128), jnp.bfloat16),
                pltpu.SemaphoreType.DMA((2,)),
            ],
        ),
        out_shape=[jax.ShapeDtypeStruct((size, SUB, 128), jnp.bfloat16) for size in (FIRST, SECOND)],
        compiler_params=pltpu.CompilerParams(vmem_limit_bytes=VMEM_GRANT),
        name="fill",
    )(send_index, eri_tiles.reshape(slots_dev, SUB, 128))

    def send(part):
        part = part.reshape(COLS, -1, SUB, 128)
        part = lax.all_to_all(part, ("x", "z"), split_axis=0, concat_axis=0, tiled=True)
        return part.reshape(-1, SUB, 128)

    first = send(outgoing[0])
    first, second, eri_slot = lax.optimization_barrier((first, outgoing[1], eri_slot))
    up, down = reach(first)
    second = send(second)
    devices = jnp.arange(DEVS, dtype=jnp.int32)
    owner_all = jnp.where(eri_slot >= 0, eri_slot // slots_dev, -1).reshape(COLS, 1, GROUP)
    held = jnp.sum((owner_all == devices[None, :, None]).astype(jnp.int32), axis=2)
    tail = jnp.maximum(held - BATCH, 0).reshape(COLS, ROWS, COLS)
    spill = jnp.any(jnp.sum(tail, axis=2) > EXTRA)
    tail = lax.dynamic_index_in_dim(tail, group, 0, keepdims=False)
    upto = jnp.sum(jnp.where(jnp.arange(COLS)[:, None] >= jnp.arange(COLS)[None, :], tail[:, None, :], 0), axis=2)
    start = upto - tail
    mine_upto = lax.dynamic_index_in_dim(upto, y * 2 + core, 0, keepdims=False)
    mine_start = lax.dynamic_index_in_dim(start, y * 2 + core, 0, keepdims=False)
    spot = jnp.arange(SECOND, dtype=jnp.int32)
    inside = jnp.logical_and(spot[:, None] >= mine_start[None, :], spot[:, None] < mine_upto[None, :])
    source = jnp.arange(COLS, dtype=jnp.int32)[None, :] * (CAP - BATCH) + spot[:, None] - mine_start[None, :]
    source = jnp.sum(jnp.where(inside, source, 0), axis=1).astype(jnp.int32)
    spill = spill.astype(jnp.int32).reshape(1)
    second, source, spill = lax.optimization_barrier((second, source, spill))
    half = FIRST // 2
    some, rest = pl.pallas_call(
        compact_kernel,
        grid_spec=pltpu.PrefetchScalarGridSpec(
            num_scalar_prefetch=2, grid=(), in_specs=[vmem], out_specs=[vmem] * 2
        ),
        out_shape=[jax.ShapeDtypeStruct((size, SUB, 128), jnp.bfloat16) for size in (EXTRA, SECOND - EXTRA)],
        compiler_params=pltpu.CompilerParams(vmem_limit_bytes=VMEM_GRANT),
        name="compact",
    )(source, spill, second)
    some, up, down = lax.optimization_barrier((some, up, down))
    from_up, from_down = pl.pallas_call(
        join_kernel,
        in_specs=[vmem] * 3,
        out_specs=[vmem] * 2,
        out_shape=[jax.ShapeDtypeStruct((half + EXTRA, SUB, 128), jnp.bfloat16)] * 2,
        scratch_shapes=[pltpu.SemaphoreType.DMA((4,))],
        compiler_params=pltpu.CompilerParams(vmem_limit_bytes=VMEM_GRANT),
        name="join",
    )(up, down, some)
    wanted = lax.dynamic_slice_in_dim(eri_slot, group * GROUP, GROUP)
    from_up, up, down, amplitudes, wanted = lax.optimization_barrier((from_up, up, down, amplitudes, wanted))
    from_up, from_down = ahead("y", from_up), behind("y", from_down)
    swapped = swap([first, up, down])

    parted = jax.ShapeDtypeStruct((rows_dev, depth_dev // 2), jnp.bfloat16)
    even, odd = pl.pallas_call(
        prep_kernel,
        grid=(depth_dev // 256,),
        out_shape=[parted] * 2,
        in_specs=[
            pl.BlockSpec(t2_mask.shape, lambda i: (0, 0)),
            pl.BlockSpec((rows_dev, 256), lambda i: (0, i)),
        ],
        out_specs=[pl.BlockSpec((rows_dev, 128), lambda i: (0, i))] * 2,
        compiler_params=pltpu.CompilerParams(vmem_limit_bytes=VMEM_GRANT),
        name="prep",
    )(t2_mask, amplitudes)

    owner = jnp.where(wanted >= 0, wanted // slots_dev, -1)
    mine = owner[:, None] == devices[None, :]
    spot = jnp.arange(GROUP, dtype=jnp.int32)
    before = (spot[:, None] > spot[None, :]).astype(jnp.bfloat16)
    counts = jnp.dot(before, mine.astype(jnp.bfloat16), preferred_element_type=jnp.float32)
    rank = jnp.sum(jnp.where(mine, counts, 0.0), axis=1).astype(jnp.int32)
    begin = jnp.sum(jnp.where(mine, start.reshape(1, DEVS), 0), axis=1)
    behind_first = begin + rank - BATCH
    owner_row = owner // COLS
    turn = (owner_row // 2 - y) % 4
    turn = jnp.where(turn == 1, 2, jnp.where(turn == 2, 3, jnp.where(turn == 3, 1, 0)))
    size = FIRST
    slot = owner % COLS * BATCH + rank
    early = turn * size + slot + jnp.where(jnp.logical_and(turn == 3, slot >= half), EXTRA, 0)
    begins = (4 * size + 2 * EXTRA, 3 * size + half, 4 * size + EXTRA, 4 * size + 3 * EXTRA)
    late = behind_first + sum(jnp.where(turn == k, begin_late, 0) for k, begin_late in enumerate(begins))
    tile_index = jnp.where(rank < BATCH, early, late) + CORE * (owner_row % 2 != core)
    spilled = 2 * CORE + owner_row * (SECOND - EXTRA) + behind_first - EXTRA
    tile_index = jnp.where(jnp.logical_or(rank < BATCH, behind_first < EXTRA), tile_index, spilled)
    tile_index = jnp.where(wanted < 0, POOL, tile_index)
    misc = jnp.stack([x, z, spill[0]]).astype(jnp.int32)
    third = lax.cond(
        misc[2] > 0,
        lambda value: lax.all_gather(value, ("y", "core"), axis=0, tiled=True),
        no_spill_call,
        rest,
    )
    from_up, from_down, swapped, even, odd, tile_index, misc, third = lax.optimization_barrier(
        (from_up, from_down, swapped, even, odd, tile_index, misc, third)
    )
    tail_up = ahead("y", from_up[half : half + EXTRA // 2])
    tail_down = behind("y", from_down[half + EXTRA // 2 :])
    swapped_late = swap([from_up, from_down])
    tail_up, tail_down, swapped_late = lax.optimization_barrier((tail_up, tail_down, swapped_late))
    tail = jnp.concatenate([some, tail_up, tail_down])
    parts = [first, up, down, from_up, from_down, tail, *swapped, *swapped_late, *swap([tail])]
    tiles = collect_call(misc, parts, third)

    scalars = (tile_index, misc)
    far, arrays = product_call("far", (2,), scalars, (even, odd, tiles))
    axes = ("x", "z")
    near, arrays = product_call("near", (1, 3), scalars, arrays)
    inputs = []
    for way, axis in enumerate(axes):
        inputs += [*near[2 * way : 2 * way + 2], ahead(axis, far[2 * way]), behind(axis, far[2 * way + 1])]
    packed = jax.ShapeDtypeStruct((2, 4, PACKED, 128), jnp.int16)
    added = whole_call(add_first_kernel, "add_first", [packed] * 4, *inputs)
    came = []
    for way, axis in enumerate(axes):
        came += [ahead(axis, added[2 * way]), behind(axis, added[2 * way + 1])]
    (one, two), _ = product_call("own", (0,), scalars, arrays)
    single = jax.ShapeDtypeStruct((1, PACKED, 128), jnp.int16)
    double = jax.ShapeDtypeStruct((2, PACKED, 128), jnp.int16)
    *outs, own = whole_call(
        middle_kernel,
        "middle",
        [single, single, double, double] * 2 + [jax.ShapeDtypeStruct((rows_dev, 256), jnp.float32)],
        one,
        two,
        *came,
        scalars=(misc,),
    )
    axes = ("z", "x")
    inputs = []
    for way, axis in enumerate(axes):
        far_a, far_b, next_ab, prev_ab = outs[4 * way : 4 * way + 4]
        inputs += [next_ab, prev_ab, ahead(axis, far_a), behind(axis, far_b)]
    added = whole_call(add_second_kernel, "add_second", [double] * 4, *inputs)
    came = []
    for way, axis in enumerate(axes):
        came += [ahead(axis, added[2 * way]), behind(axis, added[2 * way + 1])]
    return whole_call(
        last_kernel, "last", [jax.ShapeDtypeStruct((256, rows_dev), jnp.float32)], own, *came
    )[0]


def solution(mesh):
    axes = ("y", "core", "x", "z")
    fine = Mesh(mesh.devices.reshape(4, 2, 4, 4), axes)
    row, col = ("y", "core"), ("x", "z")
    in_specs = (P(row, col), P(row, col), P(axes, None), P())
    out_specs = P(col, row)
    return jax.shard_map(shards, mesh=fine, in_specs=in_specs, out_specs=out_specs, check_vma=False)
```

```python
import functools

import jax
import jax.numpy as jnp
from jax import lax
from jax.experimental import pallas as pl
from jax.experimental.pallas import tpu as pltpu
from jax.sharding import Mesh
from jax.sharding import PartitionSpec as P

TILE = 64
VTILES = 32
KOCC = 16
JOCC = 2
CAP = 20
COLS = 16
ROWS = 8
DEVS = 128
GROUP = VTILES * KOCC * VTILES * JOCC // COLS
KB = GROUP // (VTILES * JOCC)
NB = VTILES * JOCC
SUB = TILE * TILE // 128
BATCH = 11
FIRST = COLS * BATCH
SECOND = COLS * (CAP - BATCH)
EXTRA = 32
CORE = 4 * FIRST + 4 * EXTRA
THIRD = ROWS * (SECOND - EXTRA)
POOL = 2 * CORE + THIRD
PARTS = 12
HALF = 512
PACKED = HALF + HALF // 16
VMEM_GRANT = 10 * 1024 * 1024


def route_kernel(slots_dev, me_ref, slot_ref, out_ref):
    base = me_ref[0] * slots_dev
    slot = slot_ref[...]
    rows = slot.shape[0]
    per = rows // COLS
    local = slot - base
    mine = jnp.logical_and(local >= 0, local < slots_dev)
    ones = jnp.where(mine, 1.0, 0.0).astype(jnp.bfloat16)
    r = lax.broadcasted_iota(jnp.int32, (128, 128), 0)
    c = lax.broadcasted_iota(jnp.int32, (128, 128), 1)
    before = jnp.where(r < c, 1.0, 0.0).astype(jnp.bfloat16)
    within = jnp.dot(ones, before, preferred_element_type=jnp.float32)
    r = lax.broadcasted_iota(jnp.int32, (rows, rows), 0)
    c = lax.broadcasted_iota(jnp.int32, (rows, rows), 1)
    above = jnp.where(jnp.logical_and(r // per == c // per, c < r), 1.0, 0.0).astype(jnp.bfloat16)
    upto = jnp.dot(above, ones, preferred_element_type=jnp.float32)
    rank = within + jnp.sum(upto, axis=1, keepdims=True)
    rank = jnp.where(mine, rank, -1.0).reshape(COLS, per, 128)
    parity = lax.broadcasted_iota(jnp.int32, (rows, 128), 1) % 2
    local = jnp.where(mine, 2 * local + parity, 0).astype(jnp.float32).reshape(COLS, per, 128)
    lane = lax.broadcasted_iota(jnp.int32, (COLS, 128), 1)
    out = jnp.zeros((COLS, 128), jnp.float32)
    for j in range(CAP):
        picked = jnp.sum(jnp.where(rank == float(j), local, 0.0), axis=1)
        out = jnp.where(lane == j, jnp.sum(picked, axis=1, keepdims=True), out)
    out_ref[...] = out.astype(jnp.int32)


def fill_kernel(index_ref, tiles_ref, first_ref, second_ref, first_filled, second_filled, sems):
    copies = []
    for k, (filled, out_ref, base) in enumerate(((first_filled, first_ref, 0), (second_filled, second_ref, BATCH))):
        size = filled.shape[0] // COLS

        def group(g, carry, filled=filled, size=size, base=base):
            codes = [index_ref[g, base + j] for j in range(size)]
            tiles = [tiles_ref[code // 2] for code in codes]
            for j in range(size):
                turned = jnp.concatenate([tiles[j][:, TILE:], tiles[j][:, :TILE]], axis=1)
                filled[g * size + j] = jnp.where(codes[j] % 2 == 1, turned, tiles[j])
            return carry

        lax.fori_loop(0, COLS, group, 0)
        copies.append(pltpu.make_async_copy(filled, out_ref, sems.at[k]))
        copies[k].start()
    for copy in copies:
        copy.wait()


def compact_kernel(index_ref, spill_ref, second_ref, some_ref, rest_ref):
    def move(out_ref, base):
        def body(i, carry):
            tiles = [second_ref[index_ref[base + i * 16 + k]] for k in range(16)]
            for k in range(16):
                out_ref[i * 16 + k] = tiles[k]
            return carry

        lax.fori_loop(0, out_ref.shape[0] // 16, body, 0)

    move(some_ref, 0)

    @pl.when(spill_ref[0] > 0)
    def _():
        move(rest_ref, EXTRA)


def no_spill_kernel(tiles_ref, out_ref, sem):
    copy = pltpu.make_async_copy(tiles_ref.at[pl.ds(0, 1)], out_ref.at[pl.ds(0, 1)], sem)
    copy.start()
    copy.wait()


def no_spill_call(tiles):
    return pl.pallas_call(
        no_spill_kernel,
        in_specs=[pl.BlockSpec(memory_space=pl.ANY)],
        out_specs=pl.BlockSpec(memory_space=pl.ANY),
        out_shape=jax.ShapeDtypeStruct((THIRD, SUB, 128), jnp.bfloat16),
        scratch_shapes=[pltpu.SemaphoreType.DMA],
        compiler_params=pltpu.CompilerParams(vmem_limit_bytes=VMEM_GRANT),
        name="no_spill",
    )(tiles)


def prep_kernel(mask_ref, amp_ref, even_ref, odd_ref):
    blk = pl.program_id(0)
    rows = amp_ref.shape[0]
    r = lax.broadcasted_iota(jnp.int32, (256, 256), 0)
    c = lax.broadcasted_iota(jnp.int32, (256, 256), 1)
    source = (c % 128 // SUB) * TILE + 2 * (c % SUB) + c // 128
    shuffle = jnp.where(r == source, 1.0, 0.0).astype(jnp.bfloat16)
    moved = jnp.dot(amp_ref[...], shuffle, preferred_element_type=jnp.float32)
    mask = mask_ref[...].astype(jnp.bfloat16)
    r = lax.broadcasted_iota(jnp.int32, (mask.shape[1], 128), 0)
    c = lax.broadcasted_iota(jnp.int32, (mask.shape[1], 128), 1)
    spread = jnp.where(r == 4 * blk + c // SUB, 1.0, 0.0).astype(jnp.bfloat16)
    wide = jnp.dot(mask, spread, preferred_element_type=jnp.float32).astype(jnp.bfloat16)
    r = lax.broadcasted_iota(jnp.int32, (rows, mask.shape[0]), 0)
    c = lax.broadcasted_iota(jnp.int32, (rows, mask.shape[0]), 1)
    tall = jnp.where(r // TILE == c, 1.0, 0.0).astype(jnp.bfloat16)
    full = jnp.dot(tall, wide, preferred_element_type=jnp.float32)
    even_ref[...] = (moved[:, :128] * full).astype(jnp.bfloat16)
    odd_ref[...] = (moved[:, 128:] * full).astype(jnp.bfloat16)


def pack(out_ref, value):
    value = value.reshape(HALF // 16, 16, 128)
    top = jnp.maximum(jnp.max(jnp.abs(value), axis=1), 1e-30)
    exponent = jnp.ceil(jnp.log2(top * 1.0001))
    scaled = jnp.round(value * jnp.exp2(15.0 - exponent)[:, None, :]).reshape(HALF, 128)
    out_ref[pl.ds(0, HALF)] = scaled.astype(jnp.int32).astype(jnp.int16)
    out_ref[pl.ds(HALF, HALF // 16)] = exponent.astype(jnp.int32).astype(jnp.int16)


def unpack(ref):
    mantissa = ref[pl.ds(0, HALF)].astype(jnp.int32).astype(jnp.float32)
    exponent = ref[pl.ds(HALF, HALF // 16)].astype(jnp.int32).astype(jnp.float32)
    value = mantissa.reshape(HALF // 16, 16, 128) * jnp.exp2(exponent - 15.0)[:, None, :]
    return value.reshape(HALF, 128)


def collect_kernel(misc_ref, *refs):
    parts, third_ref, tiles, sems = refs[:PARTS], refs[PARTS], refs[PARTS + 1], refs[PARTS + 2]
    copies, base = [], 0
    for k, part in enumerate(parts):
        size = part.shape[0]
        copies.append(pltpu.make_async_copy(part, tiles.at[pl.ds(base, size)], sems.at[k]))
        base += size
    for copy in copies:
        copy.start()
    tiles[pl.ds(POOL, 1)] = jnp.zeros((1, SUB, 128), jnp.bfloat16)

    @pl.when(misc_ref[2] > 0)
    def _():
        copy = pltpu.make_async_copy(third_ref, tiles.at[pl.ds(base, THIRD)], sems.at[PARTS])
        copy.start()
        copy.wait()

    for copy in copies:
        copy.wait()


def collect_call(misc, parts, third):
    return pl.pallas_call(
        collect_kernel,
        in_specs=[pl.BlockSpec(memory_space=pltpu.SMEM)] + [pl.BlockSpec(memory_space=pl.ANY)] * (PARTS + 1),
        out_specs=pl.BlockSpec(memory_space=pltpu.VMEM),
        out_shape=jax.ShapeDtypeStruct((POOL + 1, SUB, 128), jnp.bfloat16),
        scratch_shapes=[pltpu.SemaphoreType.DMA((PARTS + 1,))],
        compiler_params=pltpu.CompilerParams(vmem_limit_bytes=VMEM_GRANT),
        cost_estimate=pl.CostEstimate(flops=0, bytes_accessed=POOL * 8192, transcendentals=0),
        name="collect",
    )(misc, *parts, third)


def build(hop, unit, index_ref, misc_ref, tiles, weight):
    at = [((misc_ref[0] + hop) % 4 * 4 + unit) * 4, (unit * 4 + (misc_ref[1] + hop) % 4) * 4 + 2]
    left = lax.broadcasted_iota(jnp.int32, (SUB, 128), 1) < TILE
    for kb in range(KB):
        picked = [tiles[index_ref[kb * NB + at[pair] + k]] for pair in range(2) for k in range(2)]
        rows = slice(kb * SUB, (kb + 1) * SUB)
        for pair in range(2):
            one, two = picked[2 * pair : 2 * pair + 2]
            columns = slice(128 * pair, 128 * pair + 128)
            weight[0][rows, columns] = jnp.where(left, one, two)
            weight[1][rows, columns] = jnp.where(left, two, one)


def product_kernel(hops, index_ref, misc_ref, even_ref, odd_ref, tiles, *refs):
    outs, weights = refs[:-4], (refs[-4:-2], refs[-2:])
    build(hops[0], 0, index_ref, misc_ref, tiles, weights[0])

    def emit(at, unit, weight):
        straight = jnp.dot(even_ref[...], weight[0][...], preferred_element_type=jnp.float32)
        crossed = jnp.dot(odd_ref[...], weight[1][...], preferred_element_type=jnp.float32)
        for way in range(2):
            columns = slice(way * 128, way * 128 + 128)
            value = straight[:, columns] + pltpu.roll(crossed[:, columns], TILE, 1)
            if hops == (0,):
                outs[way][unit] = value
                continue
            for half in range(2):
                out_ref = outs[2 * way + half] if len(hops) == 1 else outs[2 * way + at].at[half]
                pack(out_ref.at[unit], value[half * HALF : (half + 1) * HALF])

    for at, hop in enumerate(hops):
        after = hops[min(at + 1, len(hops) - 1)]

        def two_units(i, carry, at=at, hop=hop, after=after):
            build(hop, 2 * i + 1, index_ref, misc_ref, tiles, weights[1])
            emit(at, 2 * i, weights[0])
            build(jnp.where(i == 0, hop, after), 2 - 2 * i, index_ref, misc_ref, tiles, weights[0])
            emit(at, 2 * i + 1, weights[1])
            return carry

        lax.fori_loop(0, 2, two_units, 0)


def product_call(name, hops, scalars, arrays):
    rows_dev, depth_half = arrays[0].shape
    vmem = pl.BlockSpec(memory_space=pltpu.VMEM)
    if hops == (0,):
        outs = [jax.ShapeDtypeStruct((4, rows_dev, 128), jnp.float32)] * 2
    elif len(hops) == 1:
        outs = [jax.ShapeDtypeStruct((4, PACKED, 128), jnp.int16)] * 4
    else:
        outs = [jax.ShapeDtypeStruct((2, 4, PACKED, 128), jnp.int16)] * 4
    handed = [] if hops == (0,) else [jax.ShapeDtypeStruct(a.shape, a.dtype) for a in arrays]
    result = pl.pallas_call(
        functools.partial(product_kernel, hops),
        grid_spec=pltpu.PrefetchScalarGridSpec(
            num_scalar_prefetch=2,
            grid=(),
            in_specs=[vmem] * 3,
            out_specs=[vmem] * (len(outs) + len(handed)),
            scratch_shapes=[pltpu.VMEM((depth_half, 256), jnp.bfloat16)] * 4,
        ),
        out_shape=outs + handed,
        input_output_aliases={2 + k: len(outs) + k for k in range(len(handed))},
        compiler_params=pltpu.CompilerParams(vmem_limit_bytes=VMEM_GRANT),
        cost_estimate=pl.CostEstimate(
            flops=8 * len(hops) * rows_dev * depth_half * 512, bytes_accessed=POOL * 8192, transcendentals=0
        ),
        name=name,
    )(*scalars, *arrays)
    return result[: len(outs)], result[len(outs) :]


def ahead(axis, value):
    return lax.ppermute(value, axis, [(i, (i + 1) % 4) for i in range(4)])


def behind(axis, value):
    return lax.ppermute(value, axis, [(i, (i + 3) % 4) for i in range(4)])


def reach(tiles):
    return ahead("y", tiles), behind("y", tiles)


def swap(parts):
    return [lax.ppermute(part, "core", [(0, 1), (1, 0)]) for part in parts]


def across(up, down):
    half = up.shape[0] // 2
    return [ahead("y", up[:half]), behind("y", down[half:])]


def add_first_kernel(*refs):
    def body(i, carry):
        for way in range(2):
            ahead_in, behind_in, came_a, came_b = refs[4 * way : 4 * way + 4]
            ahead_out, behind_out = refs[8 + 2 * way : 10 + 2 * way]
            pack(ahead_out.at[0, i], unpack(ahead_in.at[0, i]) + unpack(came_a.at[i]))
            ahead_out[1, i] = ahead_in[1, i]
            behind_out[0, i] = behind_in[0, i]
            pack(behind_out.at[1, i], unpack(behind_in.at[1, i]) + unpack(came_b.at[i]))
        return carry

    lax.fori_loop(0, 4, body, 0)


def add_second_kernel(*refs):
    for way in range(2):
        ahead_in, behind_in, came_a, came_b = refs[4 * way : 4 * way + 4]
        ahead_out, behind_out = refs[8 + 2 * way : 10 + 2 * way]
        pack(ahead_out.at[0], unpack(ahead_in.at[0]) + unpack(came_a.at[0]))
        ahead_out[1] = ahead_in[1]
        behind_out[0] = behind_in[0]
        pack(behind_out.at[1], unpack(behind_in.at[1]) + unpack(came_b.at[0]))


def whole_call(body, name, outs, *arrays, scalars=()):
    vmem = pl.BlockSpec(memory_space=pltpu.VMEM)
    size = sum(a.size * a.dtype.itemsize for a in [*arrays, *outs])
    return pl.pallas_call(
        body,
        in_specs=[pl.BlockSpec(memory_space=pltpu.SMEM)] * len(scalars) + [vmem] * len(arrays),
        out_specs=[vmem] * len(outs),
        out_shape=outs,
        compiler_params=pltpu.CompilerParams(vmem_limit_bytes=VMEM_GRANT),
        cost_estimate=pl.CostEstimate(flops=10 * size, bytes_accessed=size, transcendentals=0),
        name=name,
    )(*scalars, *arrays)


def middle_kernel(misc_ref, one_ref, two_ref, *refs):
    came, outs, own_ref = refs[:4], refs[4:12], refs[12]
    for way, own in enumerate((one_ref, two_ref)):
        right, left = came[2 * way : 2 * way + 2]
        far_a, far_b, ahead_ref, behind_ref = outs[4 * way : 4 * way + 4]
        for hop, ahead_by in enumerate((2, 1, 3, 0)):
            at = (misc_ref[1 - way] + ahead_by) % 4
            total = [
                own[at, pl.ds(half * HALF, HALF)] + unpack(right.at[half, at]) + unpack(left.at[half, at])
                for half in range(2)
            ]
            for half in range(2):
                if hop == 0:
                    pack((far_a, far_b)[half].at[0], total[half])
                elif hop < 3:
                    pack((ahead_ref, behind_ref)[hop - 1].at[half], total[half])
                else:
                    own_ref[pl.ds(half * HALF, HALF), pl.ds(way * 128, 128)] = total[half]


def last_kernel(own_ref, *refs):
    came, out_ref = refs[:4], refs[4]
    for way in range(2):
        right, left = came[2 * way : 2 * way + 2]
        columns = pl.ds(way * 128, 128)
        for half in range(2):
            rows = pl.ds(half * HALF, HALF)
            total = own_ref[rows, columns] + unpack(right.at[half]) + unpack(left.at[half])
            out_ref[columns, rows] = total.T


def shards(amplitudes, t2_mask, eri_tiles, eri_slot):
    y, core, x, z = (lax.axis_index(name) for name in ("y", "core", "x", "z"))
    group = x * 4 + z
    myself = (y * 2 + core) * COLS + group
    rows_dev, depth_dev = amplitudes.shape
    slots_dev = eri_tiles.shape[0]

    send_index = pl.pallas_call(
        lambda *refs: route_kernel(slots_dev, *refs),
        out_shape=jax.ShapeDtypeStruct((COLS, 128), jnp.int32),
        in_specs=[
            pl.BlockSpec(memory_space=pltpu.SMEM),
            pl.BlockSpec(memory_space=pltpu.VMEM),
        ],
        out_specs=pl.BlockSpec(memory_space=pltpu.VMEM),
        compiler_params=pltpu.CompilerParams(vmem_limit_bytes=VMEM_GRANT),
        name="route",
    )(myself.reshape(1).astype(jnp.int32), eri_slot.reshape(-1, 128))
    vmem = pl.BlockSpec(memory_space=pltpu.VMEM)
    outgoing = pl.pallas_call(
        fill_kernel,
        grid_spec=pltpu.PrefetchScalarGridSpec(
            num_scalar_prefetch=1,
            grid=(),
            in_specs=[vmem],
            out_specs=[pl.BlockSpec(memory_space=pltpu.HBM)] * 2,
            scratch_shapes=[
                pltpu.VMEM((FIRST, SUB, 128), jnp.bfloat16),
                pltpu.VMEM((SECOND, SUB, 128), jnp.bfloat16),
                pltpu.SemaphoreType.DMA((2,)),
            ],
        ),
        out_shape=[jax.ShapeDtypeStruct((size, SUB, 128), jnp.bfloat16) for size in (FIRST, SECOND)],
        compiler_params=pltpu.CompilerParams(vmem_limit_bytes=VMEM_GRANT),
        name="fill",
    )(send_index, eri_tiles.reshape(slots_dev, SUB, 128))

    def send(part):
        part = part.reshape(COLS, -1, SUB, 128)
        part = lax.all_to_all(part, ("x", "z"), split_axis=0, concat_axis=0, tiled=True)
        return part.reshape(-1, SUB, 128)

    first = send(outgoing[0])
    first, second, eri_slot = lax.optimization_barrier((first, outgoing[1], eri_slot))
    up, down = reach(first)
    second = send(second)
    devices = jnp.arange(DEVS, dtype=jnp.int32)
    owner_all = jnp.where(eri_slot >= 0, eri_slot // slots_dev, -1).reshape(COLS, 1, GROUP)
    held = jnp.sum((owner_all == devices[None, :, None]).astype(jnp.int32), axis=2)
    tail = jnp.maximum(held - BATCH, 0).reshape(COLS, ROWS, COLS)
    spill = jnp.any(jnp.sum(tail, axis=2) > EXTRA)
    tail = lax.dynamic_index_in_dim(tail, group, 0, keepdims=False)
    upto = jnp.sum(jnp.where(jnp.arange(COLS)[:, None] >= jnp.arange(COLS)[None, :], tail[:, None, :], 0), axis=2)
    start = upto - tail
    mine_upto = lax.dynamic_index_in_dim(upto, y * 2 + core, 0, keepdims=False)
    mine_start = lax.dynamic_index_in_dim(start, y * 2 + core, 0, keepdims=False)
    spot = jnp.arange(SECOND, dtype=jnp.int32)
    inside = jnp.logical_and(spot[:, None] >= mine_start[None, :], spot[:, None] < mine_upto[None, :])
    source = jnp.arange(COLS, dtype=jnp.int32)[None, :] * (CAP - BATCH) + spot[:, None] - mine_start[None, :]
    source = jnp.sum(jnp.where(inside, source, 0), axis=1).astype(jnp.int32)
    spill = spill.astype(jnp.int32).reshape(1)
    second, source, spill = lax.optimization_barrier((second, source, spill))
    some, rest = pl.pallas_call(
        compact_kernel,
        grid_spec=pltpu.PrefetchScalarGridSpec(
            num_scalar_prefetch=2, grid=(), in_specs=[vmem], out_specs=[vmem] * 2
        ),
        out_shape=[jax.ShapeDtypeStruct((size, SUB, 128), jnp.bfloat16) for size in (EXTRA, SECOND - EXTRA)],
        compiler_params=pltpu.CompilerParams(vmem_limit_bytes=VMEM_GRANT),
        name="compact",
    )(source, spill, second)
    some_up, some_down = reach(some)
    far_parts = across(up, down)
    some_far = across(some_up, some_down)
    wanted = lax.dynamic_slice_in_dim(eri_slot, group * GROUP, GROUP)
    some, amplitudes, wanted = lax.optimization_barrier((some, amplitudes, wanted))

    parted = jax.ShapeDtypeStruct((rows_dev, depth_dev // 2), jnp.bfloat16)
    even, odd = pl.pallas_call(
        prep_kernel,
        grid=(depth_dev // 256,),
        out_shape=[parted] * 2,
        in_specs=[
            pl.BlockSpec(t2_mask.shape, lambda i: (0, 0)),
            pl.BlockSpec((rows_dev, 256), lambda i: (0, i)),
        ],
        out_specs=[pl.BlockSpec((rows_dev, 128), lambda i: (0, i))] * 2,
        compiler_params=pltpu.CompilerParams(vmem_limit_bytes=VMEM_GRANT),
        name="prep",
    )(t2_mask, amplitudes)

    owner = jnp.where(wanted >= 0, wanted // slots_dev, -1)
    mine = owner[:, None] == devices[None, :]
    spot = jnp.arange(GROUP, dtype=jnp.int32)
    before = (spot[:, None] > spot[None, :]).astype(jnp.bfloat16)
    counts = jnp.dot(before, mine.astype(jnp.bfloat16), preferred_element_type=jnp.float32)
    rank = jnp.sum(jnp.where(mine, counts, 0.0), axis=1).astype(jnp.int32)
    begin = jnp.sum(jnp.where(mine, start.reshape(1, DEVS), 0), axis=1)
    behind_first = begin + rank - BATCH
    owner_row = owner // COLS
    turn = (owner_row // 2 - y) % 4
    turn = jnp.where(turn == 1, 2, jnp.where(turn == 2, 3, jnp.where(turn == 3, 1, 0)))
    early = (turn * COLS + owner % COLS) * BATCH + rank
    late = 4 * FIRST + turn * EXTRA + behind_first
    tile_index = jnp.where(rank < BATCH, early, late) + CORE * (owner_row % 2 != core)
    spilled = 2 * CORE + owner_row * (SECOND - EXTRA) + behind_first - EXTRA
    tile_index = jnp.where(jnp.logical_or(rank < BATCH, behind_first < EXTRA), tile_index, spilled)
    tile_index = jnp.where(wanted < 0, POOL, tile_index)
    misc = jnp.stack([x, z, spill[0]]).astype(jnp.int32)
    third = lax.cond(
        misc[2] > 0,
        lambda value: lax.all_gather(value, ("y", "core"), axis=0, tiled=True),
        no_spill_call,
        rest,
    )
    some = jnp.concatenate([some, some_up, some_down, *some_far])
    first, up, down, far_parts, some, even, odd, tile_index, misc, third = lax.optimization_barrier(
        (first, up, down, far_parts, some, even, odd, tile_index, misc, third)
    )
    parts = [first, up, down, *far_parts, some]
    tiles = collect_call(misc, parts + swap(parts), third)

    scalars = (tile_index, misc)
    far, arrays = product_call("far", (2,), scalars, (even, odd, tiles))
    axes = ("x", "z")
    near, arrays = product_call("near", (1, 3), scalars, arrays)
    inputs = []
    for way, axis in enumerate(axes):
        inputs += [*near[2 * way : 2 * way + 2], ahead(axis, far[2 * way]), behind(axis, far[2 * way + 1])]
    packed = jax.ShapeDtypeStruct((2, 4, PACKED, 128), jnp.int16)
    added = whole_call(add_first_kernel, "add_first", [packed] * 4, *inputs)
    came = []
    for way, axis in enumerate(axes):
        came += [ahead(axis, added[2 * way]), behind(axis, added[2 * way + 1])]
    (one, two), _ = product_call("own", (0,), scalars, arrays)
    single = jax.ShapeDtypeStruct((1, PACKED, 128), jnp.int16)
    double = jax.ShapeDtypeStruct((2, PACKED, 128), jnp.int16)
    *outs, own = whole_call(
        middle_kernel,
        "middle",
        [single, single, double, double] * 2 + [jax.ShapeDtypeStruct((rows_dev, 256), jnp.float32)],
        one,
        two,
        *came,
        scalars=(misc,),
    )
    axes = ("z", "x")
    inputs = []
    for way, axis in enumerate(axes):
        far_a, far_b, next_ab, prev_ab = outs[4 * way : 4 * way + 4]
        inputs += [next_ab, prev_ab, ahead(axis, far_a), behind(axis, far_b)]
    added = whole_call(add_second_kernel, "add_second", [double] * 4, *inputs)
    came = []
    for way, axis in enumerate(axes):
        came += [ahead(axis, added[2 * way]), behind(axis, added[2 * way + 1])]
    return whole_call(
        last_kernel, "last", [jax.ShapeDtypeStruct((256, rows_dev), jnp.float32)], own, *came
    )[0]


def solution(mesh):
    axes = ("y", "core", "x", "z")
    fine = Mesh(mesh.devices.reshape(4, 2, 4, 4), axes)
    row, col = ("y", "core"), ("x", "z")
    in_specs = (P(row, col), P(row, col), P(axes, None), P())
    out_specs = P(col, row)
    return jax.shard_map(shards, mesh=fine, in_specs=in_specs, out_specs=out_specs, check_vma=False)
```

```python
import functools

import jax
import jax.numpy as jnp
from jax import lax
from jax.experimental import pallas as pl
from jax.experimental.pallas import tpu as pltpu
from jax.sharding import Mesh
from jax.sharding import PartitionSpec as P

TILE = 64
VTILES = 32
KOCC = 16
JOCC = 2
CAP = 20
COLS = 16
ROWS = 8
DEVS = 128
GROUP = VTILES * KOCC * VTILES * JOCC // COLS
KB = GROUP // (VTILES * JOCC)
NB = VTILES * JOCC
SUB = TILE * TILE // 128
BATCH = 8
FIRST = COLS * BATCH
SECOND = COLS * (CAP - BATCH)
EXTRA = 80
CORE = 4 * FIRST + 4 * EXTRA
THIRD = ROWS * (SECOND - EXTRA)
POOL = 2 * CORE + THIRD
PARTS = 14
HALF = 512
PACKED = HALF + HALF // 16
VMEM_GRANT = 10 * 1024 * 1024


def route_kernel(slots_dev, me_ref, slot_ref, out_ref):
    base = me_ref[0] * slots_dev
    slot = slot_ref[...]
    rows = slot.shape[0]
    per = rows // COLS
    local = slot - base
    mine = jnp.logical_and(local >= 0, local < slots_dev)
    ones = jnp.where(mine, 1.0, 0.0).astype(jnp.bfloat16)
    r = lax.broadcasted_iota(jnp.int32, (128, 128), 0)
    c = lax.broadcasted_iota(jnp.int32, (128, 128), 1)
    before = jnp.where(r < c, 1.0, 0.0).astype(jnp.bfloat16)
    within = jnp.dot(ones, before, preferred_element_type=jnp.float32)
    r = lax.broadcasted_iota(jnp.int32, (rows, rows), 0)
    c = lax.broadcasted_iota(jnp.int32, (rows, rows), 1)
    above = jnp.where(jnp.logical_and(r // per == c // per, c < r), 1.0, 0.0).astype(jnp.bfloat16)
    upto = jnp.dot(above, ones, preferred_element_type=jnp.float32)
    rank = within + jnp.sum(upto, axis=1, keepdims=True)
    rank = jnp.where(mine, rank, -1.0).reshape(COLS, per, 128)
    parity = lax.broadcasted_iota(jnp.int32, (rows, 128), 1) % 2
    local = jnp.where(mine, 2 * local + parity, 0).astype(jnp.float32).reshape(COLS, per, 128)
    lane = lax.broadcasted_iota(jnp.int32, (COLS, 128), 1)
    out = jnp.zeros((COLS, 128), jnp.float32)
    for j in range(CAP):
        picked = jnp.sum(jnp.where(rank == float(j), local, 0.0), axis=1)
        out = jnp.where(lane == j, jnp.sum(picked, axis=1, keepdims=True), out)
    out_ref[...] = out.astype(jnp.int32)


def fill_kernel(index_ref, tiles_ref, first_ref, second_ref, first_filled, second_filled, sems):
    copies = []
    for k, (filled, out_ref, base) in enumerate(((first_filled, first_ref, 0), (second_filled, second_ref, BATCH))):
        size = filled.shape[0] // COLS

        def group(g, carry, filled=filled, size=size, base=base):
            codes = [index_ref[g, base + j] for j in range(size)]
            tiles = [tiles_ref[code // 2] for code in codes]
            for j in range(size):
                turned = jnp.concatenate([tiles[j][:, TILE:], tiles[j][:, :TILE]], axis=1)
                filled[g * size + j] = jnp.where(codes[j] % 2 == 1, turned, tiles[j])
            return carry

        lax.fori_loop(0, COLS, group, 0)
        copies.append(pltpu.make_async_copy(filled, out_ref, sems.at[k]))
        copies[k].start()
    for copy in copies:
        copy.wait()


def compact_kernel(index_ref, spill_ref, second_ref, some_ref, rest_ref):
    def move(out_ref, base):
        def body(i, carry):
            tiles = [second_ref[index_ref[base + i * 16 + k]] for k in range(16)]
            for k in range(16):
                out_ref[i * 16 + k] = tiles[k]
            return carry

        lax.fori_loop(0, out_ref.shape[0] // 16, body, 0)

    move(some_ref, 0)

    @pl.when(spill_ref[0] > 0)
    def _():
        move(rest_ref, EXTRA)


def join_kernel(up_ref, down_ref, some_ref, up_out, down_out, sems):
    half = FIRST // 2
    copies = [
        pltpu.make_async_copy(up_ref.at[pl.ds(0, half)], up_out.at[pl.ds(0, half)], sems.at[0]),
        pltpu.make_async_copy(down_ref.at[pl.ds(half, half)], down_out.at[pl.ds(0, half)], sems.at[1]),
        pltpu.make_async_copy(some_ref, up_out.at[pl.ds(half, EXTRA)], sems.at[2]),
        pltpu.make_async_copy(some_ref, down_out.at[pl.ds(half, EXTRA)], sems.at[3]),
    ]
    for copy in copies:
        copy.start()
    for copy in copies:
        copy.wait()


def no_spill_kernel(tiles_ref, out_ref, sem):
    copy = pltpu.make_async_copy(tiles_ref.at[pl.ds(0, 1)], out_ref.at[pl.ds(0, 1)], sem)
    copy.start()
    copy.wait()


def no_spill_call(tiles):
    return pl.pallas_call(
        no_spill_kernel,
        in_specs=[pl.BlockSpec(memory_space=pl.ANY)],
        out_specs=pl.BlockSpec(memory_space=pl.ANY),
        out_shape=jax.ShapeDtypeStruct((THIRD, SUB, 128), jnp.bfloat16),
        scratch_shapes=[pltpu.SemaphoreType.DMA],
        compiler_params=pltpu.CompilerParams(vmem_limit_bytes=VMEM_GRANT),
        name="no_spill",
    )(tiles)


def prep_kernel(mask_ref, amp_ref, even_ref, odd_ref):
    blk = pl.program_id(0)
    rows = amp_ref.shape[0]
    r = lax.broadcasted_iota(jnp.int32, (256, 256), 0)
    c = lax.broadcasted_iota(jnp.int32, (256, 256), 1)
    source = (c % 128 // SUB) * TILE + 2 * (c % SUB) + c // 128
    shuffle = jnp.where(r == source, 1.0, 0.0).astype(jnp.bfloat16)
    moved = jnp.dot(amp_ref[...], shuffle, preferred_element_type=jnp.float32)
    mask = mask_ref[...].astype(jnp.bfloat16)
    r = lax.broadcasted_iota(jnp.int32, (mask.shape[1], 128), 0)
    c = lax.broadcasted_iota(jnp.int32, (mask.shape[1], 128), 1)
    spread = jnp.where(r == 4 * blk + c // SUB, 1.0, 0.0).astype(jnp.bfloat16)
    wide = jnp.dot(mask, spread, preferred_element_type=jnp.float32).astype(jnp.bfloat16)
    r = lax.broadcasted_iota(jnp.int32, (rows, mask.shape[0]), 0)
    c = lax.broadcasted_iota(jnp.int32, (rows, mask.shape[0]), 1)
    tall = jnp.where(r // TILE == c, 1.0, 0.0).astype(jnp.bfloat16)
    full = jnp.dot(tall, wide, preferred_element_type=jnp.float32)
    even_ref[...] = (moved[:, :128] * full).astype(jnp.bfloat16)
    odd_ref[...] = (moved[:, 128:] * full).astype(jnp.bfloat16)


def pack(out_ref, value):
    value = value.reshape(HALF // 16, 16, 128)
    top = jnp.maximum(jnp.max(jnp.abs(value), axis=1), 1e-30)
    exponent = jnp.ceil(jnp.log2(top * 1.0001))
    scaled = jnp.round(value * jnp.exp2(15.0 - exponent)[:, None, :]).reshape(HALF, 128)
    out_ref[pl.ds(0, HALF)] = scaled.astype(jnp.int32).astype(jnp.int16)
    out_ref[pl.ds(HALF, HALF // 16)] = exponent.astype(jnp.int32).astype(jnp.int16)


def unpack(ref):
    mantissa = ref[pl.ds(0, HALF)].astype(jnp.int32).astype(jnp.float32)
    exponent = ref[pl.ds(HALF, HALF // 16)].astype(jnp.int32).astype(jnp.float32)
    value = mantissa.reshape(HALF // 16, 16, 128) * jnp.exp2(exponent - 15.0)[:, None, :]
    return value.reshape(HALF, 128)


def collect_kernel(misc_ref, *refs):
    parts, third_ref, tiles, sems = refs[:PARTS], refs[PARTS], refs[PARTS + 1], refs[PARTS + 2]
    copies, base = [], 0
    for k, part in enumerate(parts):
        size = part.shape[0]
        copies.append(pltpu.make_async_copy(part, tiles.at[pl.ds(base, size)], sems.at[k]))
        base += size
    for copy in copies:
        copy.start()
    tiles[pl.ds(POOL, 1)] = jnp.zeros((1, SUB, 128), jnp.bfloat16)

    @pl.when(misc_ref[2] > 0)
    def _():
        copy = pltpu.make_async_copy(third_ref, tiles.at[pl.ds(base, THIRD)], sems.at[PARTS])
        copy.start()
        copy.wait()

    for copy in copies:
        copy.wait()


def collect_call(misc, parts, third):
    return pl.pallas_call(
        collect_kernel,
        in_specs=[pl.BlockSpec(memory_space=pltpu.SMEM)] + [pl.BlockSpec(memory_space=pl.ANY)] * (PARTS + 1),
        out_specs=pl.BlockSpec(memory_space=pltpu.VMEM),
        out_shape=jax.ShapeDtypeStruct((POOL + 1, SUB, 128), jnp.bfloat16),
        scratch_shapes=[pltpu.SemaphoreType.DMA((PARTS + 1,))],
        compiler_params=pltpu.CompilerParams(vmem_limit_bytes=2 * 1024 * 1024),
        cost_estimate=pl.CostEstimate(flops=0, bytes_accessed=POOL * 8192, transcendentals=0),
        name="collect",
    )(misc, *parts, third)


def build(hop, unit, index_ref, misc_ref, tiles, weight):
    at = [((misc_ref[0] + hop) % 4 * 4 + unit) * 4, (unit * 4 + (misc_ref[1] + hop) % 4) * 4 + 2]
    left = lax.broadcasted_iota(jnp.int32, (SUB, 128), 1) < TILE
    for kb in range(KB):
        picked = [tiles[index_ref[kb * NB + at[pair] + k]] for pair in range(2) for k in range(2)]
        rows = slice(kb * SUB, (kb + 1) * SUB)
        for pair in range(2):
            one, two = picked[2 * pair : 2 * pair + 2]
            columns = slice(128 * pair, 128 * pair + 128)
            weight[0][rows, columns] = jnp.where(left, one, two)
            weight[1][rows, columns] = jnp.where(left, two, one)


def product_kernel(hops, index_ref, misc_ref, even_ref, odd_ref, tiles, *refs):
    outs, weights = refs[:-4], (refs[-4:-2], refs[-2:])
    build(hops[0], 0, index_ref, misc_ref, tiles, weights[0])

    def emit(at, unit, weight):
        straight = jnp.dot(even_ref[...], weight[0][...], preferred_element_type=jnp.float32)
        crossed = jnp.dot(odd_ref[...], weight[1][...], preferred_element_type=jnp.float32)
        for way in range(2):
            columns = slice(way * 128, way * 128 + 128)
            value = straight[:, columns] + pltpu.roll(crossed[:, columns], TILE, 1)
            if hops == (0,):
                outs[way][unit] = value
                continue
            for half in range(2):
                out_ref = outs[2 * way + half] if len(hops) == 1 else outs[2 * way + at].at[half]
                pack(out_ref.at[unit], value[half * HALF : (half + 1) * HALF])

    for at, hop in enumerate(hops):
        after = hops[min(at + 1, len(hops) - 1)]

        def two_units(i, carry, at=at, hop=hop, after=after):
            build(hop, 2 * i + 1, index_ref, misc_ref, tiles, weights[1])
            emit(at, 2 * i, weights[0])
            build(jnp.where(i == 0, hop, after), 2 - 2 * i, index_ref, misc_ref, tiles, weights[0])
            emit(at, 2 * i + 1, weights[1])
            return carry

        lax.fori_loop(0, 2, two_units, 0)


def product_call(name, hops, scalars, arrays):
    rows_dev, depth_half = arrays[0].shape
    vmem = pl.BlockSpec(memory_space=pltpu.VMEM)
    if hops == (0,):
        outs = [jax.ShapeDtypeStruct((4, rows_dev, 128), jnp.float32)] * 2
    elif len(hops) == 1:
        outs = [jax.ShapeDtypeStruct((4, PACKED, 128), jnp.int16)] * 4
    else:
        outs = [jax.ShapeDtypeStruct((2, 4, PACKED, 128), jnp.int16)] * 4
    handed = [] if hops == (0,) else [jax.ShapeDtypeStruct(a.shape, a.dtype) for a in arrays]
    result = pl.pallas_call(
        functools.partial(product_kernel, hops),
        grid_spec=pltpu.PrefetchScalarGridSpec(
            num_scalar_prefetch=2,
            grid=(),
            in_specs=[vmem] * 3,
            out_specs=[vmem] * (len(outs) + len(handed)),
            scratch_shapes=[pltpu.VMEM((depth_half, 256), jnp.bfloat16)] * 4,
        ),
        out_shape=outs + handed,
        input_output_aliases={2 + k: len(outs) + k for k in range(len(handed))},
        compiler_params=pltpu.CompilerParams(vmem_limit_bytes=VMEM_GRANT),
        cost_estimate=pl.CostEstimate(
            flops=8 * len(hops) * rows_dev * depth_half * 512, bytes_accessed=POOL * 8192, transcendentals=0
        ),
        name=name,
    )(*scalars, *arrays)
    return result[: len(outs)], result[len(outs) :]


def ahead(axis, value):
    return lax.ppermute(value, axis, [(i, (i + 1) % 4) for i in range(4)])


def behind(axis, value):
    return lax.ppermute(value, axis, [(i, (i + 3) % 4) for i in range(4)])


def reach(tiles):
    return ahead("y", tiles), behind("y", tiles)


def swap(parts):
    return [lax.ppermute(part, "core", [(0, 1), (1, 0)]) for part in parts]


def add_first_kernel(*refs):
    def body(i, carry):
        for way in range(2):
            ahead_in, behind_in, came_a, came_b = refs[4 * way : 4 * way + 4]
            ahead_out, behind_out = refs[8 + 2 * way : 10 + 2 * way]
            pack(ahead_out.at[0, i], unpack(ahead_in.at[0, i]) + unpack(came_a.at[i]))
            ahead_out[1, i] = ahead_in[1, i]
            behind_out[0, i] = behind_in[0, i]
            pack(behind_out.at[1, i], unpack(behind_in.at[1, i]) + unpack(came_b.at[i]))
        return carry

    lax.fori_loop(0, 4, body, 0)


def add_second_kernel(*refs):
    for way in range(2):
        ahead_in, behind_in, came_a, came_b = refs[4 * way : 4 * way + 4]
        ahead_out, behind_out = refs[8 + 2 * way : 10 + 2 * way]
        pack(ahead_out.at[0], unpack(ahead_in.at[0]) + unpack(came_a.at[0]))
        ahead_out[1] = ahead_in[1]
        behind_out[0] = behind_in[0]
        pack(behind_out.at[1], unpack(behind_in.at[1]) + unpack(came_b.at[0]))


def whole_call(body, name, outs, *arrays, scalars=()):
    vmem = pl.BlockSpec(memory_space=pltpu.VMEM)
    size = sum(a.size * a.dtype.itemsize for a in [*arrays, *outs])
    return pl.pallas_call(
        body,
        in_specs=[pl.BlockSpec(memory_space=pltpu.SMEM)] * len(scalars) + [vmem] * len(arrays),
        out_specs=[vmem] * len(outs),
        out_shape=outs,
        compiler_params=pltpu.CompilerParams(vmem_limit_bytes=VMEM_GRANT),
        cost_estimate=pl.CostEstimate(flops=10 * size, bytes_accessed=size, transcendentals=0),
        name=name,
    )(*scalars, *arrays)


def middle_kernel(misc_ref, one_ref, two_ref, *refs):
    came, outs, own_ref = refs[:4], refs[4:12], refs[12]
    for way, own in enumerate((one_ref, two_ref)):
        right, left = came[2 * way : 2 * way + 2]
        far_a, far_b, ahead_ref, behind_ref = outs[4 * way : 4 * way + 4]
        for hop, ahead_by in enumerate((2, 1, 3, 0)):
            at = (misc_ref[1 - way] + ahead_by) % 4
            total = [
                own[at, pl.ds(half * HALF, HALF)] + unpack(right.at[half, at]) + unpack(left.at[half, at])
                for half in range(2)
            ]
            for half in range(2):
                if hop == 0:
                    pack((far_a, far_b)[half].at[0], total[half])
                elif hop < 3:
                    pack((ahead_ref, behind_ref)[hop - 1].at[half], total[half])
                else:
                    own_ref[pl.ds(half * HALF, HALF), pl.ds(way * 128, 128)] = total[half]


def last_kernel(own_ref, *refs):
    came, out_ref = refs[:4], refs[4]
    for way in range(2):
        right, left = came[2 * way : 2 * way + 2]
        columns = pl.ds(way * 128, 128)
        for half in range(2):
            rows = pl.ds(half * HALF, HALF)
            total = own_ref[rows, columns] + unpack(right.at[half]) + unpack(left.at[half])
            out_ref[columns, rows] = total.T


def shards(amplitudes, t2_mask, eri_tiles, eri_slot):
    y, core, x, z = (lax.axis_index(name) for name in ("y", "core", "x", "z"))
    group = x * 4 + z
    myself = (y * 2 + core) * COLS + group
    rows_dev, depth_dev = amplitudes.shape
    slots_dev = eri_tiles.shape[0]

    send_index = pl.pallas_call(
        lambda *refs: route_kernel(slots_dev, *refs),
        out_shape=jax.ShapeDtypeStruct((COLS, 128), jnp.int32),
        in_specs=[
            pl.BlockSpec(memory_space=pltpu.SMEM),
            pl.BlockSpec(memory_space=pltpu.VMEM),
        ],
        out_specs=pl.BlockSpec(memory_space=pltpu.VMEM),
        compiler_params=pltpu.CompilerParams(vmem_limit_bytes=VMEM_GRANT),
        name="route",
    )(myself.reshape(1).astype(jnp.int32), eri_slot.reshape(-1, 128))
    vmem = pl.BlockSpec(memory_space=pltpu.VMEM)
    outgoing = pl.pallas_call(
        fill_kernel,
        grid_spec=pltpu.PrefetchScalarGridSpec(
            num_scalar_prefetch=1,
            grid=(),
            in_specs=[vmem],
            out_specs=[pl.BlockSpec(memory_space=pltpu.HBM)] * 2,
            scratch_shapes=[
                pltpu.VMEM((FIRST, SUB, 128), jnp.bfloat16),
                pltpu.VMEM((SECOND, SUB, 128), jnp.bfloat16),
                pltpu.SemaphoreType.DMA((2,)),
            ],
        ),
        out_shape=[jax.ShapeDtypeStruct((size, SUB, 128), jnp.bfloat16) for size in (FIRST, SECOND)],
        compiler_params=pltpu.CompilerParams(vmem_limit_bytes=VMEM_GRANT),
        name="fill",
    )(send_index, eri_tiles.reshape(slots_dev, SUB, 128))

    def send(part):
        part = part.reshape(COLS, -1, SUB, 128)
        part = lax.all_to_all(part, ("x", "z"), split_axis=0, concat_axis=0, tiled=True)
        return part.reshape(-1, SUB, 128)

    first = send(outgoing[0])
    first, second, eri_slot = lax.optimization_barrier((first, outgoing[1], eri_slot))
    up, down = reach(first)
    second = send(second)
    devices = jnp.arange(DEVS, dtype=jnp.int32)
    owner_all = jnp.where(eri_slot >= 0, eri_slot // slots_dev, -1).reshape(COLS, 1, GROUP)
    held = jnp.sum((owner_all == devices[None, :, None]).astype(jnp.int32), axis=2)
    tail = jnp.maximum(held - BATCH, 0).reshape(COLS, ROWS, COLS)
    spill = jnp.any(jnp.sum(tail, axis=2) > EXTRA)
    tail = lax.dynamic_index_in_dim(tail, group, 0, keepdims=False)
    upto = jnp.sum(jnp.where(jnp.arange(COLS)[:, None] >= jnp.arange(COLS)[None, :], tail[:, None, :], 0), axis=2)
    start = upto - tail
    mine_upto = lax.dynamic_index_in_dim(upto, y * 2 + core, 0, keepdims=False)
    mine_start = lax.dynamic_index_in_dim(start, y * 2 + core, 0, keepdims=False)
    spot = jnp.arange(SECOND, dtype=jnp.int32)
    inside = jnp.logical_and(spot[:, None] >= mine_start[None, :], spot[:, None] < mine_upto[None, :])
    source = jnp.arange(COLS, dtype=jnp.int32)[None, :] * (CAP - BATCH) + spot[:, None] - mine_start[None, :]
    source = jnp.sum(jnp.where(inside, source, 0), axis=1).astype(jnp.int32)
    spill = spill.astype(jnp.int32).reshape(1)
    second, source, spill = lax.optimization_barrier((second, source, spill))
    half = FIRST // 2
    some, rest = pl.pallas_call(
        compact_kernel,
        grid_spec=pltpu.PrefetchScalarGridSpec(
            num_scalar_prefetch=2, grid=(), in_specs=[vmem], out_specs=[vmem] * 2
        ),
        out_shape=[jax.ShapeDtypeStruct((size, SUB, 128), jnp.bfloat16) for size in (EXTRA, SECOND - EXTRA)],
        compiler_params=pltpu.CompilerParams(vmem_limit_bytes=VMEM_GRANT),
        name="compact",
    )(source, spill, second)
    some, up, down = lax.optimization_barrier((some, up, down))
    from_up, from_down = pl.pallas_call(
        join_kernel,
        in_specs=[vmem] * 3,
        out_specs=[vmem] * 2,
        out_shape=[jax.ShapeDtypeStruct((half + EXTRA, SUB, 128), jnp.bfloat16)] * 2,
        scratch_shapes=[pltpu.SemaphoreType.DMA((4,))],
        compiler_params=pltpu.CompilerParams(vmem_limit_bytes=VMEM_GRANT),
        name="join",
    )(up, down, some)
    wanted = lax.dynamic_slice_in_dim(eri_slot, group * GROUP, GROUP)
    from_up, up, down, amplitudes, wanted = lax.optimization_barrier((from_up, up, down, amplitudes, wanted))
    from_up, from_down = ahead("y", from_up), behind("y", from_down)
    swapped = swap([first, up, down])

    parted = jax.ShapeDtypeStruct((rows_dev, depth_dev // 2), jnp.bfloat16)
    even, odd = pl.pallas_call(
        prep_kernel,
        grid=(depth_dev // 256,),
        out_shape=[parted] * 2,
        in_specs=[
            pl.BlockSpec(t2_mask.shape, lambda i: (0, 0)),
            pl.BlockSpec((rows_dev, 256), lambda i: (0, i)),
        ],
        out_specs=[pl.BlockSpec((rows_dev, 128), lambda i: (0, i))] * 2,
        compiler_params=pltpu.CompilerParams(vmem_limit_bytes=VMEM_GRANT),
        name="prep",
    )(t2_mask, amplitudes)

    owner = jnp.where(wanted >= 0, wanted // slots_dev, -1)
    mine = owner[:, None] == devices[None, :]
    spot = jnp.arange(GROUP, dtype=jnp.int32)
    before = (spot[:, None] > spot[None, :]).astype(jnp.bfloat16)
    counts = jnp.dot(before, mine.astype(jnp.bfloat16), preferred_element_type=jnp.float32)
    rank = jnp.sum(jnp.where(mine, counts, 0.0), axis=1).astype(jnp.int32)
    begin = jnp.sum(jnp.where(mine, start.reshape(1, DEVS), 0), axis=1)
    behind_first = begin + rank - BATCH
    owner_row = owner // COLS
    turn = (owner_row // 2 - y) % 4
    turn = jnp.where(turn == 1, 2, jnp.where(turn == 2, 3, jnp.where(turn == 3, 1, 0)))
    size = FIRST
    slot = owner % COLS * BATCH + rank
    early = turn * size + slot + jnp.where(jnp.logical_and(turn == 3, slot >= half), EXTRA, 0)
    begins = (4 * size + 2 * EXTRA, 3 * size + half, 4 * size + EXTRA, 4 * size + 3 * EXTRA)
    late = behind_first + sum(jnp.where(turn == k, begin_late, 0) for k, begin_late in enumerate(begins))
    tile_index = jnp.where(rank < BATCH, early, late) + CORE * (owner_row % 2 != core)
    spilled = 2 * CORE + owner_row * (SECOND - EXTRA) + behind_first - EXTRA
    tile_index = jnp.where(jnp.logical_or(rank < BATCH, behind_first < EXTRA), tile_index, spilled)
    tile_index = jnp.where(wanted < 0, POOL, tile_index)
    misc = jnp.stack([x, z, spill[0]]).astype(jnp.int32)
    third = lax.cond(
        misc[2] > 0,
        lambda value: lax.all_gather(value, ("y", "core"), axis=0, tiled=True),
        no_spill_call,
        rest,
    )
    from_up, from_down, swapped, even, odd, tile_index, misc, third = lax.optimization_barrier(
        (from_up, from_down, swapped, even, odd, tile_index, misc, third)
    )
    tails = from_up[half : half + EXTRA // 2], from_down[half + EXTRA // 2 :]
    tails, from_up, from_down = lax.optimization_barrier((tails, from_up, from_down))
    tail_up, tail_down = ahead("y", tails[0]), behind("y", tails[1])
    parts = [first, up, down, from_up, from_down, some, jnp.concatenate([tail_up, tail_down])]
    tiles = collect_call(misc, parts + swapped + swap(parts[3:]), third)

    scalars = (tile_index, misc)
    far, arrays = product_call("far", (2,), scalars, (even, odd, tiles))
    axes = ("x", "z")
    near, arrays = product_call("near", (1, 3), scalars, arrays)
    inputs = []
    for way, axis in enumerate(axes):
        inputs += [*near[2 * way : 2 * way + 2], ahead(axis, far[2 * way]), behind(axis, far[2 * way + 1])]
    packed = jax.ShapeDtypeStruct((2, 4, PACKED, 128), jnp.int16)
    added = whole_call(add_first_kernel, "add_first", [packed] * 4, *inputs)
    came = []
    for way, axis in enumerate(axes):
        came += [ahead(axis, added[2 * way]), behind(axis, added[2 * way + 1])]
    (one, two), _ = product_call("own", (0,), scalars, arrays)
    single = jax.ShapeDtypeStruct((1, PACKED, 128), jnp.int16)
    double = jax.ShapeDtypeStruct((2, PACKED, 128), jnp.int16)
    *outs, own = whole_call(
        middle_kernel,
        "middle",
        [single, single, double, double] * 2 + [jax.ShapeDtypeStruct((rows_dev, 256), jnp.float32)],
        one,
        two,
        *came,
        scalars=(misc,),
    )
    axes = ("z", "x")
    inputs = []
    for way, axis in enumerate(axes):
        far_a, far_b, next_ab, prev_ab = outs[4 * way : 4 * way + 4]
        inputs += [next_ab, prev_ab, ahead(axis, far_a), behind(axis, far_b)]
    added = whole_call(add_second_kernel, "add_second", [double] * 4, *inputs)
    came = []
    for way, axis in enumerate(axes):
        came += [ahead(axis, added[2 * way]), behind(axis, added[2 * way + 1])]
    return whole_call(
        last_kernel, "last", [jax.ShapeDtypeStruct((256, rows_dev), jnp.float32)], own, *came
    )[0]


def solution(mesh):
    axes = ("y", "core", "x", "z")
    fine = Mesh(mesh.devices.reshape(4, 2, 4, 4), axes)
    row, col = ("y", "core"), ("x", "z")
    in_specs = (P(row, col), P(row, col), P(axes, None), P())
    out_specs = P(col, row)
    return jax.shard_map(shards, mesh=fine, in_specs=in_specs, out_specs=out_specs, check_vma=False)
```

```python
import functools

import jax
import jax.numpy as jnp
from jax import lax
from jax.experimental import pallas as pl
from jax.experimental.pallas import tpu as pltpu
from jax.sharding import Mesh
from jax.sharding import PartitionSpec as P

TILE = 64
VTILES = 32
KOCC = 16
JOCC = 2
CAP = 20
COLS = 16
ROWS = 8
DEVS = 128
GROUP = VTILES * KOCC * VTILES * JOCC // COLS
KB = GROUP // (VTILES * JOCC)
NB = VTILES * JOCC
SUB = TILE * TILE // 128
BATCH = 8
FIRST = COLS * BATCH
SECOND = COLS * (CAP - BATCH)
EXTRA = 80
CORE = 4 * FIRST + 4 * EXTRA
THIRD = ROWS * (SECOND - EXTRA)
POOL = 2 * CORE + THIRD
PARTS = 14
HALF = 512
SHARE = 32
PACKED = HALF + HALF // SHARE
VMEM_GRANT = 10 * 1024 * 1024


def route_kernel(slots_dev, me_ref, slot_ref, out_ref):
    base = me_ref[0] * slots_dev
    slot = slot_ref[...]
    rows = slot.shape[0]
    per = rows // COLS
    local = slot - base
    mine = jnp.logical_and(local >= 0, local < slots_dev)
    ones = jnp.where(mine, 1.0, 0.0).astype(jnp.bfloat16)
    r = lax.broadcasted_iota(jnp.int32, (128, 128), 0)
    c = lax.broadcasted_iota(jnp.int32, (128, 128), 1)
    before = jnp.where(r < c, 1.0, 0.0).astype(jnp.bfloat16)
    within = jnp.dot(ones, before, preferred_element_type=jnp.float32)
    r = lax.broadcasted_iota(jnp.int32, (rows, rows), 0)
    c = lax.broadcasted_iota(jnp.int32, (rows, rows), 1)
    above = jnp.where(jnp.logical_and(r // per == c // per, c < r), 1.0, 0.0).astype(jnp.bfloat16)
    upto = jnp.dot(above, ones, preferred_element_type=jnp.float32)
    rank = within + jnp.sum(upto, axis=1, keepdims=True)
    rank = jnp.where(mine, rank, -1.0).reshape(COLS, per, 128)
    parity = lax.broadcasted_iota(jnp.int32, (rows, 128), 1) % 2
    local = jnp.where(mine, 2 * local + parity, 0).astype(jnp.float32).reshape(COLS, per, 128)
    lane = lax.broadcasted_iota(jnp.int32, (COLS, 128), 1)
    out = jnp.zeros((COLS, 128), jnp.float32)
    for j in range(CAP):
        picked = jnp.sum(jnp.where(rank == float(j), local, 0.0), axis=1)
        out = jnp.where(lane == j, jnp.sum(picked, axis=1, keepdims=True), out)
    out_ref[...] = out.astype(jnp.int32)


def fill_kernel(index_ref, tiles_ref, first_ref, second_ref, first_filled, second_filled, sems):
    copies = []
    for k, (filled, out_ref, base) in enumerate(((first_filled, first_ref, 0), (second_filled, second_ref, BATCH))):
        size = filled.shape[0] // COLS

        def group(g, carry, filled=filled, size=size, base=base):
            codes = [index_ref[g, base + j] for j in range(size)]
            tiles = [tiles_ref[code // 2] for code in codes]
            for j in range(size):
                turned = jnp.concatenate([tiles[j][:, TILE:], tiles[j][:, :TILE]], axis=1)
                filled[g * size + j] = jnp.where(codes[j] % 2 == 1, turned, tiles[j])
            return carry

        lax.fori_loop(0, COLS, group, 0)
        copies.append(pltpu.make_async_copy(filled, out_ref, sems.at[k]))
        copies[k].start()
    for copy in copies:
        copy.wait()


def compact_kernel(index_ref, spill_ref, second_ref, some_ref, rest_ref):
    def move(out_ref, base):
        def body(i, carry):
            tiles = [second_ref[index_ref[base + i * 16 + k]] for k in range(16)]
            for k in range(16):
                out_ref[i * 16 + k] = tiles[k]
            return carry

        lax.fori_loop(0, out_ref.shape[0] // 16, body, 0)

    move(some_ref, 0)

    @pl.when(spill_ref[0] > 0)
    def _():
        move(rest_ref, EXTRA)


def join_kernel(up_ref, down_ref, some_ref, up_out, down_out, sems):
    half = FIRST // 2
    copies = [
        pltpu.make_async_copy(up_ref.at[pl.ds(0, half)], up_out.at[pl.ds(0, half)], sems.at[0]),
        pltpu.make_async_copy(down_ref.at[pl.ds(half, half)], down_out.at[pl.ds(0, half)], sems.at[1]),
    ]
    for copy in copies:
        copy.start()

    def body(i, carry):
        tiles = [some_ref[i * 16 + k] for k in range(16)]
        for k in range(16):
            up_out[half + i * 16 + k] = tiles[k]
            down_out[half + i * 16 + k] = tiles[k]
        return carry

    lax.fori_loop(0, EXTRA // 16, body, 0)
    for copy in copies:
        copy.wait()


def tail_kernel(some_ref, up_ref, down_ref, out_ref):
    size = EXTRA // 2

    def body(i, carry):
        sources = [(some_ref, size), (up_ref, 0), (down_ref, 0)]
        tiles = [[ref[base + i * 8 + k] for k in range(8)] for ref, base in sources]
        for part in range(3):
            for k in range(8):
                out_ref[part * size + i * 8 + k] = tiles[part][k]
        return carry

    lax.fori_loop(0, size // 8, body, 0)


def no_spill_kernel(tiles_ref, out_ref, sem):
    copy = pltpu.make_async_copy(tiles_ref.at[pl.ds(0, 1)], out_ref.at[pl.ds(0, 1)], sem)
    copy.start()
    copy.wait()


def no_spill_call(tiles):
    return pl.pallas_call(
        no_spill_kernel,
        in_specs=[pl.BlockSpec(memory_space=pl.ANY)],
        out_specs=pl.BlockSpec(memory_space=pl.ANY),
        out_shape=jax.ShapeDtypeStruct((THIRD, SUB, 128), jnp.bfloat16),
        scratch_shapes=[pltpu.SemaphoreType.DMA],
        compiler_params=pltpu.CompilerParams(vmem_limit_bytes=VMEM_GRANT),
        name="no_spill",
    )(tiles)


def prep_kernel(mask_ref, amp_ref, even_ref, odd_ref):
    blk = pl.program_id(0)
    rows = amp_ref.shape[0]
    r = lax.broadcasted_iota(jnp.int32, (256, 256), 0)
    c = lax.broadcasted_iota(jnp.int32, (256, 256), 1)
    source = (c % 128 // SUB) * TILE + 2 * (c % SUB) + c // 128
    shuffle = jnp.where(r == source, 1.0, 0.0).astype(jnp.bfloat16)
    moved = jnp.dot(amp_ref[...], shuffle, preferred_element_type=jnp.float32)
    mask = mask_ref[...].astype(jnp.bfloat16)
    r = lax.broadcasted_iota(jnp.int32, (mask.shape[1], 128), 0)
    c = lax.broadcasted_iota(jnp.int32, (mask.shape[1], 128), 1)
    spread = jnp.where(r == 4 * blk + c // SUB, 1.0, 0.0).astype(jnp.bfloat16)
    wide = jnp.dot(mask, spread, preferred_element_type=jnp.float32).astype(jnp.bfloat16)
    r = lax.broadcasted_iota(jnp.int32, (rows, mask.shape[0]), 0)
    c = lax.broadcasted_iota(jnp.int32, (rows, mask.shape[0]), 1)
    tall = jnp.where(r // TILE == c, 1.0, 0.0).astype(jnp.bfloat16)
    full = jnp.dot(tall, wide, preferred_element_type=jnp.float32)
    even_ref[...] = (moved[:, :128] * full).astype(jnp.bfloat16)
    odd_ref[...] = (moved[:, 128:] * full).astype(jnp.bfloat16)


def pack(out_ref, value):
    value = value.reshape(HALF // SHARE, SHARE, 128)
    top = jnp.maximum(jnp.max(jnp.abs(value), axis=1), 1e-30)
    exponent = jnp.ceil(jnp.log2(top * 1.0001))
    scaled = jnp.round(value * jnp.exp2(15.0 - exponent)[:, None, :]).reshape(HALF, 128)
    out_ref[pl.ds(0, HALF)] = scaled.astype(jnp.int32).astype(jnp.int16)
    out_ref[pl.ds(HALF, HALF // SHARE)] = exponent.astype(jnp.int32).astype(jnp.int16)


def unpack(ref):
    mantissa = ref[pl.ds(0, HALF)].astype(jnp.int32).astype(jnp.float32)
    exponent = ref[pl.ds(HALF, HALF // SHARE)].astype(jnp.int32).astype(jnp.float32)
    value = mantissa.reshape(HALF // SHARE, SHARE, 128) * jnp.exp2(exponent - 15.0)[:, None, :]
    return value.reshape(HALF, 128)


def collect_kernel(misc_ref, *refs):
    parts, third_ref, tiles, sems = refs[:PARTS], refs[PARTS], refs[PARTS + 1], refs[PARTS + 2]
    copies, base = [], 0
    for k, part in enumerate(parts):
        size = part.shape[0]
        copies.append(pltpu.make_async_copy(part, tiles.at[pl.ds(base, size)], sems.at[k]))
        base += size
    for copy in copies:
        copy.start()
    tiles[pl.ds(POOL, 1)] = jnp.zeros((1, SUB, 128), jnp.bfloat16)

    @pl.when(misc_ref[2] > 0)
    def _():
        copy = pltpu.make_async_copy(third_ref, tiles.at[pl.ds(base, THIRD)], sems.at[PARTS])
        copy.start()
        copy.wait()

    for copy in copies:
        copy.wait()


def collect_call(misc, parts, third):
    return pl.pallas_call(
        collect_kernel,
        in_specs=[pl.BlockSpec(memory_space=pltpu.SMEM)] + [pl.BlockSpec(memory_space=pl.ANY)] * (PARTS + 1),
        out_specs=pl.BlockSpec(memory_space=pltpu.VMEM),
        out_shape=jax.ShapeDtypeStruct((POOL + 1, SUB, 128), jnp.bfloat16),
        scratch_shapes=[pltpu.SemaphoreType.DMA((PARTS + 1,))],
        compiler_params=pltpu.CompilerParams(vmem_limit_bytes=2 * 1024 * 1024),
        cost_estimate=pl.CostEstimate(flops=0, bytes_accessed=POOL * 8192, transcendentals=0),
        name="collect",
    )(misc, *parts, third)


def build(hop, unit, index_ref, misc_ref, tiles, weight):
    at = [((misc_ref[0] + hop) % 4 * 4 + unit) * 4, (unit * 4 + (misc_ref[1] + hop) % 4) * 4 + 2]
    left = lax.broadcasted_iota(jnp.int32, (SUB, 128), 1) < TILE
    for kb in range(KB):
        picked = [tiles[index_ref[kb * NB + at[pair] + k]] for pair in range(2) for k in range(2)]
        rows = slice(kb * SUB, (kb + 1) * SUB)
        for pair in range(2):
            one, two = picked[2 * pair : 2 * pair + 2]
            columns = slice(128 * pair, 128 * pair + 128)
            weight[0][rows, columns] = jnp.where(left, one, two)
            weight[1][rows, columns] = jnp.where(left, two, one)


def product_kernel(hops, index_ref, misc_ref, even_ref, odd_ref, tiles, *refs):
    outs, weights = refs[:-4], (refs[-4:-2], refs[-2:])
    build(hops[0], 0, index_ref, misc_ref, tiles, weights[0])

    def emit(at, unit, weight):
        straight = jnp.dot(even_ref[...], weight[0][...], preferred_element_type=jnp.float32)
        crossed = jnp.dot(odd_ref[...], weight[1][...], preferred_element_type=jnp.float32)
        for way in range(2):
            columns = slice(way * 128, way * 128 + 128)
            value = straight[:, columns] + pltpu.roll(crossed[:, columns], TILE, 1)
            if hops == (0,):
                outs[way][unit] = value
                continue
            for half in range(2):
                out_ref = outs[2 * way + half] if len(hops) == 1 else outs[2 * way + at].at[half]
                pack(out_ref.at[unit], value[half * HALF : (half + 1) * HALF])

    for at, hop in enumerate(hops):
        after = hops[min(at + 1, len(hops) - 1)]

        def two_units(i, carry, at=at, hop=hop, after=after):
            build(hop, 2 * i + 1, index_ref, misc_ref, tiles, weights[1])
            emit(at, 2 * i, weights[0])
            build(jnp.where(i == 0, hop, after), 2 - 2 * i, index_ref, misc_ref, tiles, weights[0])
            emit(at, 2 * i + 1, weights[1])
            return carry

        lax.fori_loop(0, 2, two_units, 0)


def product_call(name, hops, scalars, arrays):
    rows_dev, depth_half = arrays[0].shape
    vmem = pl.BlockSpec(memory_space=pltpu.VMEM)
    if hops == (0,):
        outs = [jax.ShapeDtypeStruct((4, rows_dev, 128), jnp.float32)] * 2
    elif len(hops) == 1:
        outs = [jax.ShapeDtypeStruct((4, PACKED, 128), jnp.int16)] * 4
    else:
        outs = [jax.ShapeDtypeStruct((2, 4, PACKED, 128), jnp.int16)] * 4
    handed = [] if hops == (0,) else [jax.ShapeDtypeStruct(a.shape, a.dtype) for a in arrays]
    result = pl.pallas_call(
        functools.partial(product_kernel, hops),
        grid_spec=pltpu.PrefetchScalarGridSpec(
            num_scalar_prefetch=2,
            grid=(),
            in_specs=[vmem] * 3,
            out_specs=[vmem] * (len(outs) + len(handed)),
            scratch_shapes=[pltpu.VMEM((depth_half, 256), jnp.bfloat16)] * 4,
        ),
        out_shape=outs + handed,
        input_output_aliases={2 + k: len(outs) + k for k in range(len(handed))},
        compiler_params=pltpu.CompilerParams(vmem_limit_bytes=VMEM_GRANT),
        cost_estimate=pl.CostEstimate(
            flops=8 * len(hops) * rows_dev * depth_half * 512, bytes_accessed=POOL * 8192, transcendentals=0
        ),
        name=name,
    )(*scalars, *arrays)
    return result[: len(outs)], result[len(outs) :]


def ahead(axis, value):
    return lax.ppermute(value, axis, [(i, (i + 1) % 4) for i in range(4)])


def behind(axis, value):
    return lax.ppermute(value, axis, [(i, (i + 3) % 4) for i in range(4)])


def reach(tiles):
    return ahead("y", tiles), behind("y", tiles)


def swap(parts):
    return [lax.ppermute(part, "core", [(0, 1), (1, 0)]) for part in parts]


def add_first_kernel(*refs):
    def body(i, carry):
        for way in range(2):
            ahead_in, behind_in, came_a, came_b = refs[4 * way : 4 * way + 4]
            ahead_out, behind_out = refs[8 + 2 * way : 10 + 2 * way]
            pack(ahead_out.at[0, i], unpack(ahead_in.at[0, i]) + unpack(came_a.at[i]))
            ahead_out[1, i] = ahead_in[1, i]
            behind_out[0, i] = behind_in[0, i]
            pack(behind_out.at[1, i], unpack(behind_in.at[1, i]) + unpack(came_b.at[i]))
        return carry

    lax.fori_loop(0, 4, body, 0)


def add_second_kernel(*refs):
    for way in range(2):
        ahead_in, behind_in, came_a, came_b = refs[4 * way : 4 * way + 4]
        ahead_out, behind_out = refs[8 + 2 * way : 10 + 2 * way]
        pack(ahead_out.at[0], unpack(ahead_in.at[0]) + unpack(came_a.at[0]))
        ahead_out[1] = ahead_in[1]
        behind_out[0] = behind_in[0]
        pack(behind_out.at[1], unpack(behind_in.at[1]) + unpack(came_b.at[0]))


def whole_call(body, name, outs, *arrays, scalars=()):
    vmem = pl.BlockSpec(memory_space=pltpu.VMEM)
    size = sum(a.size * a.dtype.itemsize for a in [*arrays, *outs])
    return pl.pallas_call(
        body,
        in_specs=[pl.BlockSpec(memory_space=pltpu.SMEM)] * len(scalars) + [vmem] * len(arrays),
        out_specs=[vmem] * len(outs),
        out_shape=outs,
        compiler_params=pltpu.CompilerParams(vmem_limit_bytes=VMEM_GRANT),
        cost_estimate=pl.CostEstimate(flops=10 * size, bytes_accessed=size, transcendentals=0),
        name=name,
    )(*scalars, *arrays)


def middle_kernel(misc_ref, one_ref, two_ref, *refs):
    came, outs, own_ref = refs[:4], refs[4:12], refs[12]
    for way, own in enumerate((one_ref, two_ref)):
        right, left = came[2 * way : 2 * way + 2]
        far_a, far_b, ahead_ref, behind_ref = outs[4 * way : 4 * way + 4]
        for hop, ahead_by in enumerate((2, 1, 3, 0)):
            at = (misc_ref[1 - way] + ahead_by) % 4
            total = [
                own[at, pl.ds(half * HALF, HALF)] + unpack(right.at[half, at]) + unpack(left.at[half, at])
                for half in range(2)
            ]
            for half in range(2):
                if hop == 0:
                    pack((far_a, far_b)[half].at[0], total[half])
                elif hop < 3:
                    pack((ahead_ref, behind_ref)[hop - 1].at[half], total[half])
                else:
                    own_ref[pl.ds(half * HALF, HALF), pl.ds(way * 128, 128)] = total[half]


def last_kernel(own_ref, *refs):
    came, out_ref = refs[:4], refs[4]
    for way in range(2):
        right, left = came[2 * way : 2 * way + 2]
        columns = pl.ds(way * 128, 128)
        for half in range(2):
            rows = pl.ds(half * HALF, HALF)
            total = own_ref[rows, columns] + unpack(right.at[half]) + unpack(left.at[half])
            out_ref[columns, rows] = total.T


def shards(amplitudes, t2_mask, eri_tiles, eri_slot):
    y, core, x, z = (lax.axis_index(name) for name in ("y", "core", "x", "z"))
    group = x * 4 + z
    myself = (y * 2 + core) * COLS + group
    rows_dev, depth_dev = amplitudes.shape
    slots_dev = eri_tiles.shape[0]

    send_index = pl.pallas_call(
        lambda *refs: route_kernel(slots_dev, *refs),
        out_shape=jax.ShapeDtypeStruct((COLS, 128), jnp.int32),
        in_specs=[
            pl.BlockSpec(memory_space=pltpu.SMEM),
            pl.BlockSpec(memory_space=pltpu.VMEM),
        ],
        out_specs=pl.BlockSpec(memory_space=pltpu.VMEM),
        compiler_params=pltpu.CompilerParams(vmem_limit_bytes=VMEM_GRANT),
        name="route",
    )(myself.reshape(1).astype(jnp.int32), eri_slot.reshape(-1, 128))
    vmem = pl.BlockSpec(memory_space=pltpu.VMEM)
    outgoing = pl.pallas_call(
        fill_kernel,
        grid_spec=pltpu.PrefetchScalarGridSpec(
            num_scalar_prefetch=1,
            grid=(),
            in_specs=[vmem],
            out_specs=[pl.BlockSpec(memory_space=pltpu.HBM)] * 2,
            scratch_shapes=[
                pltpu.VMEM((FIRST, SUB, 128), jnp.bfloat16),
                pltpu.VMEM((SECOND, SUB, 128), jnp.bfloat16),
                pltpu.SemaphoreType.DMA((2,)),
            ],
        ),
        out_shape=[jax.ShapeDtypeStruct((size, SUB, 128), jnp.bfloat16) for size in (FIRST, SECOND)],
        compiler_params=pltpu.CompilerParams(vmem_limit_bytes=VMEM_GRANT),
        name="fill",
    )(send_index, eri_tiles.reshape(slots_dev, SUB, 128))

    def send(part):
        part = part.reshape(COLS, -1, SUB, 128)
        part = lax.all_to_all(part, ("x", "z"), split_axis=0, concat_axis=0, tiled=True)
        return part.reshape(-1, SUB, 128)

    first = send(outgoing[0])
    first, second, eri_slot = lax.optimization_barrier((first, outgoing[1], eri_slot))
    up, down = reach(first)
    second = send(second)
    devices = jnp.arange(DEVS, dtype=jnp.int32)
    owner_all = jnp.where(eri_slot >= 0, eri_slot // slots_dev, -1).reshape(COLS, 1, GROUP)
    held = jnp.sum((owner_all == devices[None, :, None]).astype(jnp.int32), axis=2)
    tail = jnp.maximum(held - BATCH, 0).reshape(COLS, ROWS, COLS)
    spill = jnp.any(jnp.sum(tail, axis=2) > EXTRA)
    tail = lax.dynamic_index_in_dim(tail, group, 0, keepdims=False)
    upto = jnp.sum(jnp.where(jnp.arange(COLS)[:, None] >= jnp.arange(COLS)[None, :], tail[:, None, :], 0), axis=2)
    start = upto - tail
    mine_upto = lax.dynamic_index_in_dim(upto, y * 2 + core, 0, keepdims=False)
    mine_start = lax.dynamic_index_in_dim(start, y * 2 + core, 0, keepdims=False)
    spot = jnp.arange(SECOND, dtype=jnp.int32)
    inside = jnp.logical_and(spot[:, None] >= mine_start[None, :], spot[:, None] < mine_upto[None, :])
    source = jnp.arange(COLS, dtype=jnp.int32)[None, :] * (CAP - BATCH) + spot[:, None] - mine_start[None, :]
    source = jnp.sum(jnp.where(inside, source, 0), axis=1).astype(jnp.int32)
    spill = spill.astype(jnp.int32).reshape(1)
    second, source, spill = lax.optimization_barrier((second, source, spill))
    half = FIRST // 2
    some, rest = pl.pallas_call(
        compact_kernel,
        grid_spec=pltpu.PrefetchScalarGridSpec(
            num_scalar_prefetch=2, grid=(), in_specs=[vmem], out_specs=[vmem] * 2
        ),
        out_shape=[jax.ShapeDtypeStruct((size, SUB, 128), jnp.bfloat16) for size in (EXTRA, SECOND - EXTRA)],
        compiler_params=pltpu.CompilerParams(vmem_limit_bytes=VMEM_GRANT),
        name="compact",
    )(source, spill, second)
    some, up, down = lax.optimization_barrier((some, up, down))
    from_up, from_down = pl.pallas_call(
        join_kernel,
        in_specs=[vmem] * 3,
        out_specs=[vmem] * 2,
        out_shape=[jax.ShapeDtypeStruct((half + EXTRA, SUB, 128), jnp.bfloat16)] * 2,
        scratch_shapes=[pltpu.SemaphoreType.DMA((2,))],
        compiler_params=pltpu.CompilerParams(vmem_limit_bytes=VMEM_GRANT),
        name="join",
    )(up, down, some)
    wanted = lax.dynamic_slice_in_dim(eri_slot, group * GROUP, GROUP)
    from_up, up, down, amplitudes, wanted = lax.optimization_barrier((from_up, up, down, amplitudes, wanted))
    from_up, from_down = ahead("y", from_up), behind("y", from_down)
    swapped = swap([first, up, down])

    parted = jax.ShapeDtypeStruct((rows_dev, depth_dev // 2), jnp.bfloat16)
    even, odd = pl.pallas_call(
        prep_kernel,
        grid=(depth_dev // 256,),
        out_shape=[parted] * 2,
        in_specs=[
            pl.BlockSpec(t2_mask.shape, lambda i: (0, 0)),
            pl.BlockSpec((rows_dev, 256), lambda i: (0, i)),
        ],
        out_specs=[pl.BlockSpec((rows_dev, 128), lambda i: (0, i))] * 2,
        compiler_params=pltpu.CompilerParams(vmem_limit_bytes=VMEM_GRANT),
        name="prep",
    )(t2_mask, amplitudes)

    owner = jnp.where(wanted >= 0, wanted // slots_dev, -1)
    mine = owner[:, None] == devices[None, :]
    spot = jnp.arange(GROUP, dtype=jnp.int32)
    before = (spot[:, None] > spot[None, :]).astype(jnp.bfloat16)
    counts = jnp.dot(before, mine.astype(jnp.bfloat16), preferred_element_type=jnp.float32)
    rank = jnp.sum(jnp.where(mine, counts, 0.0), axis=1).astype(jnp.int32)
    begin = jnp.sum(jnp.where(mine, start.reshape(1, DEVS), 0), axis=1)
    behind_first = begin + rank - BATCH
    owner_row = owner // COLS
    turn = (owner_row // 2 - y) % 4
    turn = jnp.where(turn == 1, 2, jnp.where(turn == 2, 3, jnp.where(turn == 3, 1, 0)))
    size = FIRST
    slot = owner % COLS * BATCH + rank
    early = turn * size + slot + jnp.where(jnp.logical_and(turn == 3, slot >= half), EXTRA, 0)
    begins = (4 * size + 2 * EXTRA, 3 * size + half, 4 * size + EXTRA, 4 * size + 3 * EXTRA)
    late = behind_first + sum(jnp.where(turn == k, begin_late, 0) for k, begin_late in enumerate(begins))
    tile_index = jnp.where(rank < BATCH, early, late) + CORE * (owner_row % 2 != core)
    spilled = 2 * CORE + owner_row * (SECOND - EXTRA) + behind_first - EXTRA
    tile_index = jnp.where(jnp.logical_or(rank < BATCH, behind_first < EXTRA), tile_index, spilled)
    tile_index = jnp.where(wanted < 0, POOL, tile_index)
    misc = jnp.stack([x, z, spill[0]]).astype(jnp.int32)
    third = lax.cond(
        misc[2] > 0,
        lambda value: lax.all_gather(value, ("y", "core"), axis=0, tiled=True),
        no_spill_call,
        rest,
    )
    from_up, from_down, swapped, even, odd, tile_index, misc, third = lax.optimization_barrier(
        (from_up, from_down, swapped, even, odd, tile_index, misc, third)
    )
    tails = from_up[half : half + EXTRA // 2], from_down[half + EXTRA // 2 :]
    tails, from_up, from_down = lax.optimization_barrier((tails, from_up, from_down))
    tail_up, tail_down = ahead("y", tails[0]), behind("y", tails[1])
    tail = jax.ShapeDtypeStruct((3 * EXTRA // 2, SUB, 128), jnp.bfloat16)
    (tail,) = whole_call(tail_kernel, "tail", [tail], some, tail_up, tail_down)
    parts = [first, up, down, from_up, from_down, some[: EXTRA // 2], tail]
    tiles = collect_call(misc, parts + swapped + swap(parts[3:]), third)

    scalars = (tile_index, misc)
    far, arrays = product_call("far", (2,), scalars, (even, odd, tiles))
    axes = ("x", "z")
    near, arrays = product_call("near", (1, 3), scalars, arrays)
    inputs = []
    for way, axis in enumerate(axes):
        inputs += [*near[2 * way : 2 * way + 2], ahead(axis, far[2 * way]), behind(axis, far[2 * way + 1])]
    packed = jax.ShapeDtypeStruct((2, 4, PACKED, 128), jnp.int16)
    added = whole_call(add_first_kernel, "add_first", [packed] * 4, *inputs)
    came = []
    for way, axis in enumerate(axes):
        came += [ahead(axis, added[2 * way]), behind(axis, added[2 * way + 1])]
    (one, two), _ = product_call("own", (0,), scalars, arrays)
    single = jax.ShapeDtypeStruct((1, PACKED, 128), jnp.int16)
    double = jax.ShapeDtypeStruct((2, PACKED, 128), jnp.int16)
    *outs, own = whole_call(
        middle_kernel,
        "middle",
        [single, single, double, double] * 2 + [jax.ShapeDtypeStruct((rows_dev, 256), jnp.float32)],
        one,
        two,
        *came,
        scalars=(misc,),
    )
    axes = ("z", "x")
    inputs = []
    for way, axis in enumerate(axes):
        far_a, far_b, next_ab, prev_ab = outs[4 * way : 4 * way + 4]
        inputs += [next_ab, prev_ab, ahead(axis, far_a), behind(axis, far_b)]
    added = whole_call(add_second_kernel, "add_second", [double] * 4, *inputs)
    came = []
    for way, axis in enumerate(axes):
        came += [ahead(axis, added[2 * way]), behind(axis, added[2 * way + 1])]
    return whole_call(
        last_kernel, "last", [jax.ShapeDtypeStruct((256, rows_dev), jnp.float32)], own, *came
    )[0]


def solution(mesh):
    axes = ("y", "core", "x", "z")
    fine = Mesh(mesh.devices.reshape(4, 2, 4, 4), axes)
    row, col = ("y", "core"), ("x", "z")
    in_specs = (P(row, col), P(row, col), P(axes, None), P())
    out_specs = P(col, row)
    return jax.shard_map(shards, mesh=fine, in_specs=in_specs, out_specs=out_specs, check_vma=False)
```

```python
import functools

import jax
import jax.numpy as jnp
from jax import lax
from jax.experimental import pallas as pl
from jax.experimental.pallas import tpu as pltpu
from jax.sharding import Mesh
from jax.sharding import PartitionSpec as P

TILE = 64
VTILES = 32
KOCC = 16
JOCC = 2
CAP = 20
COLS = 16
ROWS = 8
DEVS = 128
GROUP = VTILES * KOCC * VTILES * JOCC // COLS
KB = GROUP // (VTILES * JOCC)
NB = VTILES * JOCC
SUB = TILE * TILE // 128
BATCH = 8
FIRST = COLS * BATCH
SECOND = COLS * (CAP - BATCH)
EXTRA = 80
CORE = 4 * FIRST + 4 * EXTRA
THIRD = ROWS * (SECOND - EXTRA)
POOL = 2 * CORE + THIRD
PARTS = 14
HALF = 512
SHARE = 32
PACKED = HALF + HALF // SHARE
VMEM_GRANT = 10 * 1024 * 1024


def route_kernel(slots_dev, me_ref, slot_ref, out_ref):
    base = me_ref[0] * slots_dev
    slot = slot_ref[...]
    rows = slot.shape[0]
    per = rows // COLS
    local = slot - base
    mine = jnp.logical_and(local >= 0, local < slots_dev)
    ones = jnp.where(mine, 1.0, 0.0).astype(jnp.bfloat16)
    r = lax.broadcasted_iota(jnp.int32, (128, 128), 0)
    c = lax.broadcasted_iota(jnp.int32, (128, 128), 1)
    before = jnp.where(r < c, 1.0, 0.0).astype(jnp.bfloat16)
    within = jnp.dot(ones, before, preferred_element_type=jnp.float32)
    r = lax.broadcasted_iota(jnp.int32, (rows, rows), 0)
    c = lax.broadcasted_iota(jnp.int32, (rows, rows), 1)
    above = jnp.where(jnp.logical_and(r // per == c // per, c < r), 1.0, 0.0).astype(jnp.bfloat16)
    upto = jnp.dot(above, ones, preferred_element_type=jnp.float32)
    rank = within + jnp.sum(upto, axis=1, keepdims=True)
    rank = jnp.where(mine, rank, -1.0).reshape(COLS, per, 128)
    parity = lax.broadcasted_iota(jnp.int32, (rows, 128), 1) % 2
    local = jnp.where(mine, 2 * local + parity, 0).astype(jnp.float32).reshape(COLS, per, 128)
    lane = lax.broadcasted_iota(jnp.int32, (COLS, 128), 1)
    out = jnp.zeros((COLS, 128), jnp.float32)
    for j in range(CAP):
        picked = jnp.sum(jnp.where(rank == float(j), local, 0.0), axis=1)
        out = jnp.where(lane == j, jnp.sum(picked, axis=1, keepdims=True), out)
    out_ref[...] = out.astype(jnp.int32)


def fill_kernel(index_ref, tiles_ref, first_ref, second_ref, first_filled, second_filled, sems):
    copies = []
    for k, (filled, out_ref, base) in enumerate(((first_filled, first_ref, 0), (second_filled, second_ref, BATCH))):
        size = filled.shape[0] // COLS

        def group(g, carry, filled=filled, size=size, base=base):
            codes = [index_ref[g, base + j] for j in range(size)]
            tiles = [tiles_ref[code // 2] for code in codes]
            for j in range(size):
                turned = jnp.concatenate([tiles[j][:, TILE:], tiles[j][:, :TILE]], axis=1)
                filled[g * size + j] = jnp.where(codes[j] % 2 == 1, turned, tiles[j])
            return carry

        lax.fori_loop(0, COLS, group, 0)
        copies.append(pltpu.make_async_copy(filled, out_ref, sems.at[k]))
        copies[k].start()
    for copy in copies:
        copy.wait()


def compact_kernel(index_ref, spill_ref, second_ref, some_ref, rest_ref):
    def move(out_ref, base):
        def body(i, carry):
            tiles = [second_ref[index_ref[base + i * 16 + k]] for k in range(16)]
            for k in range(16):
                out_ref[i * 16 + k] = tiles[k]
            return carry

        lax.fori_loop(0, out_ref.shape[0] // 16, body, 0)

    move(some_ref, 0)

    @pl.when(spill_ref[0] > 0)
    def _():
        move(rest_ref, EXTRA)


def join_kernel(up_ref, down_ref, some_ref, up_out, down_out, sems):
    half = FIRST // 2
    copies = [
        pltpu.make_async_copy(up_ref.at[pl.ds(0, half)], up_out.at[pl.ds(0, half)], sems.at[0]),
        pltpu.make_async_copy(down_ref.at[pl.ds(half, half)], down_out.at[pl.ds(0, half)], sems.at[1]),
    ]
    for copy in copies:
        copy.start()

    def body(i, carry):
        tiles = [some_ref[i * 16 + k] for k in range(16)]
        for k in range(16):
            up_out[half + i * 16 + k] = tiles[k]
            down_out[half + i * 16 + k] = tiles[k]
        return carry

    lax.fori_loop(0, EXTRA // 16, body, 0)
    for copy in copies:
        copy.wait()


def tail_kernel(some_ref, up_ref, down_ref, out_ref):
    size = EXTRA // 2

    def body(i, carry):
        sources = [(some_ref, size), (up_ref, 0), (down_ref, 0)]
        tiles = [[ref[base + i * 8 + k] for k in range(8)] for ref, base in sources]
        for part in range(3):
            for k in range(8):
                out_ref[part * size + i * 8 + k] = tiles[part][k]
        return carry

    lax.fori_loop(0, size // 8, body, 0)


def no_spill_kernel(tiles_ref, out_ref, sem):
    copy = pltpu.make_async_copy(tiles_ref.at[pl.ds(0, 1)], out_ref.at[pl.ds(0, 1)], sem)
    copy.start()
    copy.wait()


def no_spill_call(tiles):
    return pl.pallas_call(
        no_spill_kernel,
        in_specs=[pl.BlockSpec(memory_space=pl.ANY)],
        out_specs=pl.BlockSpec(memory_space=pl.ANY),
        out_shape=jax.ShapeDtypeStruct((THIRD, SUB, 128), jnp.bfloat16),
        scratch_shapes=[pltpu.SemaphoreType.DMA],
        compiler_params=pltpu.CompilerParams(vmem_limit_bytes=VMEM_GRANT),
        name="no_spill",
    )(tiles)


def prep_kernel(mask_ref, amp_ref, even_ref, odd_ref):
    blk = pl.program_id(0)
    rows = amp_ref.shape[0]
    r = lax.broadcasted_iota(jnp.int32, (256, 256), 0)
    c = lax.broadcasted_iota(jnp.int32, (256, 256), 1)
    source = (c % 128 // SUB) * TILE + 2 * (c % SUB) + c // 128
    shuffle = jnp.where(r == source, 1.0, 0.0).astype(jnp.bfloat16)
    moved = jnp.dot(amp_ref[...], shuffle, preferred_element_type=jnp.float32)
    mask = mask_ref[...].astype(jnp.bfloat16)
    r = lax.broadcasted_iota(jnp.int32, (mask.shape[1], 128), 0)
    c = lax.broadcasted_iota(jnp.int32, (mask.shape[1], 128), 1)
    spread = jnp.where(r == 4 * blk + c // SUB, 1.0, 0.0).astype(jnp.bfloat16)
    wide = jnp.dot(mask, spread, preferred_element_type=jnp.float32).astype(jnp.bfloat16)
    r = lax.broadcasted_iota(jnp.int32, (rows, mask.shape[0]), 0)
    c = lax.broadcasted_iota(jnp.int32, (rows, mask.shape[0]), 1)
    tall = jnp.where(r // TILE == c, 1.0, 0.0).astype(jnp.bfloat16)
    full = jnp.dot(tall, wide, preferred_element_type=jnp.float32)
    even_ref[...] = (moved[:, :128] * full).astype(jnp.bfloat16)
    odd_ref[...] = (moved[:, 128:] * full).astype(jnp.bfloat16)


def pack(out_ref, value):
    value = value.reshape(HALF // SHARE, SHARE, 128)
    top = jnp.maximum(jnp.max(jnp.abs(value), axis=1), 1e-30)
    exponent = jnp.ceil(jnp.log2(top * 1.0001))
    scaled = jnp.round(value * jnp.exp2(15.0 - exponent)[:, None, :]).reshape(HALF, 128)
    out_ref[pl.ds(0, HALF)] = scaled.astype(jnp.int32).astype(jnp.int16)
    out_ref[pl.ds(HALF, HALF // SHARE)] = exponent.astype(jnp.int32).astype(jnp.int16)


def unpack(ref):
    mantissa = ref[pl.ds(0, HALF)].astype(jnp.int32).astype(jnp.float32)
    exponent = ref[pl.ds(HALF, HALF // SHARE)].astype(jnp.int32).astype(jnp.float32)
    value = mantissa.reshape(HALF // SHARE, SHARE, 128) * jnp.exp2(exponent - 15.0)[:, None, :]
    return value.reshape(HALF, 128)


def collect_kernel(misc_ref, *refs):
    parts, third_ref, tiles, sems = refs[:PARTS], refs[PARTS], refs[PARTS + 1], refs[PARTS + 2]
    copies, base = [], 0
    for k, part in enumerate(parts):
        size = part.shape[0]
        copies.append(pltpu.make_async_copy(part, tiles.at[pl.ds(base, size)], sems.at[k]))
        base += size
    for copy in copies:
        copy.start()
    tiles[pl.ds(POOL, 1)] = jnp.zeros((1, SUB, 128), jnp.bfloat16)

    @pl.when(misc_ref[2] > 0)
    def _():
        copy = pltpu.make_async_copy(third_ref, tiles.at[pl.ds(base, THIRD)], sems.at[PARTS])
        copy.start()
        copy.wait()

    for copy in copies:
        copy.wait()


def collect_call(misc, parts, third):
    return pl.pallas_call(
        collect_kernel,
        in_specs=[pl.BlockSpec(memory_space=pltpu.SMEM)] + [pl.BlockSpec(memory_space=pl.ANY)] * (PARTS + 1),
        out_specs=pl.BlockSpec(memory_space=pltpu.VMEM),
        out_shape=jax.ShapeDtypeStruct((POOL + 1, SUB, 128), jnp.bfloat16),
        scratch_shapes=[pltpu.SemaphoreType.DMA((PARTS + 1,))],
        compiler_params=pltpu.CompilerParams(vmem_limit_bytes=2 * 1024 * 1024),
        cost_estimate=pl.CostEstimate(flops=0, bytes_accessed=POOL * 8192, transcendentals=0),
        name="collect",
    )(misc, *parts, third)


def build(hop, unit, index_ref, misc_ref, tiles, weight):
    at = [((misc_ref[0] + hop) % 4 * 4 + unit) * 4, (unit * 4 + (misc_ref[1] + hop) % 4) * 4 + 2]
    left = lax.broadcasted_iota(jnp.int32, (SUB, 128), 1) < TILE
    for kb in range(KB):
        picked = [tiles[index_ref[kb * NB + at[pair] + k]] for pair in range(2) for k in range(2)]
        rows = slice(kb * SUB, (kb + 1) * SUB)
        for pair in range(2):
            one, two = picked[2 * pair : 2 * pair + 2]
            columns = slice(128 * pair, 128 * pair + 128)
            weight[0][rows, columns] = jnp.where(left, one, two)
            weight[1][rows, columns] = jnp.where(left, two, one)


def product_kernel(hops, index_ref, misc_ref, even_ref, odd_ref, tiles, *refs):
    outs, weights = refs[:-4], (refs[-4:-2], refs[-2:])
    build(hops[0], 0, index_ref, misc_ref, tiles, weights[0])

    def emit(at, unit, weight):
        straight = jnp.dot(even_ref[...], weight[0][...], preferred_element_type=jnp.float32)
        crossed = jnp.dot(odd_ref[...], weight[1][...], preferred_element_type=jnp.float32)
        for way in range(2):
            columns = slice(way * 128, way * 128 + 128)
            value = straight[:, columns] + pltpu.roll(crossed[:, columns], TILE, 1)
            if hops == (0,):
                outs[way][unit] = value
                continue
            for half in range(2):
                out_ref = outs[2 * way + half] if len(hops) == 1 else outs[2 * way + at].at[half]
                pack(out_ref.at[unit], value[half * HALF : (half + 1) * HALF])

    for at, hop in enumerate(hops):
        after = hops[min(at + 1, len(hops) - 1)]

        def two_units(i, carry, at=at, hop=hop, after=after):
            build(hop, 2 * i + 1, index_ref, misc_ref, tiles, weights[1])
            emit(at, 2 * i, weights[0])
            build(jnp.where(i == 0, hop, after), 2 - 2 * i, index_ref, misc_ref, tiles, weights[0])
            emit(at, 2 * i + 1, weights[1])
            return carry

        lax.fori_loop(0, 2, two_units, 0)


def product_call(name, hops, scalars, arrays):
    rows_dev, depth_half = arrays[0].shape
    vmem = pl.BlockSpec(memory_space=pltpu.VMEM)
    if hops == (0,):
        outs = [jax.ShapeDtypeStruct((4, rows_dev, 128), jnp.float32)] * 2
    elif len(hops) == 1:
        outs = [jax.ShapeDtypeStruct((4, PACKED, 128), jnp.int16)] * 4
    else:
        outs = [jax.ShapeDtypeStruct((2, 4, PACKED, 128), jnp.int16)] * 4
    handed = [] if hops == (0,) else [jax.ShapeDtypeStruct(a.shape, a.dtype) for a in arrays]
    result = pl.pallas_call(
        functools.partial(product_kernel, hops),
        grid_spec=pltpu.PrefetchScalarGridSpec(
            num_scalar_prefetch=2,
            grid=(),
            in_specs=[vmem] * 3,
            out_specs=[vmem] * (len(outs) + len(handed)),
            scratch_shapes=[pltpu.VMEM((depth_half, 256), jnp.bfloat16)] * 4,
        ),
        out_shape=outs + handed,
        input_output_aliases={2 + k: len(outs) + k for k in range(len(handed))},
        compiler_params=pltpu.CompilerParams(vmem_limit_bytes=VMEM_GRANT),
        cost_estimate=pl.CostEstimate(
            flops=8 * len(hops) * rows_dev * depth_half * 512, bytes_accessed=POOL * 8192, transcendentals=0
        ),
        name=name,
    )(*scalars, *arrays)
    return result[: len(outs)], result[len(outs) :]


def ahead(axis, value):
    return lax.ppermute(value, axis, [(i, (i + 1) % 4) for i in range(4)])


def behind(axis, value):
    return lax.ppermute(value, axis, [(i, (i + 3) % 4) for i in range(4)])


def reach(tiles):
    return ahead("y", tiles), behind("y", tiles)


def swap(parts):
    return [lax.ppermute(part, "core", [(0, 1), (1, 0)]) for part in parts]


def add_first_kernel(*refs):
    def body(i, carry):
        for way in range(2):
            ahead_in, behind_in, came_a, came_b = refs[4 * way : 4 * way + 4]
            ahead_out, behind_out = refs[8 + 2 * way : 10 + 2 * way]
            pack(ahead_out.at[0, i], unpack(ahead_in.at[0, i]) + unpack(came_a.at[i]))
            ahead_out[1, i] = ahead_in[1, i]
            behind_out[0, i] = behind_in[0, i]
            pack(behind_out.at[1, i], unpack(behind_in.at[1, i]) + unpack(came_b.at[i]))
        return carry

    lax.fori_loop(0, 4, body, 0)


def whole_call(body, name, outs, *arrays, scalars=()):
    vmem = pl.BlockSpec(memory_space=pltpu.VMEM)
    size = sum(a.size * a.dtype.itemsize for a in [*arrays, *outs])
    return pl.pallas_call(
        body,
        in_specs=[pl.BlockSpec(memory_space=pltpu.SMEM)] * len(scalars) + [vmem] * len(arrays),
        out_specs=[vmem] * len(outs),
        out_shape=outs,
        compiler_params=pltpu.CompilerParams(vmem_limit_bytes=VMEM_GRANT),
        cost_estimate=pl.CostEstimate(flops=10 * size, bytes_accessed=size, transcendentals=0),
        name=name,
    )(*scalars, *arrays)


def middle_kernel(misc_ref, one_ref, two_ref, *refs):
    came, outs, own_ref = refs[:4], refs[4:10], refs[10]
    for way, own in enumerate((one_ref, two_ref)):
        right, left = came[2 * way : 2 * way + 2]
        for hop, ahead_by in enumerate((2, 1, 3, 0)):
            at = (misc_ref[1 - way] + ahead_by) % 4
            total = [
                own[at, pl.ds(half * HALF, HALF)] + unpack(right.at[half, at]) + unpack(left.at[half, at])
                for half in range(2)
            ]
            for half in range(2):
                if hop < 3:
                    pack(outs[3 * way + hop].at[half], total[half])
                else:
                    own_ref[pl.ds(half * HALF, HALF), pl.ds(way * 128, 128)] = total[half]


def last_kernel(own_ref, *refs):
    came, out_ref = refs[:6], refs[6]
    for way in range(2):
        columns = pl.ds(way * 128, 128)
        for half in range(2):
            rows = pl.ds(half * HALF, HALF)
            total = own_ref[rows, columns]
            for ref in ((came[0], came[1], came[3]), (came[2], came[4], came[5]))[way]:
                total += unpack(ref.at[half])
            out_ref[columns, rows] = total.T


def shards(amplitudes, t2_mask, eri_tiles, eri_slot):
    y, core, x, z = (lax.axis_index(name) for name in ("y", "core", "x", "z"))
    group = x * 4 + z
    myself = (y * 2 + core) * COLS + group
    rows_dev, depth_dev = amplitudes.shape
    slots_dev = eri_tiles.shape[0]

    send_index = pl.pallas_call(
        lambda *refs: route_kernel(slots_dev, *refs),
        out_shape=jax.ShapeDtypeStruct((COLS, 128), jnp.int32),
        in_specs=[
            pl.BlockSpec(memory_space=pltpu.SMEM),
            pl.BlockSpec(memory_space=pltpu.VMEM),
        ],
        out_specs=pl.BlockSpec(memory_space=pltpu.VMEM),
        compiler_params=pltpu.CompilerParams(vmem_limit_bytes=VMEM_GRANT),
        name="route",
    )(myself.reshape(1).astype(jnp.int32), eri_slot.reshape(-1, 128))
    vmem = pl.BlockSpec(memory_space=pltpu.VMEM)
    outgoing = pl.pallas_call(
        fill_kernel,
        grid_spec=pltpu.PrefetchScalarGridSpec(
            num_scalar_prefetch=1,
            grid=(),
            in_specs=[vmem],
            out_specs=[pl.BlockSpec(memory_space=pltpu.HBM)] * 2,
            scratch_shapes=[
                pltpu.VMEM((FIRST, SUB, 128), jnp.bfloat16),
                pltpu.VMEM((SECOND, SUB, 128), jnp.bfloat16),
                pltpu.SemaphoreType.DMA((2,)),
            ],
        ),
        out_shape=[jax.ShapeDtypeStruct((size, SUB, 128), jnp.bfloat16) for size in (FIRST, SECOND)],
        compiler_params=pltpu.CompilerParams(vmem_limit_bytes=VMEM_GRANT),
        name="fill",
    )(send_index, eri_tiles.reshape(slots_dev, SUB, 128))

    def send(part):
        part = part.reshape(COLS, -1, SUB, 128)
        part = lax.all_to_all(part, ("x", "z"), split_axis=0, concat_axis=0, tiled=True)
        return part.reshape(-1, SUB, 128)

    first = send(outgoing[0])
    first, second, eri_slot = lax.optimization_barrier((first, outgoing[1], eri_slot))
    up, down = reach(first)
    second = send(second)
    devices = jnp.arange(DEVS, dtype=jnp.int32)
    owner_all = jnp.where(eri_slot >= 0, eri_slot // slots_dev, -1).reshape(COLS, 1, GROUP)
    held = jnp.sum((owner_all == devices[None, :, None]).astype(jnp.int32), axis=2)
    tail = jnp.maximum(held - BATCH, 0).reshape(COLS, ROWS, COLS)
    spill = jnp.any(jnp.sum(tail, axis=2) > EXTRA)
    tail = lax.dynamic_index_in_dim(tail, group, 0, keepdims=False)
    upto = jnp.sum(jnp.where(jnp.arange(COLS)[:, None] >= jnp.arange(COLS)[None, :], tail[:, None, :], 0), axis=2)
    start = upto - tail
    mine_upto = lax.dynamic_index_in_dim(upto, y * 2 + core, 0, keepdims=False)
    mine_start = lax.dynamic_index_in_dim(start, y * 2 + core, 0, keepdims=False)
    spot = jnp.arange(SECOND, dtype=jnp.int32)
    inside = jnp.logical_and(spot[:, None] >= mine_start[None, :], spot[:, None] < mine_upto[None, :])
    source = jnp.arange(COLS, dtype=jnp.int32)[None, :] * (CAP - BATCH) + spot[:, None] - mine_start[None, :]
    source = jnp.sum(jnp.where(inside, source, 0), axis=1).astype(jnp.int32)
    spill = spill.astype(jnp.int32).reshape(1)
    second, source, spill = lax.optimization_barrier((second, source, spill))
    half = FIRST // 2
    some, rest = pl.pallas_call(
        compact_kernel,
        grid_spec=pltpu.PrefetchScalarGridSpec(
            num_scalar_prefetch=2, grid=(), in_specs=[vmem], out_specs=[vmem] * 2
        ),
        out_shape=[jax.ShapeDtypeStruct((size, SUB, 128), jnp.bfloat16) for size in (EXTRA, SECOND - EXTRA)],
        compiler_params=pltpu.CompilerParams(vmem_limit_bytes=VMEM_GRANT),
        name="compact",
    )(source, spill, second)
    some, up, down = lax.optimization_barrier((some, up, down))
    from_up, from_down = pl.pallas_call(
        join_kernel,
        in_specs=[vmem] * 3,
        out_specs=[vmem] * 2,
        out_shape=[jax.ShapeDtypeStruct((half + EXTRA, SUB, 128), jnp.bfloat16)] * 2,
        scratch_shapes=[pltpu.SemaphoreType.DMA((2,))],
        compiler_params=pltpu.CompilerParams(vmem_limit_bytes=VMEM_GRANT),
        name="join",
    )(up, down, some)
    wanted = lax.dynamic_slice_in_dim(eri_slot, group * GROUP, GROUP)
    from_up, up, down, amplitudes, wanted = lax.optimization_barrier((from_up, up, down, amplitudes, wanted))
    from_up, from_down = ahead("y", from_up), behind("y", from_down)
    swapped = swap([first, up, down])

    parted = jax.ShapeDtypeStruct((rows_dev, depth_dev // 2), jnp.bfloat16)
    even, odd = pl.pallas_call(
        prep_kernel,
        grid=(depth_dev // 256,),
        out_shape=[parted] * 2,
        in_specs=[
            pl.BlockSpec(t2_mask.shape, lambda i: (0, 0)),
            pl.BlockSpec((rows_dev, 256), lambda i: (0, i)),
        ],
        out_specs=[pl.BlockSpec((rows_dev, 128), lambda i: (0, i))] * 2,
        compiler_params=pltpu.CompilerParams(vmem_limit_bytes=VMEM_GRANT),
        name="prep",
    )(t2_mask, amplitudes)

    owner = jnp.where(wanted >= 0, wanted // slots_dev, -1)
    mine = owner[:, None] == devices[None, :]
    spot = jnp.arange(GROUP, dtype=jnp.int32)
    before = (spot[:, None] > spot[None, :]).astype(jnp.bfloat16)
    counts = jnp.dot(before, mine.astype(jnp.bfloat16), preferred_element_type=jnp.float32)
    rank = jnp.sum(jnp.where(mine, counts, 0.0), axis=1).astype(jnp.int32)
    begin = jnp.sum(jnp.where(mine, start.reshape(1, DEVS), 0), axis=1)
    behind_first = begin + rank - BATCH
    owner_row = owner // COLS
    turn = (owner_row // 2 - y) % 4
    turn = jnp.where(turn == 1, 2, jnp.where(turn == 2, 3, jnp.where(turn == 3, 1, 0)))
    size = FIRST
    slot = owner % COLS * BATCH + rank
    early = turn * size + slot + jnp.where(jnp.logical_and(turn == 3, slot >= half), EXTRA, 0)
    begins = (4 * size + 2 * EXTRA, 3 * size + half, 4 * size + EXTRA, 4 * size + 3 * EXTRA)
    late = behind_first + sum(jnp.where(turn == k, begin_late, 0) for k, begin_late in enumerate(begins))
    tile_index = jnp.where(rank < BATCH, early, late) + CORE * (owner_row % 2 != core)
    spilled = 2 * CORE + owner_row * (SECOND - EXTRA) + behind_first - EXTRA
    tile_index = jnp.where(jnp.logical_or(rank < BATCH, behind_first < EXTRA), tile_index, spilled)
    tile_index = jnp.where(wanted < 0, POOL, tile_index)
    misc = jnp.stack([x, z, spill[0]]).astype(jnp.int32)
    third = lax.cond(
        misc[2] > 0,
        lambda value: lax.all_gather(value, ("y", "core"), axis=0, tiled=True),
        no_spill_call,
        rest,
    )
    from_up, from_down, swapped, even, odd, tile_index, misc, third = lax.optimization_barrier(
        (from_up, from_down, swapped, even, odd, tile_index, misc, third)
    )
    tail_up = ahead("y", from_up[half : half + EXTRA // 2])
    tail_down = behind("y", from_down[half + EXTRA // 2 :])
    tail = jax.ShapeDtypeStruct((3 * EXTRA // 2, SUB, 128), jnp.bfloat16)
    (tail,) = whole_call(tail_kernel, "tail", [tail], some, tail_up, tail_down)
    parts = [first, up, down, from_up, from_down, some[: EXTRA // 2], tail]
    tiles = collect_call(misc, parts + swapped + swap(parts[3:]), third)

    scalars = (tile_index, misc)
    far, arrays = product_call("far", (2,), scalars, (even, odd, tiles))
    axes = ("x", "z")
    near, arrays = product_call("near", (1, 3), scalars, arrays)
    inputs = []
    for way, axis in enumerate(axes):
        inputs += [*near[2 * way : 2 * way + 2], ahead(axis, far[2 * way]), behind(axis, far[2 * way + 1])]
    packed = jax.ShapeDtypeStruct((2, 4, PACKED, 128), jnp.int16)
    added = whole_call(add_first_kernel, "add_first", [packed] * 4, *inputs)
    came = []
    for way, axis in enumerate(axes):
        came += [ahead(axis, added[2 * way]), behind(axis, added[2 * way + 1])]
    (one, two), _ = product_call("own", (0,), scalars, arrays)
    double = jax.ShapeDtypeStruct((2, PACKED, 128), jnp.int16)
    *outs, own = whole_call(
        middle_kernel,
        "middle",
        [double] * 6 + [jax.ShapeDtypeStruct((rows_dev, 256), jnp.float32)],
        one,
        two,
        *came,
        scalars=(misc,),
    )
    across_axis = [(i, (i + 2) % 4) for i in range(4)]
    came = [
        ahead("z", outs[1]),
        lax.ppermute(outs[0], "z", across_axis),
        lax.ppermute(outs[3], "x", across_axis),
        behind("z", outs[2]),
        ahead("x", outs[4]),
        behind("x", outs[5]),
    ]
    return whole_call(
        last_kernel, "last", [jax.ShapeDtypeStruct((256, rows_dev), jnp.float32)], own, *came
    )[0]


def solution(mesh):
    axes = ("y", "core", "x", "z")
    fine = Mesh(mesh.devices.reshape(4, 2, 4, 4), axes)
    row, col = ("y", "core"), ("x", "z")
    in_specs = (P(row, col), P(row, col), P(axes, None), P())
    out_specs = P(col, row)
    return jax.shard_map(shards, mesh=fine, in_specs=in_specs, out_specs=out_specs, check_vma=False)
```

```python
import functools

import jax
import jax.numpy as jnp
from jax import lax
from jax.experimental import pallas as pl
from jax.experimental.pallas import tpu as pltpu
from jax.sharding import Mesh
from jax.sharding import PartitionSpec as P

TILE = 64
VTILES = 32
KOCC = 16
JOCC = 2
CAP = 20
COLS = 16
ROWS = 8
DEVS = 128
GROUP = VTILES * KOCC * VTILES * JOCC // COLS
KB = GROUP // (VTILES * JOCC)
NB = VTILES * JOCC
SUB = TILE * TILE // 128
BATCH = 8
FIRST = COLS * BATCH
SECOND = COLS * (CAP - BATCH)
EXTRA = 80
CORE = 4 * FIRST + 4 * EXTRA
THIRD = ROWS * (SECOND - EXTRA)
POOL = 2 * CORE + THIRD
PARTS = 14
HALF = 512
SHARE = 32
PACKED = HALF + HALF // SHARE
VMEM_GRANT = 10 * 1024 * 1024


def route_kernel(slots_dev, me_ref, slot_ref, out_ref):
    base = me_ref[0] * slots_dev
    slot = slot_ref[...]
    rows = slot.shape[0]
    per = rows // COLS
    local = slot - base
    mine = jnp.logical_and(local >= 0, local < slots_dev)
    ones = jnp.where(mine, 1.0, 0.0).astype(jnp.bfloat16)
    r = lax.broadcasted_iota(jnp.int32, (128, 128), 0)
    c = lax.broadcasted_iota(jnp.int32, (128, 128), 1)
    before = jnp.where(r < c, 1.0, 0.0).astype(jnp.bfloat16)
    within = jnp.dot(ones, before, preferred_element_type=jnp.float32)
    r = lax.broadcasted_iota(jnp.int32, (rows, rows), 0)
    c = lax.broadcasted_iota(jnp.int32, (rows, rows), 1)
    above = jnp.where(jnp.logical_and(r // per == c // per, c < r), 1.0, 0.0).astype(jnp.bfloat16)
    upto = jnp.dot(above, ones, preferred_element_type=jnp.float32)
    rank = within + jnp.sum(upto, axis=1, keepdims=True)
    rank = jnp.where(mine, rank, -1.0).reshape(COLS, per, 128)
    parity = lax.broadcasted_iota(jnp.int32, (rows, 128), 1) % 2
    local = jnp.where(mine, 2 * local + parity, 0).astype(jnp.float32).reshape(COLS, per, 128)
    lane = lax.broadcasted_iota(jnp.int32, (COLS, 128), 1)
    out = jnp.zeros((COLS, 128), jnp.float32)
    for j in range(CAP):
        picked = jnp.sum(jnp.where(rank == float(j), local, 0.0), axis=1)
        out = jnp.where(lane == j, jnp.sum(picked, axis=1, keepdims=True), out)
    out_ref[...] = out.astype(jnp.int32)


def fill_kernel(base, index_ref, tiles_ref, out_ref):
    size = out_ref.shape[0] // COLS

    def group(g, carry):
        codes = [index_ref[g, base + j] for j in range(size)]
        tiles = [tiles_ref[code // 2] for code in codes]
        for j in range(size):
            turned = jnp.concatenate([tiles[j][:, TILE:], tiles[j][:, :TILE]], axis=1)
            out_ref[g * size + j] = jnp.where(codes[j] % 2 == 1, turned, tiles[j])
        return carry

    lax.fori_loop(0, COLS, group, 0)


def compact_kernel(index_ref, spill_ref, second_ref, some_ref, rest_ref):
    def move(out_ref, base):
        def body(i, carry):
            tiles = [second_ref[index_ref[base + i * 16 + k]] for k in range(16)]
            for k in range(16):
                out_ref[i * 16 + k] = tiles[k]
            return carry

        lax.fori_loop(0, out_ref.shape[0] // 16, body, 0)

    move(some_ref, 0)

    @pl.when(spill_ref[0] > 0)
    def _():
        move(rest_ref, EXTRA)


def join_kernel(up_ref, down_ref, some_ref, up_out, down_out, sems):
    half = FIRST // 2
    copies = [
        pltpu.make_async_copy(up_ref.at[pl.ds(0, half)], up_out.at[pl.ds(0, half)], sems.at[0]),
        pltpu.make_async_copy(down_ref.at[pl.ds(half, half)], down_out.at[pl.ds(0, half)], sems.at[1]),
    ]
    for copy in copies:
        copy.start()

    def body(i, carry):
        tiles = [some_ref[i * 16 + k] for k in range(16)]
        for k in range(16):
            up_out[half + i * 16 + k] = tiles[k]
            down_out[half + i * 16 + k] = tiles[k]
        return carry

    lax.fori_loop(0, EXTRA // 16, body, 0)
    for copy in copies:
        copy.wait()


def tail_kernel(some_ref, up_ref, down_ref, out_ref):
    size = EXTRA // 2

    def body(i, carry):
        sources = [(some_ref, size), (up_ref, 0), (down_ref, 0)]
        tiles = [[ref[base + i * 8 + k] for k in range(8)] for ref, base in sources]
        for part in range(3):
            for k in range(8):
                out_ref[part * size + i * 8 + k] = tiles[part][k]
        return carry

    lax.fori_loop(0, size // 8, body, 0)


def no_spill_kernel(tiles_ref, out_ref, sem):
    copy = pltpu.make_async_copy(tiles_ref.at[pl.ds(0, 1)], out_ref.at[pl.ds(0, 1)], sem)
    copy.start()
    copy.wait()


def no_spill_call(tiles):
    return pl.pallas_call(
        no_spill_kernel,
        in_specs=[pl.BlockSpec(memory_space=pl.ANY)],
        out_specs=pl.BlockSpec(memory_space=pl.ANY),
        out_shape=jax.ShapeDtypeStruct((THIRD, SUB, 128), jnp.bfloat16),
        scratch_shapes=[pltpu.SemaphoreType.DMA],
        compiler_params=pltpu.CompilerParams(vmem_limit_bytes=VMEM_GRANT),
        name="no_spill",
    )(tiles)


def prep_kernel(mask_ref, amp_ref, even_ref, odd_ref):
    blk = pl.program_id(0)
    rows = amp_ref.shape[0]
    r = lax.broadcasted_iota(jnp.int32, (256, 256), 0)
    c = lax.broadcasted_iota(jnp.int32, (256, 256), 1)
    source = (c % 128 // SUB) * TILE + 2 * (c % SUB) + c // 128
    shuffle = jnp.where(r == source, 1.0, 0.0).astype(jnp.bfloat16)
    moved = jnp.dot(amp_ref[...], shuffle, preferred_element_type=jnp.float32)
    mask = mask_ref[...].astype(jnp.bfloat16)
    r = lax.broadcasted_iota(jnp.int32, (mask.shape[1], 128), 0)
    c = lax.broadcasted_iota(jnp.int32, (mask.shape[1], 128), 1)
    spread = jnp.where(r == 4 * blk + c // SUB, 1.0, 0.0).astype(jnp.bfloat16)
    wide = jnp.dot(mask, spread, preferred_element_type=jnp.float32).astype(jnp.bfloat16)
    r = lax.broadcasted_iota(jnp.int32, (rows, mask.shape[0]), 0)
    c = lax.broadcasted_iota(jnp.int32, (rows, mask.shape[0]), 1)
    tall = jnp.where(r // TILE == c, 1.0, 0.0).astype(jnp.bfloat16)
    full = jnp.dot(tall, wide, preferred_element_type=jnp.float32)
    even_ref[...] = (moved[:, :128] * full).astype(jnp.bfloat16)
    odd_ref[...] = (moved[:, 128:] * full).astype(jnp.bfloat16)


def pack(out_ref, value):
    value = value.reshape(HALF // SHARE, SHARE, 128)
    top = jnp.maximum(jnp.max(jnp.abs(value), axis=1), 1e-30)
    exponent = jnp.ceil(jnp.log2(top * 1.0001))
    scaled = jnp.round(value * jnp.exp2(15.0 - exponent)[:, None, :]).reshape(HALF, 128)
    out_ref[pl.ds(0, HALF)] = scaled.astype(jnp.int32).astype(jnp.int16)
    out_ref[pl.ds(HALF, HALF // SHARE)] = exponent.astype(jnp.int32).astype(jnp.int16)


def unpack(ref):
    mantissa = ref[pl.ds(0, HALF)].astype(jnp.int32).astype(jnp.float32)
    exponent = ref[pl.ds(HALF, HALF // SHARE)].astype(jnp.int32).astype(jnp.float32)
    value = mantissa.reshape(HALF // SHARE, SHARE, 128) * jnp.exp2(exponent - 15.0)[:, None, :]
    return value.reshape(HALF, 128)


def collect_kernel(misc_ref, *refs):
    parts, third_ref, tiles, sems = refs[:PARTS], refs[PARTS], refs[PARTS + 1], refs[PARTS + 2]
    copies, base = [], 0
    for k, part in enumerate(parts):
        size = part.shape[0]
        copies.append(pltpu.make_async_copy(part, tiles.at[pl.ds(base, size)], sems.at[k]))
        base += size
    for copy in copies:
        copy.start()
    tiles[pl.ds(POOL, 1)] = jnp.zeros((1, SUB, 128), jnp.bfloat16)

    @pl.when(misc_ref[2] > 0)
    def _():
        copy = pltpu.make_async_copy(third_ref, tiles.at[pl.ds(base, THIRD)], sems.at[PARTS])
        copy.start()
        copy.wait()

    for copy in copies:
        copy.wait()


def collect_call(misc, parts, third):
    return pl.pallas_call(
        collect_kernel,
        in_specs=[pl.BlockSpec(memory_space=pltpu.SMEM)] + [pl.BlockSpec(memory_space=pl.ANY)] * (PARTS + 1),
        out_specs=pl.BlockSpec(memory_space=pltpu.VMEM),
        out_shape=jax.ShapeDtypeStruct((POOL + 1, SUB, 128), jnp.bfloat16),
        scratch_shapes=[pltpu.SemaphoreType.DMA((PARTS + 1,))],
        compiler_params=pltpu.CompilerParams(vmem_limit_bytes=2 * 1024 * 1024),
        cost_estimate=pl.CostEstimate(flops=0, bytes_accessed=POOL * 8192, transcendentals=0),
        name="collect",
    )(misc, *parts, third)


def build(hop, unit, index_ref, misc_ref, tiles, weight):
    at = [((misc_ref[0] + hop) % 4 * 4 + unit) * 4, (unit * 4 + (misc_ref[1] + hop) % 4) * 4 + 2]
    left = lax.broadcasted_iota(jnp.int32, (SUB, 128), 1) < TILE
    for kb in range(KB):
        picked = [tiles[index_ref[kb * NB + at[pair] + k]] for pair in range(2) for k in range(2)]
        rows = slice(kb * SUB, (kb + 1) * SUB)
        for pair in range(2):
            one, two = picked[2 * pair : 2 * pair + 2]
            columns = slice(128 * pair, 128 * pair + 128)
            weight[0][rows, columns] = jnp.where(left, one, two)
            weight[1][rows, columns] = jnp.where(left, two, one)


def product_kernel(hops, index_ref, misc_ref, even_ref, odd_ref, tiles, *refs):
    outs, weights = refs[:-4], (refs[-4:-2], refs[-2:])
    build(hops[0], 0, index_ref, misc_ref, tiles, weights[0])

    def emit(at, unit, weight):
        straight = jnp.dot(even_ref[...], weight[0][...], preferred_element_type=jnp.float32)
        crossed = jnp.dot(odd_ref[...], weight[1][...], preferred_element_type=jnp.float32)
        for way in range(2):
            columns = slice(way * 128, way * 128 + 128)
            value = straight[:, columns] + pltpu.roll(crossed[:, columns], TILE, 1)
            if hops == (0,):
                outs[way][unit] = value
                continue
            for half in range(2):
                out_ref = outs[2 * way + half] if len(hops) == 1 else outs[2 * way + at].at[half]
                pack(out_ref.at[unit], value[half * HALF : (half + 1) * HALF])

    for at, hop in enumerate(hops):
        after = hops[min(at + 1, len(hops) - 1)]

        def two_units(i, carry, at=at, hop=hop, after=after):
            build(hop, 2 * i + 1, index_ref, misc_ref, tiles, weights[1])
            emit(at, 2 * i, weights[0])
            build(jnp.where(i == 0, hop, after), 2 - 2 * i, index_ref, misc_ref, tiles, weights[0])
            emit(at, 2 * i + 1, weights[1])
            return carry

        lax.fori_loop(0, 2, two_units, 0)


def product_call(name, hops, scalars, arrays):
    rows_dev, depth_half = arrays[0].shape
    vmem = pl.BlockSpec(memory_space=pltpu.VMEM)
    if hops == (0,):
        outs = [jax.ShapeDtypeStruct((4, rows_dev, 128), jnp.float32)] * 2
    elif len(hops) == 1:
        outs = [jax.ShapeDtypeStruct((4, PACKED, 128), jnp.int16)] * 4
    else:
        outs = [jax.ShapeDtypeStruct((2, 4, PACKED, 128), jnp.int16)] * 4
    handed = [] if hops == (0,) else [jax.ShapeDtypeStruct(a.shape, a.dtype) for a in arrays]
    result = pl.pallas_call(
        functools.partial(product_kernel, hops),
        grid_spec=pltpu.PrefetchScalarGridSpec(
            num_scalar_prefetch=2,
            grid=(),
            in_specs=[vmem] * 3,
            out_specs=[vmem] * (len(outs) + len(handed)),
            scratch_shapes=[pltpu.VMEM((depth_half, 256), jnp.bfloat16)] * 4,
        ),
        out_shape=outs + handed,
        input_output_aliases={2 + k: len(outs) + k for k in range(len(handed))},
        compiler_params=pltpu.CompilerParams(vmem_limit_bytes=VMEM_GRANT),
        cost_estimate=pl.CostEstimate(
            flops=8 * len(hops) * rows_dev * depth_half * 512, bytes_accessed=POOL * 8192, transcendentals=0
        ),
        name=name,
    )(*scalars, *arrays)
    return result[: len(outs)], result[len(outs) :]


def ahead(axis, value):
    return lax.ppermute(value, axis, [(i, (i + 1) % 4) for i in range(4)])


def behind(axis, value):
    return lax.ppermute(value, axis, [(i, (i + 3) % 4) for i in range(4)])


def reach(tiles):
    return ahead("y", tiles), behind("y", tiles)


def swap(parts):
    return [lax.ppermute(part, "core", [(0, 1), (1, 0)]) for part in parts]


def add_first_kernel(*refs):
    def body(i, carry):
        for way in range(2):
            ahead_in, behind_in, came_a, came_b = refs[4 * way : 4 * way + 4]
            ahead_out, behind_out = refs[8 + 2 * way : 10 + 2 * way]
            pack(ahead_out.at[0, i], unpack(ahead_in.at[0, i]) + unpack(came_a.at[i]))
            ahead_out[1, i] = ahead_in[1, i]
            behind_out[0, i] = behind_in[0, i]
            pack(behind_out.at[1, i], unpack(behind_in.at[1, i]) + unpack(came_b.at[i]))
        return carry

    lax.fori_loop(0, 4, body, 0)


def whole_call(body, name, outs, *arrays, scalars=()):
    vmem = pl.BlockSpec(memory_space=pltpu.VMEM)
    size = sum(a.size * a.dtype.itemsize for a in [*arrays, *outs])
    return pl.pallas_call(
        body,
        in_specs=[pl.BlockSpec(memory_space=pltpu.SMEM)] * len(scalars) + [vmem] * len(arrays),
        out_specs=[vmem] * len(outs),
        out_shape=outs,
        compiler_params=pltpu.CompilerParams(vmem_limit_bytes=VMEM_GRANT),
        cost_estimate=pl.CostEstimate(flops=10 * size, bytes_accessed=size, transcendentals=0),
        name=name,
    )(*scalars, *arrays)


def middle_kernel(misc_ref, one_ref, two_ref, *refs):
    came, outs, own_ref = refs[:4], refs[4:10], refs[10]
    for way, own in enumerate((one_ref, two_ref)):
        right, left = came[2 * way : 2 * way + 2]
        for hop, ahead_by in enumerate((2, 1, 3, 0)):
            at = (misc_ref[1 - way] + ahead_by) % 4
            total = [
                own[at, pl.ds(half * HALF, HALF)] + unpack(right.at[half, at]) + unpack(left.at[half, at])
                for half in range(2)
            ]
            for half in range(2):
                if hop < 3:
                    pack(outs[3 * way + hop].at[half], total[half])
                else:
                    own_ref[pl.ds(half * HALF, HALF), pl.ds(way * 128, 128)] = total[half]


def last_kernel(own_ref, *refs):
    came, out_ref = refs[:6], refs[6]
    for way in range(2):
        columns = pl.ds(way * 128, 128)
        for half in range(2):
            rows = pl.ds(half * HALF, HALF)
            total = own_ref[rows, columns]
            for ref in ((came[0], came[1], came[3]), (came[2], came[4], came[5]))[way]:
                total += unpack(ref.at[half])
            out_ref[columns, rows] = total.T


def shards(amplitudes, t2_mask, eri_tiles, eri_slot):
    y, core, x, z = (lax.axis_index(name) for name in ("y", "core", "x", "z"))
    group = x * 4 + z
    myself = (y * 2 + core) * COLS + group
    rows_dev, depth_dev = amplitudes.shape
    slots_dev = eri_tiles.shape[0]

    send_index = pl.pallas_call(
        lambda *refs: route_kernel(slots_dev, *refs),
        out_shape=jax.ShapeDtypeStruct((COLS, 128), jnp.int32),
        in_specs=[
            pl.BlockSpec(memory_space=pltpu.SMEM),
            pl.BlockSpec(memory_space=pltpu.VMEM),
        ],
        out_specs=pl.BlockSpec(memory_space=pltpu.VMEM),
        compiler_params=pltpu.CompilerParams(vmem_limit_bytes=VMEM_GRANT),
        name="route",
    )(myself.reshape(1).astype(jnp.int32), eri_slot.reshape(-1, 128))
    vmem = pl.BlockSpec(memory_space=pltpu.VMEM)
    stored = eri_tiles.reshape(slots_dev, SUB, 128)

    def fill(base, size):
        return pl.pallas_call(
            functools.partial(fill_kernel, base),
            grid_spec=pltpu.PrefetchScalarGridSpec(
                num_scalar_prefetch=1, grid=(), in_specs=[vmem], out_specs=vmem
            ),
            out_shape=jax.ShapeDtypeStruct((size, SUB, 128), jnp.bfloat16),
            compiler_params=pltpu.CompilerParams(vmem_limit_bytes=VMEM_GRANT),
            name="fill",
        )(send_index, stored)

    outgoing = fill(0, FIRST), fill(BATCH, SECOND)

    def send(part):
        part = part.reshape(COLS, -1, SUB, 128)
        part = lax.all_to_all(part, ("x", "z"), split_axis=0, concat_axis=0, tiled=True)
        return part.reshape(-1, SUB, 128)

    first = send(outgoing[0])
    first, second, eri_slot = lax.optimization_barrier((first, outgoing[1], eri_slot))
    up, down = reach(first)
    second = send(second)
    devices = jnp.arange(DEVS, dtype=jnp.int32)
    owner_all = jnp.where(eri_slot >= 0, eri_slot // slots_dev, -1).reshape(COLS, 1, GROUP)
    held = jnp.sum((owner_all == devices[None, :, None]).astype(jnp.int32), axis=2)
    tail = jnp.maximum(held - BATCH, 0).reshape(COLS, ROWS, COLS)
    spill = jnp.any(jnp.sum(tail, axis=2) > EXTRA)
    tail = lax.dynamic_index_in_dim(tail, group, 0, keepdims=False)
    upto = jnp.sum(jnp.where(jnp.arange(COLS)[:, None] >= jnp.arange(COLS)[None, :], tail[:, None, :], 0), axis=2)
    start = upto - tail
    mine_upto = lax.dynamic_index_in_dim(upto, y * 2 + core, 0, keepdims=False)
    mine_start = lax.dynamic_index_in_dim(start, y * 2 + core, 0, keepdims=False)
    spot = jnp.arange(SECOND, dtype=jnp.int32)
    inside = jnp.logical_and(spot[:, None] >= mine_start[None, :], spot[:, None] < mine_upto[None, :])
    source = jnp.arange(COLS, dtype=jnp.int32)[None, :] * (CAP - BATCH) + spot[:, None] - mine_start[None, :]
    source = jnp.sum(jnp.where(inside, source, 0), axis=1).astype(jnp.int32)
    spill = spill.astype(jnp.int32).reshape(1)
    second, source, spill = lax.optimization_barrier((second, source, spill))
    half = FIRST // 2
    some, rest = pl.pallas_call(
        compact_kernel,
        grid_spec=pltpu.PrefetchScalarGridSpec(
            num_scalar_prefetch=2, grid=(), in_specs=[vmem], out_specs=[vmem] * 2
        ),
        out_shape=[jax.ShapeDtypeStruct((size, SUB, 128), jnp.bfloat16) for size in (EXTRA, SECOND - EXTRA)],
        compiler_params=pltpu.CompilerParams(vmem_limit_bytes=VMEM_GRANT),
        name="compact",
    )(source, spill, second)
    some, up, down = lax.optimization_barrier((some, up, down))
    from_up, from_down = pl.pallas_call(
        join_kernel,
        in_specs=[vmem] * 3,
        out_specs=[vmem] * 2,
        out_shape=[jax.ShapeDtypeStruct((half + EXTRA, SUB, 128), jnp.bfloat16)] * 2,
        scratch_shapes=[pltpu.SemaphoreType.DMA((2,))],
        compiler_params=pltpu.CompilerParams(vmem_limit_bytes=VMEM_GRANT),
        name="join",
    )(up, down, some)
    wanted = lax.dynamic_slice_in_dim(eri_slot, group * GROUP, GROUP)
    from_up, up, down, amplitudes, wanted = lax.optimization_barrier((from_up, up, down, amplitudes, wanted))
    from_up, from_down = ahead("y", from_up), behind("y", from_down)
    swapped = swap([first, up, down])

    parted = jax.ShapeDtypeStruct((rows_dev, depth_dev // 2), jnp.bfloat16)
    even, odd = pl.pallas_call(
        prep_kernel,
        grid=(depth_dev // 256,),
        out_shape=[parted] * 2,
        in_specs=[
            pl.BlockSpec(t2_mask.shape, lambda i: (0, 0)),
            pl.BlockSpec((rows_dev, 256), lambda i: (0, i)),
        ],
        out_specs=[pl.BlockSpec((rows_dev, 128), lambda i: (0, i))] * 2,
        compiler_params=pltpu.CompilerParams(vmem_limit_bytes=VMEM_GRANT),
        name="prep",
    )(t2_mask, amplitudes)

    owner = jnp.where(wanted >= 0, wanted // slots_dev, -1)
    mine = owner[:, None] == devices[None, :]
    spot = jnp.arange(GROUP, dtype=jnp.int32)
    before = (spot[:, None] > spot[None, :]).astype(jnp.bfloat16)
    counts = jnp.dot(before, mine.astype(jnp.bfloat16), preferred_element_type=jnp.float32)
    rank = jnp.sum(jnp.where(mine, counts, 0.0), axis=1).astype(jnp.int32)
    begin = jnp.sum(jnp.where(mine, start.reshape(1, DEVS), 0), axis=1)
    behind_first = begin + rank - BATCH
    owner_row = owner // COLS
    turn = (owner_row // 2 - y) % 4
    turn = jnp.where(turn == 1, 2, jnp.where(turn == 2, 3, jnp.where(turn == 3, 1, 0)))
    size = FIRST
    slot = owner % COLS * BATCH + rank
    early = turn * size + slot + jnp.where(jnp.logical_and(turn == 3, slot >= half), EXTRA, 0)
    begins = (4 * size + 2 * EXTRA, 3 * size + half, 4 * size + EXTRA, 4 * size + 3 * EXTRA)
    late = behind_first + sum(jnp.where(turn == k, begin_late, 0) for k, begin_late in enumerate(begins))
    tile_index = jnp.where(rank < BATCH, early, late) + CORE * (owner_row % 2 != core)
    spilled = 2 * CORE + owner_row * (SECOND - EXTRA) + behind_first - EXTRA
    tile_index = jnp.where(jnp.logical_or(rank < BATCH, behind_first < EXTRA), tile_index, spilled)
    tile_index = jnp.where(wanted < 0, POOL, tile_index)
    misc = jnp.stack([x, z, spill[0]]).astype(jnp.int32)
    third = lax.cond(
        misc[2] > 0,
        lambda value: lax.all_gather(value, ("y", "core"), axis=0, tiled=True),
        no_spill_call,
        rest,
    )
    from_up, from_down, swapped, even, odd, tile_index, misc, third = lax.optimization_barrier(
        (from_up, from_down, swapped, even, odd, tile_index, misc, third)
    )
    tails = from_up[half : half + EXTRA // 2], from_down[half + EXTRA // 2 :]
    tails, from_up, from_down = lax.optimization_barrier((tails, from_up, from_down))
    tail_up, tail_down = ahead("y", tails[0]), behind("y", tails[1])
    tail = jax.ShapeDtypeStruct((3 * EXTRA // 2, SUB, 128), jnp.bfloat16)
    (tail,) = whole_call(tail_kernel, "tail", [tail], some, tail_up, tail_down)
    parts = [first, up, down, from_up, from_down, some[: EXTRA // 2], tail]
    tiles = collect_call(misc, parts + swapped + swap(parts[3:]), third)

    scalars = (tile_index, misc)
    far, arrays = product_call("far", (2,), scalars, (even, odd, tiles))
    axes = ("x", "z")
    near, arrays = product_call("near", (1, 3), scalars, arrays)
    inputs = []
    for way, axis in enumerate(axes):
        inputs += [*near[2 * way : 2 * way + 2], ahead(axis, far[2 * way]), behind(axis, far[2 * way + 1])]
    packed = jax.ShapeDtypeStruct((2, 4, PACKED, 128), jnp.int16)
    added = whole_call(add_first_kernel, "add_first", [packed] * 4, *inputs)
    came = []
    for way, axis in enumerate(axes):
        came += [ahead(axis, added[2 * way]), behind(axis, added[2 * way + 1])]
    (one, two), _ = product_call("own", (0,), scalars, arrays)
    double = jax.ShapeDtypeStruct((2, PACKED, 128), jnp.int16)
    *outs, own = whole_call(
        middle_kernel,
        "middle",
        [double] * 6 + [jax.ShapeDtypeStruct((rows_dev, 256), jnp.float32)],
        one,
        two,
        *came,
        scalars=(misc,),
    )
    across_axis = [(i, (i + 2) % 4) for i in range(4)]
    came = [
        ahead("z", outs[1]),
        lax.ppermute(outs[0], "z", across_axis),
        lax.ppermute(outs[3], "x", across_axis),
        behind("z", outs[2]),
        ahead("x", outs[4]),
        behind("x", outs[5]),
    ]
    return whole_call(
        last_kernel, "last", [jax.ShapeDtypeStruct((256, rows_dev), jnp.float32)], own, *came
    )[0]


def solution(mesh):
    axes = ("y", "core", "x", "z")
    fine = Mesh(mesh.devices.reshape(4, 2, 4, 4), axes)
    row, col = ("y", "core"), ("x", "z")
    in_specs = (P(row, col), P(row, col), P(axes, None), P())
    out_specs = P(col, row)
    return jax.shard_map(shards, mesh=fine, in_specs=in_specs, out_specs=out_specs, check_vma=False)
```

```python
import functools

import jax
import jax.numpy as jnp
from jax import lax
from jax.experimental import pallas as pl
from jax.experimental.pallas import tpu as pltpu
from jax.sharding import Mesh
from jax.sharding import PartitionSpec as P

TILE = 64
VTILES = 32
KOCC = 16
JOCC = 2
CAP = 20
COLS = 16
ROWS = 8
DEVS = 128
GROUP = VTILES * KOCC * VTILES * JOCC // COLS
KB = GROUP // (VTILES * JOCC)
NB = VTILES * JOCC
SUB = TILE * TILE // 128
BATCH = 8
FIRST = COLS * BATCH
SECOND = COLS * (CAP - BATCH)
EXTRA = 80
CORE = 4 * FIRST + 4 * EXTRA
THIRD = ROWS * (SECOND - EXTRA)
POOL = 2 * CORE + THIRD
PARTS = 14
HALF = 512
SHARE = 32
PACKED = HALF + HALF // SHARE
VMEM_GRANT = 6 * 1024 * 1024


def route_kernel(slots_dev, me_ref, slot_ref, out_ref):
    base = me_ref[0] * slots_dev
    slot = slot_ref[...]
    rows = slot.shape[0]
    per = rows // COLS
    local = slot - base
    mine = jnp.logical_and(local >= 0, local < slots_dev)
    ones = jnp.where(mine, 1.0, 0.0).astype(jnp.bfloat16)
    r = lax.broadcasted_iota(jnp.int32, (128, 128), 0)
    c = lax.broadcasted_iota(jnp.int32, (128, 128), 1)
    before = jnp.where(r < c, 1.0, 0.0).astype(jnp.bfloat16)
    within = jnp.dot(ones, before, preferred_element_type=jnp.float32)
    r = lax.broadcasted_iota(jnp.int32, (rows, rows), 0)
    c = lax.broadcasted_iota(jnp.int32, (rows, rows), 1)
    above = jnp.where(jnp.logical_and(r // per == c // per, c < r), 1.0, 0.0).astype(jnp.bfloat16)
    upto = jnp.dot(above, ones, preferred_element_type=jnp.float32)
    rank = within + jnp.sum(upto, axis=1, keepdims=True)
    rank = jnp.where(mine, rank, -1.0).reshape(COLS, per, 128)
    parity = lax.broadcasted_iota(jnp.int32, (rows, 128), 1) % 2
    local = jnp.where(mine, 2 * local + parity, 0).astype(jnp.float32).reshape(COLS, per, 128)
    lane = lax.broadcasted_iota(jnp.int32, (COLS, 128), 1)
    out = jnp.zeros((COLS, 128), jnp.float32)
    for j in range(CAP):
        picked = jnp.sum(jnp.where(rank == float(j), local, 0.0), axis=1)
        out = jnp.where(lane == j, jnp.sum(picked, axis=1, keepdims=True), out)
    out_ref[...] = out.astype(jnp.int32)


def fill_kernel(base, index_ref, tiles_ref, out_ref):
    size = out_ref.shape[0] // COLS

    def group(g, carry):
        codes = [index_ref[g, base + j] for j in range(size)]
        tiles = [tiles_ref[code // 2] for code in codes]
        for j in range(size):
            turned = jnp.concatenate([tiles[j][:, TILE:], tiles[j][:, :TILE]], axis=1)
            out_ref[g * size + j] = jnp.where(codes[j] % 2 == 1, turned, tiles[j])
        return carry

    lax.fori_loop(0, COLS, group, 0)


def mix_kernel(index_ref, spill_ref, second_ref, up_ref, down_ref, some_ref, rest_ref, up_out, down_out, sems):
    half = FIRST // 2
    copies = [
        pltpu.make_async_copy(up_ref.at[pl.ds(0, half)], up_out.at[pl.ds(0, half)], sems.at[0]),
        pltpu.make_async_copy(down_ref.at[pl.ds(half, half)], down_out.at[pl.ds(0, half)], sems.at[1]),
    ]
    for copy in copies:
        copy.start()

    def body(i, carry):
        tiles = [second_ref[index_ref[i * 16 + k]] for k in range(16)]
        for k in range(16):
            some_ref[i * 16 + k] = tiles[k]
            up_out[half + i * 16 + k] = tiles[k]
            down_out[half + i * 16 + k] = tiles[k]
        return carry

    lax.fori_loop(0, EXTRA // 16, body, 0)

    @pl.when(spill_ref[0] > 0)
    def _():
        def body_rest(i, carry):
            tiles = [second_ref[index_ref[EXTRA + i * 16 + k]] for k in range(16)]
            for k in range(16):
                rest_ref[i * 16 + k] = tiles[k]
            return carry

        lax.fori_loop(0, (SECOND - EXTRA) // 16, body_rest, 0)

    for copy in copies:
        copy.wait()


def tail_kernel(some_ref, up_ref, down_ref, out_ref):
    size = EXTRA // 2

    def body(i, carry):
        sources = [(some_ref, size), (up_ref, 0), (down_ref, 0)]
        tiles = [[ref[base + i * 8 + k] for k in range(8)] for ref, base in sources]
        for part in range(3):
            for k in range(8):
                out_ref[part * size + i * 8 + k] = tiles[part][k]
        return carry

    lax.fori_loop(0, size // 8, body, 0)


def no_spill_kernel(tiles_ref, out_ref, sem):
    copy = pltpu.make_async_copy(tiles_ref.at[pl.ds(0, 1)], out_ref.at[pl.ds(0, 1)], sem)
    copy.start()
    copy.wait()


def no_spill_call(tiles):
    return pl.pallas_call(
        no_spill_kernel,
        in_specs=[pl.BlockSpec(memory_space=pl.ANY)],
        out_specs=pl.BlockSpec(memory_space=pl.ANY),
        out_shape=jax.ShapeDtypeStruct((THIRD, SUB, 128), jnp.bfloat16),
        scratch_shapes=[pltpu.SemaphoreType.DMA],
        compiler_params=pltpu.CompilerParams(vmem_limit_bytes=VMEM_GRANT),
        name="no_spill",
    )(tiles)


def prep_kernel(mask_ref, amp_ref, even_ref, odd_ref):
    blk = pl.program_id(0)
    rows = amp_ref.shape[0]
    r = lax.broadcasted_iota(jnp.int32, (256, 256), 0)
    c = lax.broadcasted_iota(jnp.int32, (256, 256), 1)
    source = (c % 128 // SUB) * TILE + 2 * (c % SUB) + c // 128
    shuffle = jnp.where(r == source, 1.0, 0.0).astype(jnp.bfloat16)
    moved = jnp.dot(amp_ref[...], shuffle, preferred_element_type=jnp.float32)
    mask = mask_ref[...].astype(jnp.bfloat16)
    r = lax.broadcasted_iota(jnp.int32, (mask.shape[1], 128), 0)
    c = lax.broadcasted_iota(jnp.int32, (mask.shape[1], 128), 1)
    spread = jnp.where(r == 4 * blk + c // SUB, 1.0, 0.0).astype(jnp.bfloat16)
    wide = jnp.dot(mask, spread, preferred_element_type=jnp.float32).astype(jnp.bfloat16)
    r = lax.broadcasted_iota(jnp.int32, (rows, mask.shape[0]), 0)
    c = lax.broadcasted_iota(jnp.int32, (rows, mask.shape[0]), 1)
    tall = jnp.where(r // TILE == c, 1.0, 0.0).astype(jnp.bfloat16)
    full = jnp.dot(tall, wide, preferred_element_type=jnp.float32)
    even_ref[...] = (moved[:, :128] * full).astype(jnp.bfloat16)
    odd_ref[...] = (moved[:, 128:] * full).astype(jnp.bfloat16)


def pack(out_ref, value):
    value = value.reshape(HALF // SHARE, SHARE, 128)
    top = jnp.maximum(jnp.max(jnp.abs(value), axis=1), 1e-30)
    exponent = jnp.ceil(jnp.log2(top * 1.0001))
    scaled = jnp.round(value * jnp.exp2(15.0 - exponent)[:, None, :]).reshape(HALF, 128)
    out_ref[pl.ds(0, HALF)] = scaled.astype(jnp.int32).astype(jnp.int16)
    out_ref[pl.ds(HALF, HALF // SHARE)] = exponent.astype(jnp.int32).astype(jnp.int16)


def unpack(ref):
    mantissa = ref[pl.ds(0, HALF)].astype(jnp.int32).astype(jnp.float32)
    exponent = ref[pl.ds(HALF, HALF // SHARE)].astype(jnp.int32).astype(jnp.float32)
    value = mantissa.reshape(HALF // SHARE, SHARE, 128) * jnp.exp2(exponent - 15.0)[:, None, :]
    return value.reshape(HALF, 128)


def collect_kernel(misc_ref, *refs):
    parts, third_ref, tiles, sems = refs[:PARTS], refs[PARTS], refs[PARTS + 1], refs[PARTS + 2]
    copies, base = [], 0
    for k, part in enumerate(parts):
        size = part.shape[0]
        copies.append(pltpu.make_async_copy(part, tiles.at[pl.ds(base, size)], sems.at[k]))
        base += size
    for copy in copies:
        copy.start()
    tiles[pl.ds(POOL, 1)] = jnp.zeros((1, SUB, 128), jnp.bfloat16)

    @pl.when(misc_ref[2] > 0)
    def _():
        copy = pltpu.make_async_copy(third_ref, tiles.at[pl.ds(base, THIRD)], sems.at[PARTS])
        copy.start()
        copy.wait()

    for copy in copies:
        copy.wait()


def collect_call(misc, parts, third):
    return pl.pallas_call(
        collect_kernel,
        in_specs=[pl.BlockSpec(memory_space=pltpu.SMEM)] + [pl.BlockSpec(memory_space=pl.ANY)] * (PARTS + 1),
        out_specs=pl.BlockSpec(memory_space=pltpu.VMEM),
        out_shape=jax.ShapeDtypeStruct((POOL + 1, SUB, 128), jnp.bfloat16),
        scratch_shapes=[pltpu.SemaphoreType.DMA((PARTS + 1,))],
        compiler_params=pltpu.CompilerParams(vmem_limit_bytes=2 * 1024 * 1024),
        cost_estimate=pl.CostEstimate(flops=0, bytes_accessed=POOL * 8192, transcendentals=0),
        name="collect",
    )(misc, *parts, third)


def build(hop, unit, index_ref, misc_ref, tiles, weight):
    at = [((misc_ref[0] + hop) % 4 * 4 + unit) * 4, (unit * 4 + (misc_ref[1] + hop) % 4) * 4 + 2]
    left = lax.broadcasted_iota(jnp.int32, (SUB, 128), 1) < TILE
    for kb in range(KB):
        picked = [tiles[index_ref[kb * NB + at[pair] + k]] for pair in range(2) for k in range(2)]
        rows = slice(kb * SUB, (kb + 1) * SUB)
        for pair in range(2):
            one, two = picked[2 * pair : 2 * pair + 2]
            columns = slice(128 * pair, 128 * pair + 128)
            weight[0][rows, columns] = jnp.where(left, one, two)
            weight[1][rows, columns] = jnp.where(left, two, one)


def product_kernel(hops, index_ref, misc_ref, even_ref, odd_ref, tiles, *refs):
    outs, weights = refs[:-4], (refs[-4:-2], refs[-2:])
    build(hops[0], 0, index_ref, misc_ref, tiles, weights[0])

    def emit(at, unit, weight):
        straight = jnp.dot(even_ref[...], weight[0][...], preferred_element_type=jnp.float32)
        crossed = jnp.dot(odd_ref[...], weight[1][...], preferred_element_type=jnp.float32)
        for way in range(2):
            columns = slice(way * 128, way * 128 + 128)
            value = straight[:, columns] + pltpu.roll(crossed[:, columns], TILE, 1)
            if hops == (0,):
                outs[way][unit] = value
                continue
            for half in range(2):
                out_ref = outs[2 * way + half] if len(hops) == 1 else outs[2 * way + at].at[half]
                pack(out_ref.at[unit], value[half * HALF : (half + 1) * HALF])

    for at, hop in enumerate(hops):
        after = hops[min(at + 1, len(hops) - 1)]

        def two_units(i, carry, at=at, hop=hop, after=after):
            build(hop, 2 * i + 1, index_ref, misc_ref, tiles, weights[1])
            emit(at, 2 * i, weights[0])
            build(jnp.where(i == 0, hop, after), 2 - 2 * i, index_ref, misc_ref, tiles, weights[0])
            emit(at, 2 * i + 1, weights[1])
            return carry

        lax.fori_loop(0, 2, two_units, 0)


def product_call(name, hops, scalars, arrays):
    rows_dev, depth_half = arrays[0].shape
    vmem = pl.BlockSpec(memory_space=pltpu.VMEM)
    if hops == (0,):
        outs = [jax.ShapeDtypeStruct((4, rows_dev, 128), jnp.float32)] * 2
    elif len(hops) == 1:
        outs = [jax.ShapeDtypeStruct((4, PACKED, 128), jnp.int16)] * 4
    else:
        outs = [jax.ShapeDtypeStruct((2, 4, PACKED, 128), jnp.int16)] * 4
    handed = [] if hops == (0,) else [jax.ShapeDtypeStruct(a.shape, a.dtype) for a in arrays]
    result = pl.pallas_call(
        functools.partial(product_kernel, hops),
        grid_spec=pltpu.PrefetchScalarGridSpec(
            num_scalar_prefetch=2,
            grid=(),
            in_specs=[vmem] * 3,
            out_specs=[vmem] * (len(outs) + len(handed)),
            scratch_shapes=[pltpu.VMEM((depth_half, 256), jnp.bfloat16)] * 4,
        ),
        out_shape=outs + handed,
        input_output_aliases={2 + k: len(outs) + k for k in range(len(handed))},
        compiler_params=pltpu.CompilerParams(vmem_limit_bytes=VMEM_GRANT),
        cost_estimate=pl.CostEstimate(
            flops=8 * len(hops) * rows_dev * depth_half * 512, bytes_accessed=POOL * 8192, transcendentals=0
        ),
        name=name,
    )(*scalars, *arrays)
    return result[: len(outs)], result[len(outs) :]


def ahead(axis, value):
    return lax.ppermute(value, axis, [(i, (i + 1) % 4) for i in range(4)])


def behind(axis, value):
    return lax.ppermute(value, axis, [(i, (i + 3) % 4) for i in range(4)])


def reach(tiles):
    return ahead("y", tiles), behind("y", tiles)


def swap(parts):
    return [lax.ppermute(part, "core", [(0, 1), (1, 0)]) for part in parts]


def add_first_kernel(*refs):
    def body(i, carry):
        for way in range(2):
            ahead_in, behind_in, came_a, came_b = refs[4 * way : 4 * way + 4]
            ahead_out, behind_out = refs[8 + 2 * way : 10 + 2 * way]
            pack(ahead_out.at[0, i], unpack(ahead_in.at[0, i]) + unpack(came_a.at[i]))
            ahead_out[1, i] = ahead_in[1, i]
            behind_out[0, i] = behind_in[0, i]
            pack(behind_out.at[1, i], unpack(behind_in.at[1, i]) + unpack(came_b.at[i]))
        return carry

    lax.fori_loop(0, 4, body, 0)


def whole_call(body, name, outs, *arrays, scalars=()):
    vmem = pl.BlockSpec(memory_space=pltpu.VMEM)
    size = sum(a.size * a.dtype.itemsize for a in [*arrays, *outs])
    return pl.pallas_call(
        body,
        in_specs=[pl.BlockSpec(memory_space=pltpu.SMEM)] * len(scalars) + [vmem] * len(arrays),
        out_specs=[vmem] * len(outs),
        out_shape=outs,
        compiler_params=pltpu.CompilerParams(vmem_limit_bytes=VMEM_GRANT),
        cost_estimate=pl.CostEstimate(flops=10 * size, bytes_accessed=size, transcendentals=0),
        name=name,
    )(*scalars, *arrays)


def middle_kernel(misc_ref, one_ref, two_ref, *refs):
    came, outs, own_ref = refs[:4], refs[4:10], refs[10]
    for way, own in enumerate((one_ref, two_ref)):
        right, left = came[2 * way : 2 * way + 2]
        for hop, ahead_by in enumerate((2, 1, 3, 0)):
            at = (misc_ref[1 - way] + ahead_by) % 4
            total = [
                own[at, pl.ds(half * HALF, HALF)] + unpack(right.at[half, at]) + unpack(left.at[half, at])
                for half in range(2)
            ]
            for half in range(2):
                if hop < 3:
                    pack(outs[3 * way + hop].at[half], total[half])
                else:
                    own_ref[pl.ds(half * HALF, HALF), pl.ds(way * 128, 128)] = total[half]


def last_kernel(own_ref, *refs):
    came, out_ref = refs[:6], refs[6]
    for way in range(2):
        columns = pl.ds(way * 128, 128)
        for half in range(2):
            rows = pl.ds(half * HALF, HALF)
            total = own_ref[rows, columns]
            for ref in ((came[0], came[1], came[3]), (came[2], came[4], came[5]))[way]:
                total += unpack(ref.at[half])
            out_ref[columns, rows] = total.T


def shards(amplitudes, t2_mask, eri_tiles, eri_slot):
    y, core, x, z = (lax.axis_index(name) for name in ("y", "core", "x", "z"))
    group = x * 4 + z
    myself = (y * 2 + core) * COLS + group
    rows_dev, depth_dev = amplitudes.shape
    slots_dev = eri_tiles.shape[0]

    send_index = pl.pallas_call(
        lambda *refs: route_kernel(slots_dev, *refs),
        out_shape=jax.ShapeDtypeStruct((COLS, 128), jnp.int32),
        in_specs=[
            pl.BlockSpec(memory_space=pltpu.SMEM),
            pl.BlockSpec(memory_space=pltpu.VMEM),
        ],
        out_specs=pl.BlockSpec(memory_space=pltpu.VMEM),
        compiler_params=pltpu.CompilerParams(vmem_limit_bytes=VMEM_GRANT),
        name="route",
    )(myself.reshape(1).astype(jnp.int32), eri_slot.reshape(-1, 128))
    vmem = pl.BlockSpec(memory_space=pltpu.VMEM)
    stored = eri_tiles.reshape(slots_dev, SUB, 128)

    def fill(base, size):
        return pl.pallas_call(
            functools.partial(fill_kernel, base),
            grid_spec=pltpu.PrefetchScalarGridSpec(
                num_scalar_prefetch=1, grid=(), in_specs=[vmem], out_specs=vmem
            ),
            out_shape=jax.ShapeDtypeStruct((size, SUB, 128), jnp.bfloat16),
            compiler_params=pltpu.CompilerParams(vmem_limit_bytes=VMEM_GRANT),
            name="fill",
        )(send_index, stored)

    outgoing = fill(0, FIRST), fill(BATCH, SECOND)

    def send(part):
        part = part.reshape(COLS, -1, SUB, 128)
        part = lax.all_to_all(part, ("x", "z"), split_axis=0, concat_axis=0, tiled=True)
        return part.reshape(-1, SUB, 128)

    first = send(outgoing[0])
    first, second, eri_slot = lax.optimization_barrier((first, outgoing[1], eri_slot))
    up, down = reach(first)
    second = send(second)
    devices = jnp.arange(DEVS, dtype=jnp.int32)
    owner_all = jnp.where(eri_slot >= 0, eri_slot // slots_dev, -1).reshape(COLS, 1, GROUP)
    held = jnp.sum((owner_all == devices[None, :, None]).astype(jnp.int32), axis=2)
    tail = jnp.maximum(held - BATCH, 0).reshape(COLS, ROWS, COLS)
    spill = jnp.any(jnp.sum(tail, axis=2) > EXTRA)
    tail = lax.dynamic_index_in_dim(tail, group, 0, keepdims=False)
    upto = jnp.sum(jnp.where(jnp.arange(COLS)[:, None] >= jnp.arange(COLS)[None, :], tail[:, None, :], 0), axis=2)
    start = upto - tail
    mine_upto = lax.dynamic_index_in_dim(upto, y * 2 + core, 0, keepdims=False)
    mine_start = lax.dynamic_index_in_dim(start, y * 2 + core, 0, keepdims=False)
    spot = jnp.arange(SECOND, dtype=jnp.int32)
    inside = jnp.logical_and(spot[:, None] >= mine_start[None, :], spot[:, None] < mine_upto[None, :])
    source = jnp.arange(COLS, dtype=jnp.int32)[None, :] * (CAP - BATCH) + spot[:, None] - mine_start[None, :]
    source = jnp.sum(jnp.where(inside, source, 0), axis=1).astype(jnp.int32)
    spill = spill.astype(jnp.int32).reshape(1)
    second, source, spill, up, down = lax.optimization_barrier((second, source, spill, up, down))
    half = FIRST // 2
    sizes = (EXTRA, SECOND - EXTRA, half + EXTRA, half + EXTRA)
    some, rest, from_up, from_down = pl.pallas_call(
        mix_kernel,
        grid_spec=pltpu.PrefetchScalarGridSpec(
            num_scalar_prefetch=2,
            grid=(),
            in_specs=[vmem] * 3,
            out_specs=[vmem] * 4,
            scratch_shapes=[pltpu.SemaphoreType.DMA((2,))],
        ),
        out_shape=[jax.ShapeDtypeStruct((size, SUB, 128), jnp.bfloat16) for size in sizes],
        compiler_params=pltpu.CompilerParams(vmem_limit_bytes=VMEM_GRANT),
        name="mix",
    )(source, spill, second, up, down)
    wanted = lax.dynamic_slice_in_dim(eri_slot, group * GROUP, GROUP)
    from_up, up, down, amplitudes, wanted = lax.optimization_barrier((from_up, up, down, amplitudes, wanted))
    from_up, from_down = ahead("y", from_up), behind("y", from_down)
    swapped = swap([first, up, down])

    parted = jax.ShapeDtypeStruct((rows_dev, depth_dev // 2), jnp.bfloat16)
    even, odd = pl.pallas_call(
        prep_kernel,
        grid=(depth_dev // 256,),
        out_shape=[parted] * 2,
        in_specs=[
            pl.BlockSpec(t2_mask.shape, lambda i: (0, 0)),
            pl.BlockSpec((rows_dev, 256), lambda i: (0, i)),
        ],
        out_specs=[pl.BlockSpec((rows_dev, 128), lambda i: (0, i))] * 2,
        compiler_params=pltpu.CompilerParams(vmem_limit_bytes=VMEM_GRANT),
        name="prep",
    )(t2_mask, amplitudes)

    owner = jnp.where(wanted >= 0, wanted // slots_dev, -1)
    mine = owner[:, None] == devices[None, :]
    spot = jnp.arange(GROUP, dtype=jnp.int32)
    before = (spot[:, None] > spot[None, :]).astype(jnp.bfloat16)
    counts = jnp.dot(before, mine.astype(jnp.bfloat16), preferred_element_type=jnp.float32)
    rank = jnp.sum(jnp.where(mine, counts, 0.0), axis=1).astype(jnp.int32)
    begin = jnp.sum(jnp.where(mine, start.reshape(1, DEVS), 0), axis=1)
    behind_first = begin + rank - BATCH
    owner_row = owner // COLS
    turn = (owner_row // 2 - y) % 4
    turn = jnp.where(turn == 1, 2, jnp.where(turn == 2, 3, jnp.where(turn == 3, 1, 0)))
    size = FIRST
    slot = owner % COLS * BATCH + rank
    early = turn * size + slot + jnp.where(jnp.logical_and(turn == 3, slot >= half), EXTRA, 0)
    begins = (4 * size + 2 * EXTRA, 3 * size + half, 4 * size + EXTRA, 4 * size + 3 * EXTRA)
    late = behind_first + sum(jnp.where(turn == k, begin_late, 0) for k, begin_late in enumerate(begins))
    tile_index = jnp.where(rank < BATCH, early, late) + CORE * (owner_row % 2 != core)
    spilled = 2 * CORE + owner_row * (SECOND - EXTRA) + behind_first - EXTRA
    tile_index = jnp.where(jnp.logical_or(rank < BATCH, behind_first < EXTRA), tile_index, spilled)
    tile_index = jnp.where(wanted < 0, POOL, tile_index)
    misc = jnp.stack([x, z, spill[0]]).astype(jnp.int32)
    third = lax.cond(
        misc[2] > 0,
        lambda value: lax.all_gather(value, ("y", "core"), axis=0, tiled=True),
        no_spill_call,
        rest,
    )
    from_up, from_down, swapped, even, odd, tile_index, misc, third = lax.optimization_barrier(
        (from_up, from_down, swapped, even, odd, tile_index, misc, third)
    )
    tails = from_up[half : half + EXTRA // 2], from_down[half + EXTRA // 2 :]
    tails, from_up, from_down = lax.optimization_barrier((tails, from_up, from_down))
    tail_up, tail_down = ahead("y", tails[0]), behind("y", tails[1])
    tail = jax.ShapeDtypeStruct((3 * EXTRA // 2, SUB, 128), jnp.bfloat16)
    (tail,) = whole_call(tail_kernel, "tail", [tail], some, tail_up, tail_down)
    parts = [first, up, down, from_up, from_down, some[: EXTRA // 2], tail]
    tiles = collect_call(misc, parts + swapped + swap(parts[3:]), third)

    scalars = (tile_index, misc)
    far, arrays = product_call("far", (2,), scalars, (even, odd, tiles))
    axes = ("x", "z")
    near, arrays = product_call("near", (1, 3), scalars, arrays)
    inputs = []
    for way, axis in enumerate(axes):
        inputs += [*near[2 * way : 2 * way + 2], ahead(axis, far[2 * way]), behind(axis, far[2 * way + 1])]
    packed = jax.ShapeDtypeStruct((2, 4, PACKED, 128), jnp.int16)
    added = whole_call(add_first_kernel, "add_first", [packed] * 4, *inputs)
    came = []
    for way, axis in enumerate(axes):
        came += [ahead(axis, added[2 * way]), behind(axis, added[2 * way + 1])]
    (one, two), _ = product_call("own", (0,), scalars, arrays)
    double = jax.ShapeDtypeStruct((2, PACKED, 128), jnp.int16)
    *outs, own = whole_call(
        middle_kernel,
        "middle",
        [double] * 6 + [jax.ShapeDtypeStruct((rows_dev, 256), jnp.float32)],
        one,
        two,
        *came,
        scalars=(misc,),
    )
    across_axis = [(i, (i + 2) % 4) for i in range(4)]
    came = [
        ahead("z", outs[1]),
        lax.ppermute(outs[0], "z", across_axis),
        lax.ppermute(outs[3], "x", across_axis),
        behind("z", outs[2]),
        ahead("x", outs[4]),
        behind("x", outs[5]),
    ]
    return whole_call(
        last_kernel, "last", [jax.ShapeDtypeStruct((256, rows_dev), jnp.float32)], own, *came
    )[0]


def solution(mesh):
    axes = ("y", "core", "x", "z")
    fine = Mesh(mesh.devices.reshape(4, 2, 4, 4), axes)
    row, col = ("y", "core"), ("x", "z")
    in_specs = (P(row, col), P(row, col), P(axes, None), P())
    out_specs = P(col, row)
    return jax.shard_map(shards, mesh=fine, in_specs=in_specs, out_specs=out_specs, check_vma=False)
```
